32 devices in a mesh: vel: 8 (over y, x, core), space: 4 (over z).
Axes of the slice: x: 2, y: 2, z: 4, core: 2. Of those that a mesh axis runs over, the one named last changes fastest.
Arguments:
- distribution: float32 [1024, 64, 512], P('vel', 'space'), may hold values from -6 to 6
- courant: float32 [1024], replicated, may hold values from -0.9 to 0.9
- gain_matrix: bfloat16 [1024, 1024], replicated, may hold values from -0.1875 to 0.1875
- product_matrix: bfloat16 [1024, 1024], replicated, may hold values from -0.1875 to 0.1875
- collision_rate: float32 [64, 512], P('space'), may hold values from 0.5 to 2
Outputs:
- final_state: float32 [1024, 64, 512], P('vel', 'space')
The draws below stay inside these ranges and needn't reach their ends.
All inputs are finite; a program needn't handle non-finite values.
Results may differ from the reference program's by a relative error of at most 0.0016.
Values may be sent and summed in bfloat16 or wider, within the bound.
No kernel may reach another device: no remote copies, remote signals or barrier semaphores. Data moves between devices by JAX's collectives and lax.ppermute only.
A program may use at most 64 MiB of HBM per device.

```python
import math
import jax
import jax.numpy as jnp
from jax import lax

V = 1024
PLANE = 512
STEPS = 2
NX = 64


def levels(stream_key, shape, shards, smallest, largest):
    loudness, own = 1.0, jax.random.fold_in(stream_key, 6)
    for axis_at, blocks in shards:
        heights = jnp.exp(jax.random.uniform(jax.random.fold_in(own, axis_at), (blocks,), jnp.float32, smallest / len(shards), largest / len(shards)))
        loudness = loudness * jnp.repeat(heights, shape[axis_at] // blocks).reshape([-1 if axis == axis_at else 1 for axis in range(len(shape))])
    return loudness


def centred(rng, shape, scale, limit, cuts=(), dtype=jnp.bfloat16):
    result = scale * jax.random.normal(rng, shape, jnp.float32)
    if cuts:
        result = result * levels(rng, shape, cuts, -0.22, 0.18)
    return jnp.clip(result, -limit, limit).astype(dtype)


def setup_inputs(seed: int = 0) -> dict:
    seeds = jax.random.split(jax.random.key(seed), 6)
    distribution = centred(seeds[0], (V, NX, PLANE), 1.0, 6.0, ((0, 8), (1, 4)), jnp.float32)
    courant = jnp.clip(jax.random.uniform(seeds[1], (V,), jnp.float32, -0.9, 0.9), -0.9, 0.9)
    gain_matrix = centred(seeds[2], (V, V), V ** -0.5, 0.1875)
    product_matrix = centred(seeds[3], (V, V), V ** -0.5, 0.1875)
    collision_rate = jnp.clip(jnp.exp(math.log(2.0) - 1.3862944 * jax.random.uniform(seeds[4], (NX, PLANE), jnp.float32) ** levels(seeds[4], (NX, PLANE), ((0, 4),), -0.2, 0.2)), 0.5, 2.0)
    return {"distribution": distribution, "courant": courant, "gain_matrix": gain_matrix, "product_matrix": product_matrix, "collision_rate": collision_rate}


time_step = 0.2


def minmod(first, second):
    return jnp.maximum(jnp.minimum(first, second), 0.0) + jnp.minimum(jnp.maximum(first, second), 0.0)


def change(widened, speeds):
    differ = widened[:, 1:] - widened[:, :-1]
    slopes = minmod(differ[:, 1:], differ[:, :-1])
    inner = widened.shape[1] - 4
    left_value = widened[:, 1:inner + 2]
    right_value = widened[:, 2:inner + 3]
    left_slope = slopes[:, 0:inner + 1]
    right_slope = slopes[:, 1:inner + 2]
    upward = jnp.maximum(speeds, 0.0)
    downward = jnp.minimum(speeds, 0.0)
    fluxes = upward * (left_value + 0.5 * (1.0 - speeds) * left_slope) + downward * (right_value - 0.5 * (1.0 + speeds) * right_slope)
    return -(fluxes[:, 1:] - fluxes[:, :-1])


def wrap_pad(field, width):
    return jnp.concatenate([field[:, -width:], field, field[:, :width]], axis=1)


def advect(field, speeds):
    section = field + change(wrap_pad(field, 2), speeds)
    return 0.5 * field + 0.5 * (section + change(wrap_pad(section, 2), speeds))


def collide(columns, gain_matrix, product_matrix):
    first_term = jnp.dot(gain_matrix, columns, preferred_element_type=jnp.float32)
    second_term = jnp.dot(product_matrix, columns, preferred_element_type=jnp.float32)
    return (first_term * second_term).astype(jnp.bfloat16)


def reference(distribution, courant, gain_matrix, product_matrix, collision_rate):
    state = distribution
    for step_index in range(STEPS):
        blocks = state.reshape(V // 16, 16, NX, PLANE)
        speed_blocks = courant.reshape(V // 16, 16, 1, 1)
        smoothed = lax.map(lambda pair: advect(pair[0], pair[1]), (blocks, speed_blocks)).reshape(V, NX, PLANE)
        rounded = smoothed.astype(jnp.bfloat16)
        planes = jnp.moveaxis(rounded, 1, 0)
        gains = lax.map(lambda plane_slice: collide(plane_slice, gain_matrix, product_matrix), planes)
        gained = jnp.moveaxis(gains, 0, 1)
        state = smoothed + time_step * (gained.astype(jnp.float32) - collision_rate[None] * rounded.astype(jnp.float32))
    return state
```

```python
import functools

import jax
import jax.numpy as jnp
from jax import lax
from jax.experimental import pallas as pl
from jax.experimental.pallas import tpu as pltpu
from jax.sharding import PartitionSpec as P

STEPS = 2
HALO = 4
HEAD = 8
CHUNKS = 2
LANES = 128
VMEM = 48 * 1024 * 1024

time_step = 0.2


def with_halo(block, sides, width):
    for axis, dim in sides:
        count = lax.axis_size(axis)
        forward = [(i, i + 1) for i in range(count - 1)]
        forward.append((count - 1, 0))
        backward = [(target, source) for source, target in forward]
        low = lax.ppermute(
            lax.slice_in_dim(block, block.shape[dim] - width, None, axis=dim), axis, forward
        )
        high = lax.ppermute(lax.slice_in_dim(block, 0, width, axis=dim), axis, backward)
        block = jnp.concatenate([low, block, high], axis=dim)
    return block


def minmod(first, second):
    return jnp.maximum(jnp.minimum(first, second), 0.0) + jnp.minimum(
        jnp.maximum(first, second), 0.0
    )


def change(widened, speeds):
    differ = widened[:, 1:] - widened[:, :-1]
    slopes = minmod(differ[:, 1:], differ[:, :-1])
    inner = widened.shape[1] - 4
    left_value = widened[:, 1 : inner + 2]
    right_value = widened[:, 2 : inner + 3]
    left_slope = slopes[:, 0 : inner + 1]
    right_slope = slopes[:, 1 : inner + 2]
    upward = jnp.maximum(speeds, 0.0)
    downward = jnp.minimum(speeds, 0.0)
    fluxes = upward * (left_value + 0.5 * (1.0 - speeds) * left_slope) + downward * (
        right_value - 0.5 * (1.0 + speeds) * right_slope
    )
    return -(fluxes[:, 1:] - fluxes[:, :-1])


def extend(field):
    return with_halo(field, (("space", 1),), 2)


def advect(field, speeds):
    section = field + change(extend(field), speeds)
    return 0.5 * field + 0.5 * (section + change(extend(section), speeds))


def collide(pieces, gain_matrix, product_matrix):
    columns = pieces.reshape(pieces.shape[0], -1)
    first_term = jnp.dot(gain_matrix, columns, preferred_element_type=jnp.float32)
    second_term = jnp.dot(product_matrix, columns, preferred_element_type=jnp.float32)
    return (first_term * second_term).astype(jnp.bfloat16).reshape(pieces.shape)


def update(smoothed, rounded, gained, rate):
    return smoothed + time_step * (gained.astype(jnp.float32) - rate * rounded.astype(jnp.float32))


def general_body(distribution, courant, gain_matrix, product_matrix, collision_rate):
    local_count = distribution.shape[0]
    groups = lax.axis_size("vel")
    member = lax.axis_index("vel")
    own_speeds = lax.dynamic_slice_in_dim(courant, member * local_count, local_count, 0)[
        :, None, None
    ]
    field = distribution
    for step_index in range(STEPS):
        smoothed = advect(field, own_speeds)
        rounded = smoothed.astype(jnp.bfloat16)
        grouped = rounded.reshape(local_count, groups, -1)
        gained = lax.all_to_all(
            collide(
                lax.all_to_all(grouped, "vel", split_axis=1, concat_axis=0, tiled=True),
                gain_matrix,
                product_matrix,
            ),
            "vel",
            split_axis=0,
            concat_axis=1,
            tiled=True,
        )
        field = update(smoothed, rounded, gained.reshape(rounded.shape), collision_rate[None])
    return field


def params(count=1):
    return pltpu.CompilerParams(
        dimension_semantics=("arbitrary",) * count, vmem_limit_bytes=VMEM
    )


def cost(flops, moved):
    return pl.CostEstimate(flops=int(flops), bytes_accessed=int(moved), transcendentals=0)


def exponent_of(largest):
    power = jnp.floor(14.0 - jnp.log2(jnp.maximum(largest, 1e-36)))
    return jnp.clip(power, -115.0, 120.0)


def pack_kernel(order, planes, cells, chip_ref, d_ref, *refs):
    outs, scratch = refs[:-1], refs[-1]
    chip = chip_ref[0]
    step = pl.program_id(0)
    rows = d_ref.reshape(LANES * planes, LANES)
    for x in range(planes):
        part = rows[pl.ds(x, LANES, stride=planes), :]
        scratch[x, pl.ds(pl.multiple_of(step * LANES, LANES), LANES), :] = part.T

    @pl.when(step == pl.num_programs(0) - 1)
    def _():
        for mask, out in zip(order, outs):
            first = pl.multiple_of((chip ^ mask) * cells, cells)

            def peak(x, carry):
                return jnp.maximum(carry, jnp.abs(scratch[x, pl.ds(first, cells), :]))

            top = lax.fori_loop(0, planes, peak, jnp.zeros((cells, LANES), jnp.float32))
            power = exponent_of(jnp.max(top, axis=0, keepdims=True))
            scale = jnp.exp2(power)

            def write(x, carry):
                out[pl.ds(pl.multiple_of(x * cells, cells), cells), :] = (
                    scratch[x, pl.ds(first, cells), :] * scale
                )
                return carry

            lax.fori_loop(0, planes, write, 0)
            out[planes * cells :, :] = jnp.broadcast_to(power, (HEAD, LANES))


def pack(distribution, chip, order, chunk, cells):
    planes = distribution.shape[1]
    width = cells * len(order)
    steps = width // LANES
    shape = (planes * cells + HEAD, LANES)
    return pl.pallas_call(
        functools.partial(pack_kernel, order, planes, cells),
        grid_spec=pltpu.PrefetchScalarGridSpec(
            num_scalar_prefetch=1,
            grid=(steps,),
            in_specs=[
                pl.BlockSpec((LANES, planes, LANES), lambda i, s: (0, 0, chunk * steps + i))
            ],
            out_specs=[pl.BlockSpec(shape, lambda i, s: (0, 0)) for _ in order],
            scratch_shapes=[pltpu.VMEM((planes, width, LANES), jnp.float32)],
        ),
        out_shape=[jax.ShapeDtypeStruct(shape, jnp.float32) for _ in order],
        compiler_params=params(),
        cost_estimate=cost(1e6, 8 * LANES * planes * width),
        name="pack",
    )(chip, distribution)


def stage(values, speed, bend, positive):
    differ = [b - a for a, b in zip(values[:-1], values[1:])]
    slopes = [
        jnp.maximum(jnp.minimum(a, b), jnp.minimum(jnp.maximum(a, b), 0.0))
        for a, b in zip(differ[:-1], differ[1:])
    ]
    inner = [speed * u + bend * s for u, s in zip(values[1:-1], slopes)]
    faces = [jnp.where(positive, a, b) for a, b in zip(inner[:-1], inner[1:])]
    return [u - (b - a) for u, a, b in zip(values[2:-2], faces[:-1], faces[1:])]


def advect_kernel(planes, cells, tile, scaled, c_ref, low_ref, high_ref, *refs):
    bodies, smoothed_ref, rounded_ref = refs[:-2], refs[-2], refs[-1]
    speed = c_ref[0:1, :]
    size = jnp.abs(speed)
    bend = 0.5 * size * (1.0 - size)
    positive = jnp.broadcast_to(speed, (tile, LANES)) > 0.0

    def back(ref):
        return jnp.exp2(-ref[HALO * cells : HALO * cells + 1, :])

    back_low, back_high = back(low_ref), back(high_ref)
    if scaled:
        back_body = jnp.exp2(-bodies[0][planes * cells : planes * cells + 1, :])

    def at(ref, x, t):
        return ref[pl.ds(pl.multiple_of(x * cells + t * tile, tile), tile), :]

    def body(t, carry):
        values = [at(low_ref, x, t) * back_low for x in range(HALO)]
        if scaled:
            values += [at(bodies[0], x, t) * back_body for x in range(planes)]
        else:
            low, middle, high = bodies
            values += [at(low, x, t) for x in range(HALO)]
            values += [at(middle, x, t) for x in range(planes - 2 * HALO)]
            values += [at(high, x, t) for x in range(HALO)]
        values += [at(high_ref, x, t) * back_high for x in range(HALO)]
        section = stage(values, speed, bend, positive)
        moved = stage(section, speed, bend, positive)
        for x in range(planes):
            result = 0.5 * values[x + HALO] + 0.5 * moved[x]
            where = pl.ds(pl.multiple_of(x * cells + t * tile, tile), tile)
            smoothed_ref[where, :] = result
            rounded_ref[where, :] = result.astype(jnp.bfloat16)
        return carry

    lax.fori_loop(0, cells // tile, body, 0)


def transport(speeds, low, high, bodies, planes, cells, scaled):
    rows, width = planes * cells, low.shape[1]

    def spec(a):
        return pl.BlockSpec((a.shape[0], LANES), lambda j: (0, j))

    return pl.pallas_call(
        functools.partial(advect_kernel, planes, cells, 16, scaled),
        grid=(width // LANES,),
        in_specs=[spec(a) for a in (speeds, low, high, *bodies)],
        out_specs=[pl.BlockSpec((rows, LANES), lambda j: (0, j))] * 2,
        out_shape=[
            jax.ShapeDtypeStruct((rows, width), jnp.float32),
            jax.ShapeDtypeStruct((rows, width), jnp.bfloat16),
        ],
        compiler_params=params(),
        cost_estimate=cost(40 * rows * width, 12 * rows * width),
        name="transport",
    )(speeds, low, high, *bodies)


def gains(own, other, matrix_ref, columns):
    half = own.shape[1]
    dims = (((1,), (1,)), ((), ()))
    return lax.dot_general(
        own, matrix_ref[columns, :half], dims, preferred_element_type=jnp.float32
    ) + lax.dot_general(
        other, matrix_ref[columns, half:], dims, preferred_element_type=jnp.float32
    )


def collided(own_ref, other_ref, smoothed, rounded, rate_ref, gain_ref, product_ref, columns):
    own, other = own_ref[...], other_ref[...]
    gained = gains(own, other, gain_ref, columns) * gains(own, other, product_ref, columns)
    gained = gained.astype(jnp.bfloat16).astype(jnp.float32)
    rate = rate_ref[...]
    rate = jnp.concatenate([rate] * (rounded.shape[1] // LANES), axis=1)
    return smoothed + time_step * (gained - rate * rounded.astype(jnp.float32))


def faces_kernel(own_ref, other_ref, smoothed_ref, rate_ref, gain_ref, product_ref, state_ref, message_ref):
    rows, width = own_ref.shape
    group = 2 * LANES
    for start in range(0, width, group):
        columns = slice(start, start + group)
        state = collided(
            own_ref, other_ref, smoothed_ref[:, columns], own_ref[:, columns], rate_ref,
            gain_ref, product_ref, columns,
        )
        state_ref[0, :, columns] = state
        power = exponent_of(jnp.max(jnp.abs(state), axis=0, keepdims=True))
        message_ref[0, :rows, columns] = state * jnp.exp2(power)
        message_ref[0, rows:, columns] = jnp.broadcast_to(power, (HEAD, group))


def faces(own, other, smoothed, rate, gain, product, planes, cells):
    rows, width = HALO * cells, own.shape[1]
    last = planes // HALO - 1
    block = pl.BlockSpec((rows, width), lambda i: (i * last, 0))
    whole = pl.BlockSpec(gain.shape, lambda i: (0, 0))
    return pl.pallas_call(
        faces_kernel,
        grid=(2,),
        in_specs=[block, block, block, pl.BlockSpec((rows, LANES), lambda i: (i * last, 0)), whole, whole],
        out_specs=[
            pl.BlockSpec((1, rows, width), lambda i: (i, 0, 0)),
            pl.BlockSpec((1, rows + HEAD, width), lambda i: (i, 0, 0)),
        ],
        out_shape=[
            jax.ShapeDtypeStruct((2, rows, width), jnp.float32),
            jax.ShapeDtypeStruct((2, rows + HEAD, width), jnp.float32),
        ],
        compiler_params=params(),
        cost_estimate=cost(16 * rows * width * width, 30 * rows * width),
        name="faces",
    )(own, other, smoothed, rate, gain, product)


def inside_kernel(own_ref, other_ref, smoothed_ref, rate_ref, gain_ref, product_ref, state_ref):
    width = own_ref.shape[1]
    group = 2 * LANES
    for start in range(0, width, group):
        columns = slice(start, start + group)
        state_ref[:, columns] = collided(
            own_ref, other_ref, smoothed_ref[:, columns], own_ref[:, columns], rate_ref,
            gain_ref, product_ref, columns,
        )


def inside(own, other, smoothed, rate, gain, product, planes, cells):
    rows, width = HALO * cells, own.shape[1]
    count = planes // HALO - 2
    block = pl.BlockSpec((rows, width), lambda i: (i + 1, 0))
    whole = pl.BlockSpec(gain.shape, lambda i: (0, 0))
    return pl.pallas_call(
        inside_kernel,
        grid=(count,),
        in_specs=[block, block, block, pl.BlockSpec((rows, LANES), lambda i: (i + 1, 0)), whole, whole],
        out_specs=pl.BlockSpec((rows, width), lambda i: (i, 0)),
        out_shape=jax.ShapeDtypeStruct((count * rows, width), jnp.float32),
        compiler_params=params(),
        cost_estimate=cost(8 * count * rows * width * width, 20 * count * rows * width),
        name="inside",
    )(own, other, smoothed, rate, gain, product)


def final_kernel(blocks, own_ref, other_ref, rounded_ref, smoothed_ref, rate_ref, gain_ref, product_ref, *refs):
    outs, scratch = refs[:-1], refs[-1]
    step = pl.program_id(0)
    rows, group = smoothed_ref.shape
    state = collided(
        own_ref, other_ref, smoothed_ref[...], rounded_ref[...], rate_ref,
        gain_ref, product_ref, slice(0, group),
    )
    scratch[pl.ds(pl.multiple_of(step * rows, rows), rows), :] = state

    @pl.when(step == blocks - 1)
    def _():
        for index, out in enumerate(outs):
            columns = slice(index * LANES, (index + 1) * LANES)

            def peak(i, carry):
                return jnp.maximum(
                    carry, jnp.abs(scratch[pl.ds(pl.multiple_of(i * LANES, LANES), LANES), columns])
                )

            top = lax.fori_loop(0, blocks * rows // LANES, peak, jnp.zeros((LANES, LANES), jnp.float32))
            power = exponent_of(jnp.max(top, axis=0, keepdims=True))
            scale = jnp.exp2(power)

            def write(i, carry):
                where = pl.ds(pl.multiple_of(i * LANES, LANES), LANES)
                out[where, :] = scratch[where, columns] * scale
                return carry

            lax.fori_loop(0, blocks * rows // LANES, write, 0)
            out[blocks * rows :, :] = jnp.broadcast_to(power, (HEAD, LANES))


def final(own, other, smoothed, rate, gain, product, planes, cells, part):
    rows, width = HALO * cells, own.shape[1]
    blocks = planes // HALO
    group = 2 * LANES
    block = pl.BlockSpec((rows, width), lambda i: (i, 0))
    narrow = pl.BlockSpec((rows, group), lambda i: (i, part))
    matrix = pl.BlockSpec((group, gain.shape[1]), lambda i: (part, 0))
    shape = (blocks * rows + HEAD, LANES)
    return pl.pallas_call(
        functools.partial(final_kernel, blocks),
        grid=(blocks,),
        in_specs=[block, block, narrow, narrow, pl.BlockSpec((rows, LANES), lambda i: (i, 0)), matrix, matrix],
        out_specs=[pl.BlockSpec(shape, lambda i: (0, 0))] * 2,
        out_shape=[jax.ShapeDtypeStruct(shape, jnp.float32)] * 2,
        scratch_shapes=[pltpu.VMEM((blocks * rows, group), jnp.float32)],
        compiler_params=params(),
        cost_estimate=cost(8 * blocks * rows * width * group, 20 * blocks * rows * group),
        name="final",
    )(own, other, own, smoothed, rate, gain, product)


def unpack_kernel(order, planes, cells, chip_ref, *refs):
    count = len(order)
    pieces, out, scratch = refs[:count], refs[-2], refs[-1]
    chip = chip_ref[0]
    step = pl.program_id(0)
    flat = out.reshape(LANES * planes, LANES)

    @pl.when(step == 0)
    def _():
        for mask, piece in zip(order, pieces):
            first = pl.multiple_of((chip ^ mask) * cells, cells)
            scale = jnp.exp2(-piece[planes * cells : planes * cells + 1, :])

            def place(x, carry):
                scratch[x, pl.ds(first, cells), :] = (
                    piece[pl.ds(pl.multiple_of(x * cells, cells), cells), :] * scale
                )
                return carry

            lax.fori_loop(0, planes, place, 0)

    for x in range(planes):
        part = scratch[x, pl.ds(pl.multiple_of(step * LANES, LANES), LANES), :]
        flat[pl.ds(x, LANES, stride=planes), :] = part.T


def unpack(pieces, target, chip, order, chunk, planes, cells):
    width = cells * len(order)
    steps = width // LANES
    shape = (LANES, planes, width * CHUNKS)
    specs = [pl.BlockSpec(p.shape, lambda i, s: (0, 0)) for p in pieces]
    operands = list(pieces)
    aliases = {}
    if target is not None:
        specs.append(pl.BlockSpec(memory_space=pl.ANY))
        operands.append(target)
        aliases = {len(operands): 0}
    return pl.pallas_call(
        functools.partial(unpack_kernel, order, planes, cells),
        grid_spec=pltpu.PrefetchScalarGridSpec(
            num_scalar_prefetch=1,
            grid=(steps,),
            in_specs=specs,
            out_specs=pl.BlockSpec((LANES, planes, LANES), lambda i, s: (0, 0, chunk * steps + i)),
            scratch_shapes=[pltpu.VMEM((planes, width, LANES), jnp.float32)],
        ),
        out_shape=jax.ShapeDtypeStruct(shape, jnp.float32),
        input_output_aliases=aliases,
        compiler_params=params(),
        cost_estimate=cost(1e6, 8 * LANES * planes * width),
        name="unpack",
    )(chip, *operands)


def exchange(array, mask):
    count = lax.axis_size("vel")
    return lax.ppermute(array, "vel", [(i, i ^ mask) for i in range(count)])


def shift(array, step):
    count = lax.axis_size("space")
    return lax.ppermute(array, "space", [(i, (i + step) % count) for i in range(count)])


def half(array):
    return array.astype(jnp.float16)


def full(array):
    return array.astype(jnp.float32)


def first_faces(pieces, cells, planes):
    body = HALO * cells
    top = planes * cells

    def message(start):
        return jnp.concatenate(
            [jnp.concatenate([p[start : start + body], p[top:]], axis=0) for p in pieces], axis=1
        )

    return message(top - body), message(0)


def body(distribution, courant, gain_matrix, product_matrix, collision_rate):
    planes, plane = distribution.shape[1:]
    chips = lax.axis_size("vel") // 2
    member = lax.axis_index("vel")
    chip, core = member // 2, member % 2
    order = list(range(1, chips)) + [0]
    cells = plane // (chips * CHUNKS)
    span = cells * chips
    chip_word = chip.astype(jnp.int32).reshape(1)

    pieces = [pack(distribution, chip_word, order, k, cells) for k in range(CHUNKS)]
    sent = [
        [half(a) if mask == 0 else exchange(half(a), 2 * mask) for a, mask in zip(pieces[k], order)]
        for k in range(CHUNKS)
    ]

    own_blocks = [2 * (chip ^ mask) + core for mask in order]
    other_blocks = [2 * (chip ^ mask) + 1 - core for mask in order]

    def arranged(matrix):
        lines = jnp.concatenate(
            [lax.dynamic_slice_in_dim(matrix, b * LANES, LANES, 0) for b in own_blocks], axis=0
        )
        return jnp.concatenate(
            [lax.dynamic_slice_in_dim(lines, b * LANES, LANES, 1) for b in own_blocks + other_blocks],
            axis=1,
        )

    gain, product = arranged(gain_matrix), arranged(product_matrix)
    speeds = jnp.concatenate(
        [lax.dynamic_slice_in_dim(courant, b * LANES, LANES, 0) for b in own_blocks]
    )
    speeds = jnp.broadcast_to(speeds[None], (8, speeds.shape[0]))
    rates = []
    for k in range(CHUNKS):
        own = lax.dynamic_slice_in_dim(collision_rate, k * span + chip * cells, cells, 1)
        rates.append(jnp.broadcast_to(own.reshape(planes * cells, 1), (planes * cells, LANES)))

    result = None
    states = []
    for k in range(CHUNKS):
        up, down = first_faces(sent[k], cells, planes)
        low, high = full(shift(up, 1)), full(shift(down, -1))
        local = jnp.concatenate(
            [a if mask == 0 else full(b) for a, b, mask in zip(pieces[k], sent[k], order)], axis=1
        )
        smoothed, rounded = transport(speeds, low, high, [local], planes, cells, True)
        other = exchange(rounded, 1)
        ends, messages = faces(rounded, other, smoothed, rates[k], gain, product, planes, cells)
        messages = half(messages)
        low, high = full(shift(messages[1], 1)), full(shift(messages[0], -1))
        middle = inside(rounded, other, smoothed, rates[k], gain, product, planes, cells)
        states.append((low, high, [ends[0], middle, ends[1]]))
    for k in range(CHUNKS):
        low, high, parts = states[k]
        smoothed, rounded = transport(speeds, low, high, parts, planes, cells, False)
        other = exchange(rounded, 1)
        ready = []
        for part in range(chips // 2):
            ready += final(rounded, other, smoothed, rates[k], gain, product, planes, cells, part)
        back = [
            a if mask == 0 else full(exchange(half(a), 2 * mask)) for a, mask in zip(ready, order)
        ]
        result = unpack(back, result, chip_word, order, k, planes, cells)
    return result


def fits(mesh, shape, spaces):
    groups = mesh.shape["vel"]
    local, planes = shape[0] // groups, shape[1] // spaces
    chips = groups // 2
    return (
        groups % 4 == 0
        and chips & (chips - 1) == 0
        and local == LANES
        and planes % HALO == 0
        and planes >= 3 * HALO
        and shape[2] % (CHUNKS * LANES) == 0
        and shape[2] % (CHUNKS * chips * 16) == 0
    )


def solution(mesh):
    in_specs = (P("vel", "space", None), P(), P(), P(), P("space", None))
    out_specs = P("vel", "space", None)

    def run(distribution, courant, gain_matrix, product_matrix, collision_rate):
        special = fits(mesh, distribution.shape, mesh.shape["space"])
        return jax.shard_map(
            body if special else general_body,
            mesh=mesh, in_specs=in_specs, out_specs=out_specs, check_vma=False,
        )(distribution, courant, gain_matrix, product_matrix, collision_rate)

    return run
```

```python
import functools

import jax
import jax.numpy as jnp
from jax import lax
from jax.experimental import pallas as pl
from jax.experimental.pallas import tpu as pltpu
from jax.sharding import PartitionSpec as P

STEPS = 2
HALO = 4
HEAD = 16
CHUNKS = 2
LANES = 128
VMEM = 16 * 1024 * 1024

time_step = 0.2


def with_halo(block, sides, width):
    for axis, dim in sides:
        count = lax.axis_size(axis)
        forward = [(i, i + 1) for i in range(count - 1)]
        forward.append((count - 1, 0))
        backward = [(target, source) for source, target in forward]
        low = lax.ppermute(
            lax.slice_in_dim(block, block.shape[dim] - width, None, axis=dim), axis, forward
        )
        high = lax.ppermute(lax.slice_in_dim(block, 0, width, axis=dim), axis, backward)
        block = jnp.concatenate([low, block, high], axis=dim)
    return block


def minmod(first, second):
    return jnp.maximum(jnp.minimum(first, second), 0.0) + jnp.minimum(
        jnp.maximum(first, second), 0.0
    )


def change(widened, speeds):
    differ = widened[:, 1:] - widened[:, :-1]
    slopes = minmod(differ[:, 1:], differ[:, :-1])
    inner = widened.shape[1] - 4
    left_value = widened[:, 1 : inner + 2]
    right_value = widened[:, 2 : inner + 3]
    left_slope = slopes[:, 0 : inner + 1]
    right_slope = slopes[:, 1 : inner + 2]
    upward = jnp.maximum(speeds, 0.0)
    downward = jnp.minimum(speeds, 0.0)
    fluxes = upward * (left_value + 0.5 * (1.0 - speeds) * left_slope) + downward * (
        right_value - 0.5 * (1.0 + speeds) * right_slope
    )
    return -(fluxes[:, 1:] - fluxes[:, :-1])


def extend(field):
    return with_halo(field, (("space", 1),), 2)


def advect(field, speeds):
    section = field + change(extend(field), speeds)
    return 0.5 * field + 0.5 * (section + change(extend(section), speeds))


def collide(pieces, gain_matrix, product_matrix):
    columns = pieces.reshape(pieces.shape[0], -1)
    first_term = jnp.dot(gain_matrix, columns, preferred_element_type=jnp.float32)
    second_term = jnp.dot(product_matrix, columns, preferred_element_type=jnp.float32)
    return (first_term * second_term).astype(jnp.bfloat16).reshape(pieces.shape)


def update(smoothed, rounded, gained, rate):
    return smoothed + time_step * (gained.astype(jnp.float32) - rate * rounded.astype(jnp.float32))


def general_body(distribution, courant, gain_matrix, product_matrix, collision_rate):
    local_count = distribution.shape[0]
    groups = lax.axis_size("vel")
    member = lax.axis_index("vel")
    own_speeds = lax.dynamic_slice_in_dim(courant, member * local_count, local_count, 0)[
        :, None, None
    ]
    field = distribution
    for step_index in range(STEPS):
        smoothed = advect(field, own_speeds)
        rounded = smoothed.astype(jnp.bfloat16)
        grouped = rounded.reshape(local_count, groups, -1)
        gained = lax.all_to_all(
            collide(
                lax.all_to_all(grouped, "vel", split_axis=1, concat_axis=0, tiled=True),
                gain_matrix,
                product_matrix,
            ),
            "vel",
            split_axis=0,
            concat_axis=1,
            tiled=True,
        )
        field = update(smoothed, rounded, gained.reshape(rounded.shape), collision_rate[None])
    return field


def params(fusable=None):
    return pltpu.CompilerParams(
        dimension_semantics=("arbitrary",), vmem_limit_bytes=VMEM, allow_input_fusion=fusable
    )


def cost(flops, moved):
    return pl.CostEstimate(flops=int(flops), bytes_accessed=int(moved), transcendentals=0)


def exponent_of(largest):
    power = jnp.floor(14.0 - jnp.log2(jnp.maximum(largest, 1e-36)))
    return jnp.clip(power, -115.0, 120.0)


def pack_kernel(order, planes, cells, chip_ref, d_ref, *refs):
    outs, scratch = refs[:-1], refs[-1]
    chip = chip_ref[0]
    step = pl.program_id(0)
    rows = d_ref.reshape(LANES * planes, LANES)
    for x in range(planes):
        part = rows[pl.ds(x, LANES, stride=planes), :]
        scratch[x, pl.ds(pl.multiple_of(step * LANES, LANES), LANES), :] = part.T

    @pl.when(step == pl.num_programs(0) - 1)
    def _():
        for mask, out in zip(order, outs):
            first = pl.multiple_of((chip ^ mask) * cells, cells)

            def peak(x, carry):
                return jnp.maximum(carry, jnp.abs(scratch[x, pl.ds(first, cells), :]))

            top = lax.fori_loop(0, planes, peak, jnp.zeros((cells, LANES), jnp.float32))
            power = exponent_of(jnp.max(top, axis=0, keepdims=True))
            scale = jnp.exp2(power)

            def write(x, carry):
                start = place_of(x, planes, cells)
                out[pl.ds(pl.multiple_of(start, 16), cells), :] = (
                    scratch[x, pl.ds(first, cells), :] * scale
                )
                return carry

            lax.fori_loop(0, planes, write, 0)
            out[HALO * cells : HALO * cells + HEAD, :] = jnp.broadcast_to(power, (HEAD, LANES))


def place_of(x, planes, cells):
    first = planes - HALO
    if isinstance(x, int):
        return (x - first) * cells if x >= first else HALO * cells + HEAD + x * cells
    return jnp.where(x >= first, (x - first) * cells, HALO * cells + HEAD + x * cells)


def pack(distribution, chip, order, chunk, cells):
    planes = distribution.shape[1]
    width = cells * len(order)
    steps = width // LANES
    shape = (planes * cells + HEAD, LANES)
    return pl.pallas_call(
        functools.partial(pack_kernel, order, planes, cells),
        grid_spec=pltpu.PrefetchScalarGridSpec(
            num_scalar_prefetch=1,
            grid=(steps,),
            in_specs=[
                pl.BlockSpec((LANES, planes, LANES), lambda i, s: (0, 0, chunk * steps + i))
            ],
            out_specs=[pl.BlockSpec(shape, lambda i, s: (0, 0)) for _ in order],
            scratch_shapes=[pltpu.VMEM((planes, width, LANES), jnp.float32)],
        ),
        out_shape=[jax.ShapeDtypeStruct(shape, jnp.float32) for _ in order],
        compiler_params=params(),
        cost_estimate=cost(1e6, 8 * LANES * planes * width),
        name="pack",
    )(chip, distribution)


def message_kernel(cells, *refs):
    pieces, up_ref, down_ref = refs[:-2], refs[-2], refs[-1]
    rows = HALO * cells
    for index, piece in enumerate(pieces):
        columns = slice(index * LANES, (index + 1) * LANES)
        up_ref[:, columns] = piece[: rows + HEAD, :]
        down_ref[:, columns] = piece[rows : 2 * rows + HEAD, :]


def messages_of(pieces, cells):
    rows = 2 * HALO * cells + HEAD
    shape = (HALO * cells + HEAD, LANES * len(pieces))
    return pl.pallas_call(
        functools.partial(message_kernel, cells),
        grid=(1,),
        in_specs=[pl.BlockSpec(p.shape, lambda i: (0, 0)) for p in pieces],
        out_specs=[pl.BlockSpec(shape, lambda i: (0, 0))] * 2,
        out_shape=[jax.ShapeDtypeStruct(shape, jnp.float32)] * 2,
        compiler_params=params([True] * len(pieces)),
        cost_estimate=cost(1e5, 8 * rows * LANES * len(pieces)),
        name="messages",
    )(*pieces)


def spread_kernel(planes, cells, *refs):
    pieces, out = refs[:-1], refs[-1]
    rows = HALO * cells
    for index, piece in enumerate(pieces):
        columns = slice(index * LANES, (index + 1) * LANES)
        scale = jnp.exp2(-piece[rows : rows + 1, :])
        for x in range(planes):
            start = place_of(x, planes, cells)
            out[x * cells : (x + 1) * cells, columns] = piece[start : start + cells, :] * scale


def spread(pieces, planes, cells):
    shape = (planes * cells, LANES * len(pieces))
    return pl.pallas_call(
        functools.partial(spread_kernel, planes, cells),
        grid=(1,),
        in_specs=[pl.BlockSpec(p.shape, lambda i: (0, 0)) for p in pieces],
        out_specs=pl.BlockSpec(shape, lambda i: (0, 0)),
        out_shape=jax.ShapeDtypeStruct(shape, jnp.float32),
        compiler_params=params([True] * len(pieces)),
        cost_estimate=cost(1e6, 8 * shape[0] * shape[1]),
        name="spread",
    )(*pieces)


def arrange_kernel(order, word_ref, c_ref, g_ref, p_ref, speeds_ref, gain_ref, product_ref):
    chip, core = word_ref[0], word_ref[1]
    count = len(order)
    for row, mask in enumerate(order):
        own = 2 * (chip ^ mask) + core
        lines = slice(row * LANES, (row + 1) * LANES)
        speeds_ref[:, lines] = jnp.broadcast_to(c_ref[pl.ds(own, 1), :], (8, LANES))
        source = pl.ds(pl.multiple_of(own * LANES, LANES), LANES)
        for column in range(2 * count):
            other = order[column % count]
            block = 2 * (chip ^ other) + (core if column < count else 1 - core)
            lanes = pl.ds(pl.multiple_of(block * LANES, LANES), LANES)
            target = slice(column * LANES, (column + 1) * LANES)
            gain_ref[lines, target] = g_ref[source, lanes]
            product_ref[lines, target] = p_ref[source, lanes]


def arrange(courant, gain_matrix, product_matrix, word, order):
    count = len(order)
    whole = pl.BlockSpec(gain_matrix.shape, lambda i, s: (0, 0))
    half = (count * LANES, 2 * count * LANES)
    table = courant.reshape(-1, LANES)
    return pl.pallas_call(
        functools.partial(arrange_kernel, order),
        grid_spec=pltpu.PrefetchScalarGridSpec(
            num_scalar_prefetch=1,
            grid=(1,),
            in_specs=[pl.BlockSpec(table.shape, lambda i, s: (0, 0)), whole, whole],
            out_specs=[
                pl.BlockSpec((8, count * LANES), lambda i, s: (0, 0)),
                pl.BlockSpec(half, lambda i, s: (0, 0)),
                pl.BlockSpec(half, lambda i, s: (0, 0)),
            ],
        ),
        out_shape=[
            jax.ShapeDtypeStruct((8, count * LANES), jnp.float32),
            jax.ShapeDtypeStruct(half, jnp.bfloat16),
            jax.ShapeDtypeStruct(half, jnp.bfloat16),
        ],
        compiler_params=params(),
        cost_estimate=cost(1e5, 12 * half[0] * half[1]),
        name="arrange",
    )(word, table, gain_matrix, product_matrix)


def stage(values, speed, bend, positive):
    differ = [b - a for a, b in zip(values[:-1], values[1:])]
    slopes = [
        jnp.maximum(jnp.minimum(a, b), jnp.minimum(jnp.maximum(a, b), 0.0))
        for a, b in zip(differ[:-1], differ[1:])
    ]
    inner = [speed * u + bend * s for u, s in zip(values[1:-1], slopes)]
    faces = [jnp.where(positive, a, b) for a, b in zip(inner[:-1], inner[1:])]
    return [u - (b - a) for u, a, b in zip(values[2:-2], faces[:-1], faces[1:])]


def advect_kernel(planes, cells, tile, c_ref, low_ref, high_ref, *refs):
    bodies, smoothed_ref, rounded_ref = refs[:-2], refs[-2], refs[-1]
    rows = HALO * cells
    speed = c_ref[0:1, :]
    size = jnp.abs(speed)
    bend = 0.5 * size * (1.0 - size)
    positive = jnp.broadcast_to(speed, (tile, LANES)) > 0.0
    back_low = jnp.exp2(-low_ref[rows : rows + 1, :])
    back_high = jnp.exp2(-high_ref[0:1, :])

    def run(read):
        def body(t, carry):
            def at(ref, start):
                return ref[pl.ds(pl.multiple_of(start + t * tile, 16), tile), :]

            values = [at(low_ref, x * cells) * back_low for x in range(HALO)]
            values += [read(x, at) for x in range(planes)]
            values += [at(high_ref, HEAD + x * cells) * back_high for x in range(HALO)]
            section = stage(values, speed, bend, positive)
            moved = stage(section, speed, bend, positive)
            for x in range(planes):
                result = 0.5 * values[x + HALO] + 0.5 * moved[x]
                where = pl.ds(pl.multiple_of(x * cells + t * tile, tile), tile)
                smoothed_ref[where, :] = result
                rounded_ref[where, :] = result.astype(jnp.bfloat16)
            return carry

        lax.fori_loop(0, cells // tile, body, 0)

    if len(bodies) == 1:
        run(lambda x, at: at(bodies[0], x * cells))
    else:
        ends, middle = bodies

        def read(x, at):
            if x < HALO:
                return at(ends.at[0], x * cells)
            if x >= planes - HALO:
                return at(ends.at[1], (x - planes + HALO) * cells)
            return at(middle, (x - HALO) * cells)

        run(read)


def transport(speeds, low, high, bodies, planes, cells):
    rows, width = planes * cells, low.shape[1]

    def spec(a):
        if a.ndim == 3:
            return pl.BlockSpec((2, a.shape[1], LANES), lambda j: (0, 0, j))
        return pl.BlockSpec((a.shape[0], LANES), lambda j: (0, j))

    return pl.pallas_call(
        functools.partial(advect_kernel, planes, cells, 16),
        grid=(width // LANES,),
        in_specs=[spec(a) for a in (speeds, low, high, *bodies)],
        out_specs=[pl.BlockSpec((rows, LANES), lambda j: (0, j))] * 2,
        out_shape=[
            jax.ShapeDtypeStruct((rows, width), jnp.float32),
            jax.ShapeDtypeStruct((rows, width), jnp.bfloat16),
        ],
        compiler_params=params(),
        cost_estimate=cost(40 * rows * width, 12 * rows * width),
        name="transport",
    )(speeds, low, high, *bodies)


def gains(own, other, matrix_ref, columns):
    half = own.shape[1]
    dims = (((1,), (1,)), ((), ()))
    return lax.dot_general(
        own, matrix_ref[columns, :half], dims, preferred_element_type=jnp.float32
    ) + lax.dot_general(
        other, matrix_ref[columns, half:], dims, preferred_element_type=jnp.float32
    )


def collided(own_ref, other_ref, smoothed, rounded, rate_ref, gain_ref, product_ref, columns):
    own, other = own_ref[...], other_ref[...]
    gained = gains(own, other, gain_ref, columns) * gains(own, other, product_ref, columns)
    gained = gained.astype(jnp.bfloat16).astype(jnp.float32)
    rate = rate_ref[...]
    rate = jnp.concatenate([rate] * (rounded.shape[1] // LANES), axis=1)
    return smoothed + time_step * (gained - rate * rounded.astype(jnp.float32))


def faces_kernel(own_ref, other_ref, smoothed_ref, rate_ref, gain_ref, product_ref, state_ref, down_ref, up_ref):
    rows, width = own_ref.shape
    group = 2 * LANES
    step = pl.program_id(0)
    for start in range(0, width, group):
        columns = slice(start, start + group)
        state = collided(
            own_ref, other_ref, smoothed_ref[:, columns], own_ref[:, columns], rate_ref,
            gain_ref, product_ref, columns,
        )
        state_ref[0, :, columns] = state
        power = exponent_of(jnp.max(jnp.abs(state), axis=0, keepdims=True))
        scaled = state * jnp.exp2(power)
        head = jnp.broadcast_to(power, (HEAD, group))

        @pl.when(step == 0)
        def _():
            down_ref[:HEAD, columns] = head
            down_ref[HEAD:, columns] = scaled

        @pl.when(step == 1)
        def _():
            up_ref[:rows, columns] = scaled
            up_ref[rows:, columns] = head


def faces(own, other, smoothed, rate, gain, product, planes, cells):
    rows, width = HALO * cells, own.shape[1]
    last = planes // HALO - 1
    block = pl.BlockSpec((rows, width), lambda i: (i * last, 0))
    whole = pl.BlockSpec(gain.shape, lambda i: (0, 0))
    message = (rows + HEAD, width)
    return pl.pallas_call(
        faces_kernel,
        grid=(2,),
        in_specs=[block, block, block, pl.BlockSpec((rows, LANES), lambda i: (i * last, 0)), whole, whole],
        out_specs=[
            pl.BlockSpec((1, rows, width), lambda i: (i, 0, 0)),
            pl.BlockSpec(message, lambda i: (0, 0)),
            pl.BlockSpec(message, lambda i: (0, 0)),
        ],
        out_shape=[
            jax.ShapeDtypeStruct((2, rows, width), jnp.float32),
            jax.ShapeDtypeStruct(message, jnp.float32),
            jax.ShapeDtypeStruct(message, jnp.float32),
        ],
        compiler_params=params(),
        cost_estimate=cost(16 * rows * width * width, 30 * rows * width),
        name="faces",
    )(own, other, smoothed, rate, gain, product)


def inside_kernel(own_ref, other_ref, smoothed_ref, rate_ref, gain_ref, product_ref, state_ref):
    width = own_ref.shape[1]
    group = 2 * LANES
    for start in range(0, width, group):
        columns = slice(start, start + group)
        state_ref[:, columns] = collided(
            own_ref, other_ref, smoothed_ref[:, columns], own_ref[:, columns], rate_ref,
            gain_ref, product_ref, columns,
        )


def inside(own, other, smoothed, rate, gain, product, planes, cells):
    rows, width = HALO * cells, own.shape[1]
    count = planes // HALO - 2
    block = pl.BlockSpec((rows, width), lambda i: (i + 1, 0))
    whole = pl.BlockSpec(gain.shape, lambda i: (0, 0))
    return pl.pallas_call(
        inside_kernel,
        grid=(count,),
        in_specs=[block, block, block, pl.BlockSpec((rows, LANES), lambda i: (i + 1, 0)), whole, whole],
        out_specs=pl.BlockSpec((rows, width), lambda i: (i, 0)),
        out_shape=jax.ShapeDtypeStruct((count * rows, width), jnp.float32),
        compiler_params=params(),
        cost_estimate=cost(8 * count * rows * width * width, 20 * count * rows * width),
        name="inside",
    )(own, other, smoothed, rate, gain, product)


def final_kernel(blocks, own_ref, other_ref, rounded_ref, smoothed_ref, rate_ref, gain_ref, product_ref, *refs):
    outs, scratch = refs[:-1], refs[-1]
    step = pl.program_id(0)
    rows, group = smoothed_ref.shape
    state = collided(
        own_ref, other_ref, smoothed_ref[...], rounded_ref[...], rate_ref,
        gain_ref, product_ref, slice(0, group),
    )
    scratch[pl.ds(pl.multiple_of(step * rows, rows), rows), :] = state

    @pl.when(step == blocks - 1)
    def _():
        for index, out in enumerate(outs):
            columns = slice(index * LANES, (index + 1) * LANES)

            def peak(i, carry):
                return jnp.maximum(
                    carry, jnp.abs(scratch[pl.ds(pl.multiple_of(i * LANES, LANES), LANES), columns])
                )

            top = lax.fori_loop(0, blocks * rows // LANES, peak, jnp.zeros((LANES, LANES), jnp.float32))
            power = exponent_of(jnp.max(top, axis=0, keepdims=True))
            scale = jnp.exp2(power)

            def write(i, carry):
                where = pl.ds(pl.multiple_of(i * LANES, LANES), LANES)
                out[where, :] = scratch[where, columns] * scale
                return carry

            lax.fori_loop(0, blocks * rows // LANES, write, 0)
            out[blocks * rows :, :] = jnp.broadcast_to(power, (HEAD, LANES))


def final(own, other, smoothed, rate, gain, product, planes, cells, part):
    rows, width = HALO * cells, own.shape[1]
    blocks = planes // HALO
    group = 2 * LANES
    block = pl.BlockSpec((rows, width), lambda i: (i, 0))
    narrow = pl.BlockSpec((rows, group), lambda i: (i, part))
    matrix = pl.BlockSpec((group, gain.shape[1]), lambda i: (part, 0))
    shape = (blocks * rows + HEAD, LANES)
    return pl.pallas_call(
        functools.partial(final_kernel, blocks),
        grid=(blocks,),
        in_specs=[block, block, narrow, narrow, pl.BlockSpec((rows, LANES), lambda i: (i, 0)), matrix, matrix],
        out_specs=[pl.BlockSpec(shape, lambda i: (0, 0))] * 2,
        out_shape=[jax.ShapeDtypeStruct(shape, jnp.float32)] * 2,
        scratch_shapes=[pltpu.VMEM((blocks * rows, group), jnp.float32)],
        compiler_params=params(),
        cost_estimate=cost(8 * blocks * rows * width * group, 20 * blocks * rows * group),
        name="final",
    )(own, other, own, smoothed, rate, gain, product)


def unpack_kernel(order, planes, cells, chip_ref, *refs):
    count = len(order)
    pieces, out, scratch = refs[:count], refs[-2], refs[-1]
    chip = chip_ref[0]
    step = pl.program_id(0)
    flat = out.reshape(LANES * planes, LANES)

    @pl.when(step == 0)
    def _():
        for mask, piece in zip(order, pieces):
            first = pl.multiple_of((chip ^ mask) * cells, cells)
            scale = jnp.exp2(-piece[planes * cells : planes * cells + 1, :])

            for x in range(planes):
                scratch[x, pl.ds(first, cells), :] = piece[x * cells : (x + 1) * cells, :] * scale

    for x in range(planes):
        part = scratch[x, pl.ds(pl.multiple_of(step * LANES, LANES), LANES), :]
        flat[pl.ds(x, LANES, stride=planes), :] = part.T


def unpack(pieces, target, chip, order, chunk, planes, cells):
    width = cells * len(order)
    steps = width // LANES
    shape = (LANES, planes, width * CHUNKS)
    specs = [pl.BlockSpec(p.shape, lambda i, s: (0, 0)) for p in pieces]
    operands = list(pieces)
    count = len(pieces)
    aliases = {}
    if target is not None:
        specs.append(pl.BlockSpec(memory_space=pl.ANY))
        operands.append(target)
        aliases = {len(operands): 0}
    return pl.pallas_call(
        functools.partial(unpack_kernel, order, planes, cells),
        grid_spec=pltpu.PrefetchScalarGridSpec(
            num_scalar_prefetch=1,
            grid=(steps,),
            in_specs=specs,
            out_specs=pl.BlockSpec((LANES, planes, LANES), lambda i, s: (0, 0, chunk * steps + i)),
            scratch_shapes=[pltpu.VMEM((planes, width, LANES), jnp.float32)],
        ),
        out_shape=jax.ShapeDtypeStruct(shape, jnp.float32),
        input_output_aliases=aliases,
        compiler_params=params([False] + [True] * count + [False] * (len(operands) - count)),
        cost_estimate=cost(1e6, 8 * LANES * planes * width),
        name="unpack",
    )(chip, *operands)


def exchange(array, mask):
    count = lax.axis_size("vel")
    return lax.ppermute(array, "vel", [(i, i ^ mask) for i in range(count)])


def shift(array, step):
    count = lax.axis_size("space")
    return lax.ppermute(array, "space", [(i, (i + step) % count) for i in range(count)])


def half(array):
    return array.astype(jnp.float16)


def full(array):
    return array.astype(jnp.float32)


def body(distribution, courant, gain_matrix, product_matrix, collision_rate):
    planes, plane = distribution.shape[1:]
    chips = lax.axis_size("vel") // 2
    member = lax.axis_index("vel").astype(jnp.int32)
    chip, core = lax.shift_right_logical(member, 1), member & 1
    order = list(range(1, chips)) + [0]
    cells = plane // (chips * CHUNKS)
    span = cells * chips
    word = jnp.stack([chip, core])

    sent = []
    for k in range(CHUNKS):
        pieces = pack(distribution, word, order, k, cells)
        sent.append(
            [a if m == 0 else full(exchange(half(a), 2 * m)) for a, m in zip(pieces, order)]
        )
    speeds, gain, product = arrange(courant, gain_matrix, product_matrix, word, order)
    rates = []
    for k in range(CHUNKS):
        own = lax.dynamic_slice_in_dim(collision_rate, k * span + chip * cells, cells, 1)
        rates.append(jnp.broadcast_to(own.reshape(planes * cells, 1), (planes * cells, LANES)))

    result = None
    states = []
    for k in range(CHUNKS):
        up, down = messages_of(sent[k], cells)
        low, high = full(shift(half(up), 1)), full(shift(half(down), -1))
        smoothed, rounded = transport(speeds, low, high, [spread(sent[k], planes, cells)], planes, cells)
        other = exchange(rounded, 1)
        ends, down, up = faces(rounded, other, smoothed, rates[k], gain, product, planes, cells)
        low, high = full(shift(half(up), 1)), full(shift(half(down), -1))
        middle = inside(rounded, other, smoothed, rates[k], gain, product, planes, cells)
        states.append((low, high, [ends, middle]))
    for k in range(CHUNKS):
        low, high, parts = states[k]
        smoothed, rounded = transport(speeds, low, high, parts, planes, cells)
        other = exchange(rounded, 1)
        ready = []
        for part in range(chips // 2):
            ready += final(rounded, other, smoothed, rates[k], gain, product, planes, cells, part)
        back = [a if m == 0 else full(exchange(half(a), 2 * m)) for a, m in zip(ready, order)]
        result = unpack(back, result, word, order, k, planes, cells)
    return result


def fits(mesh, shape, spaces):
    groups = mesh.shape["vel"]
    local, planes = shape[0] // groups, shape[1] // spaces
    chips = groups // 2
    return (
        groups % 4 == 0
        and chips & (chips - 1) == 0
        and local == LANES
        and planes % HALO == 0
        and planes >= 3 * HALO
        and shape[2] % (CHUNKS * LANES) == 0
        and shape[2] % (CHUNKS * chips * 16) == 0
    )


def solution(mesh):
    in_specs = (P("vel", "space", None), P(), P(), P(), P("space", None))
    out_specs = P("vel", "space", None)

    def run(distribution, courant, gain_matrix, product_matrix, collision_rate):
        special = fits(mesh, distribution.shape, mesh.shape["space"])
        return jax.shard_map(
            body if special else general_body,
            mesh=mesh, in_specs=in_specs, out_specs=out_specs, check_vma=False,
        )(distribution, courant, gain_matrix, product_matrix, collision_rate)

    return run
```

```python
import functools

import jax
import jax.numpy as jnp
from jax import lax
from jax.experimental import pallas as pl
from jax.experimental.pallas import tpu as pltpu
from jax.sharding import PartitionSpec as P

STEPS = 2
HALO = 4
HEAD = 16
CHUNKS = 2
LANES = 128
VMEM = 12 * 1024 * 1024

time_step = 0.2


def with_halo(block, sides, width):
    for axis, dim in sides:
        count = lax.axis_size(axis)
        forward = [(i, i + 1) for i in range(count - 1)]
        forward.append((count - 1, 0))
        backward = [(target, source) for source, target in forward]
        low = lax.ppermute(
            lax.slice_in_dim(block, block.shape[dim] - width, None, axis=dim), axis, forward
        )
        high = lax.ppermute(lax.slice_in_dim(block, 0, width, axis=dim), axis, backward)
        block = jnp.concatenate([low, block, high], axis=dim)
    return block


def minmod(first, second):
    return jnp.maximum(jnp.minimum(first, second), 0.0) + jnp.minimum(
        jnp.maximum(first, second), 0.0
    )


def change(widened, speeds):
    differ = widened[:, 1:] - widened[:, :-1]
    slopes = minmod(differ[:, 1:], differ[:, :-1])
    inner = widened.shape[1] - 4
    left_value = widened[:, 1 : inner + 2]
    right_value = widened[:, 2 : inner + 3]
    left_slope = slopes[:, 0 : inner + 1]
    right_slope = slopes[:, 1 : inner + 2]
    upward = jnp.maximum(speeds, 0.0)
    downward = jnp.minimum(speeds, 0.0)
    fluxes = upward * (left_value + 0.5 * (1.0 - speeds) * left_slope) + downward * (
        right_value - 0.5 * (1.0 + speeds) * right_slope
    )
    return -(fluxes[:, 1:] - fluxes[:, :-1])


def extend(field):
    return with_halo(field, (("space", 1),), 2)


def advect(field, speeds):
    section = field + change(extend(field), speeds)
    return 0.5 * field + 0.5 * (section + change(extend(section), speeds))


def collide(pieces, gain_matrix, product_matrix):
    columns = pieces.reshape(pieces.shape[0], -1)
    first_term = jnp.dot(gain_matrix, columns, preferred_element_type=jnp.float32)
    second_term = jnp.dot(product_matrix, columns, preferred_element_type=jnp.float32)
    return (first_term * second_term).astype(jnp.bfloat16).reshape(pieces.shape)


def update(smoothed, rounded, gained, rate):
    return smoothed + time_step * (gained.astype(jnp.float32) - rate * rounded.astype(jnp.float32))


def general_body(distribution, courant, gain_matrix, product_matrix, collision_rate):
    local_count = distribution.shape[0]
    groups = lax.axis_size("vel")
    member = lax.axis_index("vel")
    own_speeds = lax.dynamic_slice_in_dim(courant, member * local_count, local_count, 0)[
        :, None, None
    ]
    field = distribution
    for step_index in range(STEPS):
        smoothed = advect(field, own_speeds)
        rounded = smoothed.astype(jnp.bfloat16)
        grouped = rounded.reshape(local_count, groups, -1)
        gained = lax.all_to_all(
            collide(
                lax.all_to_all(grouped, "vel", split_axis=1, concat_axis=0, tiled=True),
                gain_matrix,
                product_matrix,
            ),
            "vel",
            split_axis=0,
            concat_axis=1,
            tiled=True,
        )
        field = update(smoothed, rounded, gained.reshape(rounded.shape), collision_rate[None])
    return field


def params(fusable=None, grid=True):
    return pltpu.CompilerParams(
        dimension_semantics=("arbitrary",) if grid else None,
        vmem_limit_bytes=VMEM,
        allow_input_fusion=fusable,
    )


def resident():
    return pl.BlockSpec(memory_space=pltpu.VMEM)


def anywhere():
    return pl.BlockSpec(memory_space=pl.ANY)


def cost(flops, moved):
    return pl.CostEstimate(flops=int(flops), bytes_accessed=int(moved), transcendentals=0)


def exponent_of(largest):
    power = jnp.floor(14.0 - jnp.log2(jnp.maximum(largest, 1e-36)))
    return jnp.clip(power, -115.0, 120.0)


def pack_kernel(order, planes, cells, chip_ref, d_ref, *refs):
    outs, scratch = refs[:-1], refs[-1]
    chip = chip_ref[0]
    step = pl.program_id(0)
    rows = d_ref.reshape(LANES * planes, LANES)
    for x in range(planes):
        part = rows[pl.ds(x, LANES, stride=planes), :]
        scratch[x, pl.ds(pl.multiple_of(step * LANES, LANES), LANES), :] = part.T

    @pl.when(step == pl.num_programs(0) - 1)
    def _():
        for mask, out in zip(order, outs):
            first = pl.multiple_of((chip ^ mask) * cells, cells)

            def peak(x, carry):
                return jnp.maximum(carry, jnp.abs(scratch[x, pl.ds(first, cells), :]))

            top = lax.fori_loop(0, planes, peak, jnp.zeros((cells, LANES), jnp.float32))
            power = exponent_of(jnp.max(top, axis=0, keepdims=True))
            scale = jnp.exp2(power)

            def write(x, carry):
                start = place_of(x, planes, cells)
                out[pl.ds(pl.multiple_of(start, 16), cells), :] = (
                    scratch[x, pl.ds(first, cells), :] * scale
                )
                return carry

            lax.fori_loop(0, planes, write, 0)
            out[HALO * cells : HALO * cells + HEAD, :] = jnp.broadcast_to(power, (HEAD, LANES))


def place_of(x, planes, cells):
    first = planes - HALO
    if isinstance(x, int):
        return (x - first) * cells if x >= first else HALO * cells + HEAD + x * cells
    return jnp.where(x >= first, (x - first) * cells, HALO * cells + HEAD + x * cells)


def pack(distribution, chip, order, chunk, cells):
    planes = distribution.shape[1]
    width = cells * len(order)
    steps = width // LANES
    shape = (planes * cells + HEAD, LANES)
    return pl.pallas_call(
        functools.partial(pack_kernel, order, planes, cells),
        grid_spec=pltpu.PrefetchScalarGridSpec(
            num_scalar_prefetch=1,
            grid=(steps,),
            in_specs=[
                pl.BlockSpec((LANES, planes, LANES), lambda i, s: (0, 0, chunk * steps + i))
            ],
            out_specs=[resident() for _ in order],
            scratch_shapes=[pltpu.VMEM((planes, width, LANES), jnp.float32)],
        ),
        out_shape=[jax.ShapeDtypeStruct(shape, jnp.float32) for _ in order],
        compiler_params=params(),
        cost_estimate=cost(1e6, 8 * LANES * planes * width),
        name="pack",
    )(chip, pltpu.with_memory_space_constraint(distribution, pltpu.HBM))


def message_kernel(cells, *refs):
    pieces, up_ref, down_ref = refs[:-3], refs[-2], refs[-1]
    rows = HALO * cells
    for index, piece in enumerate(pieces):
        columns = slice(index * LANES, (index + 1) * LANES)
        up_ref[:, columns] = piece[: rows + HEAD, :]
        down_ref[:, columns] = piece[rows : 2 * rows + HEAD, :]


def messages_of(pieces, cells, after):
    rows = 2 * HALO * cells + HEAD
    shape = (HALO * cells + HEAD, LANES * len(pieces))
    return pl.pallas_call(
        functools.partial(message_kernel, cells),
        grid=(1,),
        in_specs=[pl.BlockSpec(p.shape, lambda i: (0, 0)) for p in pieces] + [anywhere()],
        out_specs=[resident()] * 2,
        out_shape=[jax.ShapeDtypeStruct(shape, jnp.float32)] * 2,
        compiler_params=params([True] * len(pieces) + [False]),
        cost_estimate=cost(1e5, 8 * rows * LANES * len(pieces)),
        name="messages",
    )(*pieces, after)


def spread_kernel(planes, cells, *refs):
    pieces, out = refs[:-1], refs[-1]
    rows = HALO * cells
    for index, piece in enumerate(pieces):
        columns = slice(index * LANES, (index + 1) * LANES)
        scale = jnp.exp2(-piece[rows : rows + 1, :])
        for x in range(planes):
            start = place_of(x, planes, cells)
            out[x * cells : (x + 1) * cells, columns] = piece[start : start + cells, :] * scale


def spread(pieces, planes, cells):
    shape = (planes * cells, LANES * len(pieces))
    return pl.pallas_call(
        functools.partial(spread_kernel, planes, cells),
        grid=(1,),
        in_specs=[pl.BlockSpec(p.shape, lambda i: (0, 0)) for p in pieces],
        out_specs=resident(),
        out_shape=jax.ShapeDtypeStruct(shape, jnp.float32),
        compiler_params=params([True] * len(pieces)),
        cost_estimate=cost(1e6, 8 * shape[0] * shape[1]),
        name="spread",
    )(*pieces)


def arrange_kernel(order, word_ref, c_ref, g_ref, p_ref, speeds_ref, gain_ref, product_ref):
    chip, core = word_ref[0], word_ref[1]
    count = len(order)
    for row, mask in enumerate(order):
        own = 2 * (chip ^ mask) + core
        lines = slice(row * LANES, (row + 1) * LANES)
        speeds_ref[:, lines] = jnp.broadcast_to(c_ref[pl.ds(own, 1), :], (8, LANES))
        source = pl.ds(pl.multiple_of(own * LANES, LANES), LANES)
        for column in range(2 * count):
            other = order[column % count]
            block = 2 * (chip ^ other) + (core if column < count else 1 - core)
            lanes = pl.ds(pl.multiple_of(block * LANES, LANES), LANES)
            target = slice(column * LANES, (column + 1) * LANES)
            gain_ref[lines, target] = g_ref[source, lanes]
            product_ref[lines, target] = p_ref[source, lanes]


def arrange(courant, gain_matrix, product_matrix, word, order):
    count = len(order)
    shape = (count * LANES, 2 * count * LANES)
    return pl.pallas_call(
        functools.partial(arrange_kernel, order),
        in_specs=[pl.BlockSpec(memory_space=pltpu.SMEM)] + [resident()] * 3,
        out_specs=[resident()] * 3,
        out_shape=[
            jax.ShapeDtypeStruct((8, count * LANES), jnp.float32),
            jax.ShapeDtypeStruct(shape, jnp.bfloat16),
            jax.ShapeDtypeStruct(shape, jnp.bfloat16),
        ],
        compiler_params=params(grid=False),
        cost_estimate=cost(1e5, 12 * shape[0] * shape[1]),
        name="arrange",
    )(word, courant.reshape(-1, LANES), gain_matrix, product_matrix)


def stage(values, speed, bend, positive):
    differ = [b - a for a, b in zip(values[:-1], values[1:])]
    slopes = [
        jnp.maximum(jnp.minimum(a, b), jnp.minimum(jnp.maximum(a, b), 0.0))
        for a, b in zip(differ[:-1], differ[1:])
    ]
    inner = [speed * u + bend * s for u, s in zip(values[1:-1], slopes)]
    faces = [jnp.where(positive, a, b) for a, b in zip(inner[:-1], inner[1:])]
    return [u - (b - a) for u, a, b in zip(values[2:-2], faces[:-1], faces[1:])]


def advect_kernel(planes, cells, tile, count, c_ref, low_ref, high_ref, *refs):
    bodies, smoothed_ref, rounded_ref = refs[: count], refs[-2], refs[-1]
    rows = HALO * cells

    def read(x, start, lanes):
        if count == 1:
            ref, first = bodies[0], x * cells
        elif x < HALO:
            ref, first = bodies[0].at[0], x * cells
        elif x >= planes - HALO:
            ref, first = bodies[0].at[1], (x - planes + HALO) * cells
        else:
            ref, first = bodies[1], (x - HALO) * cells
        return ref[pl.ds(pl.multiple_of(first + start, tile), tile), lanes]

    def column(j, outer):
        lanes = pl.ds(pl.multiple_of(j * LANES, LANES), LANES)
        speed = c_ref[0:1, lanes]
        size = jnp.abs(speed)
        bend = 0.5 * size * (1.0 - size)
        positive = jnp.broadcast_to(speed, (tile, LANES)) > 0.0
        back_low = jnp.exp2(-low_ref[rows : rows + 1, lanes])
        back_high = jnp.exp2(-high_ref[0:1, lanes])

        def body(t, carry):
            start = t * tile

            def halo(ref, first):
                return ref[pl.ds(pl.multiple_of(first + start, tile), tile), lanes]

            values = [halo(low_ref, x * cells) * back_low for x in range(HALO)]
            values += [read(x, start, lanes) for x in range(planes)]
            values += [halo(high_ref, HEAD + x * cells) * back_high for x in range(HALO)]
            section = stage(values, speed, bend, positive)
            moved = stage(section, speed, bend, positive)
            for x in range(planes):
                result = 0.5 * read(x, start, lanes) + 0.5 * moved[x]
                where = pl.ds(pl.multiple_of(x * cells + start, tile), tile)
                smoothed_ref[where, lanes] = result
                rounded_ref[where, lanes] = result.astype(jnp.bfloat16)
            return carry

        return lax.fori_loop(0, cells // tile, body, outer)

    lax.fori_loop(0, low_ref.shape[1] // LANES, column, 0)


def transport(speeds, low, high, bodies, planes, cells, after):
    rows, width = planes * cells, low.shape[1]
    return pl.pallas_call(
        functools.partial(advect_kernel, planes, cells, 16, len(bodies)),
        in_specs=[resident()] * (3 + len(bodies)) + [anywhere()],
        out_specs=[resident()] * 2,
        out_shape=[
            jax.ShapeDtypeStruct((rows, width), jnp.float32),
            jax.ShapeDtypeStruct((rows, width), jnp.bfloat16),
        ],
        compiler_params=params(grid=False),
        cost_estimate=cost(40 * rows * width, 12 * rows * width),
        name="transport",
    )(speeds, low, high, *bodies, after)


def collided(lhs, smoothed, rounded, rate, gain_ref, product_ref, columns):
    dims = (((1,), (1,)), ((), ()))

    def term(ref):
        return lax.dot_general(lhs, ref[columns, :], dims, preferred_element_type=jnp.float32)

    gained = (term(gain_ref) * term(product_ref)).astype(jnp.bfloat16).astype(jnp.float32)
    rate = jnp.concatenate([rate] * (rounded.shape[1] // LANES), axis=1)
    return smoothed + time_step * (gained - rate * rounded.astype(jnp.float32))


def joined(own_ref, other_ref, rows):
    return jnp.concatenate([own_ref[rows, :], other_ref[rows, :]], axis=1)


def faces_kernel(planes, cells, own_ref, other_ref, smoothed_ref, rate_ref, gain_ref, product_ref, state_ref, down_ref, up_ref):
    rows, group = HALO * cells, 2 * LANES
    first, last = slice(0, rows), slice((planes - HALO) * cells, planes * cells)
    lhs = jnp.concatenate(
        [joined(own_ref, other_ref, first), joined(own_ref, other_ref, last)], axis=0
    )
    rate = jnp.concatenate([rate_ref[first, :], rate_ref[last, :]], axis=0)
    for start in range(0, own_ref.shape[1], group):
        columns = slice(start, start + group)
        smoothed = jnp.concatenate([smoothed_ref[first, columns], smoothed_ref[last, columns]], axis=0)
        rounded = jnp.concatenate([own_ref[first, columns], own_ref[last, columns]], axis=0)
        state = collided(lhs, smoothed, rounded, rate, gain_ref, product_ref, columns)
        for index, part in enumerate((state[:rows], state[rows:])):
            state_ref[index, :, columns] = part
            power = exponent_of(jnp.max(jnp.abs(part), axis=0, keepdims=True))
            scaled = part * jnp.exp2(power)
            head = jnp.broadcast_to(power, (HEAD, group))
            if index == 0:
                down_ref[:HEAD, columns] = head
                down_ref[HEAD:, columns] = scaled
            else:
                up_ref[:rows, columns] = scaled
                up_ref[rows:, columns] = head


def faces(own, other, smoothed, rate, gain, product, planes, cells):
    rows, width = HALO * cells, own.shape[1]
    message = jax.ShapeDtypeStruct((rows + HEAD, width), jnp.float32)
    return pl.pallas_call(
        functools.partial(faces_kernel, planes, cells),
        in_specs=[resident()] * 6,
        out_specs=[resident()] * 3,
        out_shape=[jax.ShapeDtypeStruct((2, rows, width), jnp.float32), message, message],
        compiler_params=params(grid=False),
        cost_estimate=cost(16 * rows * width * width, 30 * rows * width),
        name="faces",
    )(own, other, smoothed, rate, gain, product)


def inside_kernel(planes, cells, own_ref, other_ref, smoothed_ref, rate_ref, gain_ref, product_ref, after_ref, state_ref):
    group = 2 * LANES
    rows = slice(HALO * cells, (planes - HALO) * cells)
    lhs = joined(own_ref, other_ref, rows)
    for start in range(0, own_ref.shape[1], group):
        columns = slice(start, start + group)
        state_ref[:, columns] = collided(
            lhs, smoothed_ref[rows, columns], own_ref[rows, columns], rate_ref[rows, :],
            gain_ref, product_ref, columns,
        )


def inside(own, other, smoothed, rate, gain, product, planes, cells, after):
    rows, width = (planes - 2 * HALO) * cells, own.shape[1]
    return pl.pallas_call(
        functools.partial(inside_kernel, planes, cells),
        in_specs=[resident()] * 6 + [anywhere()],
        out_specs=resident(),
        out_shape=jax.ShapeDtypeStruct((rows, width), jnp.float32),
        compiler_params=params(grid=False),
        cost_estimate=cost(8 * rows * width * width, 20 * rows * width),
        name="inside",
    )(own, other, smoothed, rate, gain, product, after)


def final_kernel(part, own_ref, other_ref, smoothed_ref, rate_ref, gain_ref, product_ref, *refs):
    outs, scratch = refs[1:-1], refs[-1]
    rows, group = scratch.shape
    columns = slice(part * group, (part + 1) * group)
    size = 512 if rows % 512 == 0 else rows
    for start in range(0, rows, size):
        lines = slice(start, start + size)
        scratch[lines, :] = collided(
            joined(own_ref, other_ref, lines), smoothed_ref[lines, columns], own_ref[lines, columns],
            rate_ref[lines, :], gain_ref, product_ref, columns,
        )
    for index, out in enumerate(outs):
        lanes = slice(index * LANES, (index + 1) * LANES)

        def block(i):
            return pl.ds(pl.multiple_of(i * LANES, LANES), LANES)

        def peak(i, carry):
            return jnp.maximum(carry, jnp.abs(scratch[block(i), lanes]))

        top = lax.fori_loop(0, rows // LANES, peak, jnp.zeros((LANES, LANES), jnp.float32))
        power = exponent_of(jnp.max(top, axis=0, keepdims=True))
        scale = jnp.exp2(power)

        def write(i, carry):
            out[block(i), :] = scratch[block(i), lanes] * scale
            return carry

        lax.fori_loop(0, rows // LANES, write, 0)
        out[rows:, :] = jnp.broadcast_to(power, (HEAD, LANES))


def final(own, other, smoothed, rate, gain, product, part, after):
    rows, width = own.shape
    group = 2 * LANES
    shape = jax.ShapeDtypeStruct((rows + HEAD, LANES), jnp.float32)
    return pl.pallas_call(
        functools.partial(final_kernel, part),
        in_specs=[resident()] * 6 + [anywhere()],
        out_specs=[resident()] * 2,
        out_shape=[shape] * 2,
        scratch_shapes=[pltpu.VMEM((rows, group), jnp.float32)],
        compiler_params=params(grid=False),
        cost_estimate=cost(8 * rows * width * group, 20 * rows * group),
        name="final",
    )(own, other, smoothed, rate, gain, product, after)


def unpack_kernel(order, planes, cells, chip_ref, *refs):
    count = len(order)
    pieces, out, scratch = refs[:count], refs[-2], refs[-1]
    chip = chip_ref[0]
    step = pl.program_id(0)
    flat = out.reshape(LANES * planes, LANES)

    @pl.when(step == 0)
    def _():
        for mask, piece in zip(order, pieces):
            first = pl.multiple_of((chip ^ mask) * cells, cells)
            scale = jnp.exp2(-piece[planes * cells : planes * cells + 1, :])

            for x in range(planes):
                scratch[x, pl.ds(first, cells), :] = piece[x * cells : (x + 1) * cells, :] * scale

    for x in range(planes):
        part = scratch[x, pl.ds(pl.multiple_of(step * LANES, LANES), LANES), :]
        flat[pl.ds(x, LANES, stride=planes), :] = part.T


def unpack(pieces, target, chip, order, chunk, planes, cells):
    width = cells * len(order)
    steps = width // LANES
    shape = (LANES, planes, width * CHUNKS)
    specs = [pl.BlockSpec(p.shape, lambda i, s: (0, 0)) for p in pieces]
    operands = list(pieces)
    count = len(pieces)
    aliases = {}
    if target is not None:
        specs.append(pl.BlockSpec(memory_space=pl.ANY))
        operands.append(target)
        aliases = {len(operands): 0}
    return pl.pallas_call(
        functools.partial(unpack_kernel, order, planes, cells),
        grid_spec=pltpu.PrefetchScalarGridSpec(
            num_scalar_prefetch=1,
            grid=(steps,),
            in_specs=specs,
            out_specs=pl.BlockSpec((LANES, planes, LANES), lambda i, s: (0, 0, chunk * steps + i)),
            scratch_shapes=[pltpu.VMEM((planes, width, LANES), jnp.float32)],
        ),
        out_shape=jax.ShapeDtypeStruct(shape, jnp.float32),
        input_output_aliases=aliases,
        compiler_params=params([False] + [True] * count + [False] * (len(operands) - count)),
        cost_estimate=cost(1e6, 8 * LANES * planes * width),
        name="unpack",
    )(chip, *operands)


def exchange(array, mask):
    count = lax.axis_size("vel")
    return lax.ppermute(array, "vel", [(i, i ^ mask) for i in range(count)])


def shift(array, step):
    count = lax.axis_size("space")
    return lax.ppermute(array, "space", [(i, (i + step) % count) for i in range(count)])


def half(array):
    return array.astype(jnp.float16)


def full(array):
    return array.astype(jnp.float32)


def body(distribution, courant, gain_matrix, product_matrix, collision_rate):
    planes, plane = distribution.shape[1:]
    chips = lax.axis_size("vel") // 2
    member = lax.axis_index("vel").astype(jnp.int32)
    chip, core = lax.shift_right_logical(member, 1), member & 1
    order = list(range(1, chips)) + [0]
    cells = plane // (chips * CHUNKS)
    span = cells * chips
    word = jnp.stack([chip, core])

    sent = []
    for k in range(CHUNKS):
        pieces = pack(distribution, word, order, k, cells)
        sent.append(
            [a if m == 0 else full(exchange(half(a), 2 * m)) for a, m in zip(pieces, order)]
        )
    speeds, gain, product = arrange(courant, gain_matrix, product_matrix, word, order)
    rates = []
    for k in range(CHUNKS):
        own = lax.dynamic_slice_in_dim(collision_rate, k * span + chip * cells, cells, 1)
        rates.append(jnp.broadcast_to(own.reshape(planes * cells, 1), (planes * cells, LANES)))

    result = None
    states = []
    after = product
    for k in range(CHUNKS):
        up, down = messages_of(sent[k], cells, product)
        low, high = full(shift(half(up), 1)), full(shift(half(down), -1))
        local = [spread(sent[k], planes, cells)]
        smoothed, rounded = transport(speeds, low, high, local, planes, cells, after)
        other = exchange(rounded, 1)
        ends, down, up = faces(rounded, other, smoothed, rates[k], gain, product, planes, cells)
        low, high = full(shift(half(up), 1)), full(shift(half(down), -1))
        middle = inside(rounded, other, smoothed, rates[k], gain, product, planes, cells, ends)
        states.append((low, high, [ends, middle]))
        after = middle
    for k in range(CHUNKS):
        low, high, parts = states[k]
        smoothed, rounded = transport(speeds, low, high, parts, planes, cells, after)
        other = exchange(rounded, 1)
        ready = []
        for part in range(chips // 2):
            ready += final(rounded, other, smoothed, rates[k], gain, product, part, (ready or [gain])[0])
        after = ready[-1]
        back = [a if m == 0 else full(exchange(half(a), 2 * m)) for a, m in zip(ready, order)]
        result = unpack(back, result, word, order, k, planes, cells)
    return result


def fits(mesh, shape, spaces):
    groups = mesh.shape["vel"]
    local, planes = shape[0] // groups, shape[1] // spaces
    chips = groups // 2
    return (
        groups % 4 == 0
        and chips & (chips - 1) == 0
        and local == LANES
        and planes % HALO == 0
        and planes >= 3 * HALO
        and shape[2] % (CHUNKS * LANES) == 0
        and shape[2] % (CHUNKS * chips * 16) == 0
    )


def solution(mesh):
    in_specs = (P("vel", "space", None), P(), P(), P(), P("space", None))
    out_specs = P("vel", "space", None)

    def run(distribution, courant, gain_matrix, product_matrix, collision_rate):
        special = fits(mesh, distribution.shape, mesh.shape["space"])
        return jax.shard_map(
            body if special else general_body,
            mesh=mesh, in_specs=in_specs, out_specs=out_specs, check_vma=False,
        )(distribution, courant, gain_matrix, product_matrix, collision_rate)

    return run
```

```python
import functools

import jax
import jax.numpy as jnp
from jax import lax
from jax.experimental import pallas as pl
from jax.experimental.pallas import tpu as pltpu
from jax.sharding import PartitionSpec as P

STEPS = 2
HALO = 4
WIDE = 2 * HALO
HEAD = 16
CHUNKS = 2
LANES = 128
QUARTERS = 4
VMEM = 12 * 1024 * 1024

time_step = 0.2


def with_halo(block, sides, width):
    for axis, dim in sides:
        count = lax.axis_size(axis)
        forward = [(i, i + 1) for i in range(count - 1)]
        forward.append((count - 1, 0))
        backward = [(target, source) for source, target in forward]
        low = lax.ppermute(
            lax.slice_in_dim(block, block.shape[dim] - width, None, axis=dim), axis, forward
        )
        high = lax.ppermute(lax.slice_in_dim(block, 0, width, axis=dim), axis, backward)
        block = jnp.concatenate([low, block, high], axis=dim)
    return block


def minmod(first, second):
    return jnp.maximum(jnp.minimum(first, second), 0.0) + jnp.minimum(
        jnp.maximum(first, second), 0.0
    )


def change(widened, speeds):
    differ = widened[:, 1:] - widened[:, :-1]
    slopes = minmod(differ[:, 1:], differ[:, :-1])
    inner = widened.shape[1] - 4
    left_value = widened[:, 1 : inner + 2]
    right_value = widened[:, 2 : inner + 3]
    left_slope = slopes[:, 0 : inner + 1]
    right_slope = slopes[:, 1 : inner + 2]
    upward = jnp.maximum(speeds, 0.0)
    downward = jnp.minimum(speeds, 0.0)
    fluxes = upward * (left_value + 0.5 * (1.0 - speeds) * left_slope) + downward * (
        right_value - 0.5 * (1.0 + speeds) * right_slope
    )
    return -(fluxes[:, 1:] - fluxes[:, :-1])


def extend(field):
    return with_halo(field, (("space", 1),), 2)


def advect(field, speeds):
    section = field + change(extend(field), speeds)
    return 0.5 * field + 0.5 * (section + change(extend(section), speeds))


def collide(pieces, gain_matrix, product_matrix):
    columns = pieces.reshape(pieces.shape[0], -1)
    first_term = jnp.dot(gain_matrix, columns, preferred_element_type=jnp.float32)
    second_term = jnp.dot(product_matrix, columns, preferred_element_type=jnp.float32)
    return (first_term * second_term).astype(jnp.bfloat16).reshape(pieces.shape)


def update(smoothed, rounded, gained, rate):
    return smoothed + time_step * (gained.astype(jnp.float32) - rate * rounded.astype(jnp.float32))


def general_body(distribution, courant, gain_matrix, product_matrix, collision_rate):
    local_count = distribution.shape[0]
    groups = lax.axis_size("vel")
    member = lax.axis_index("vel")
    own_speeds = lax.dynamic_slice_in_dim(courant, member * local_count, local_count, 0)[
        :, None, None
    ]
    field = distribution
    for step_index in range(STEPS):
        smoothed = advect(field, own_speeds)
        rounded = smoothed.astype(jnp.bfloat16)
        grouped = rounded.reshape(local_count, groups, -1)
        gained = lax.all_to_all(
            collide(
                lax.all_to_all(grouped, "vel", split_axis=1, concat_axis=0, tiled=True),
                gain_matrix,
                product_matrix,
            ),
            "vel",
            split_axis=0,
            concat_axis=1,
            tiled=True,
        )
        field = update(smoothed, rounded, gained.reshape(rounded.shape), collision_rate[None])
    return field


def params(fusable=None, grid=True):
    return pltpu.CompilerParams(
        dimension_semantics=("arbitrary",) if grid else None,
        vmem_limit_bytes=VMEM,
        allow_input_fusion=fusable,
    )


def resident():
    return pl.BlockSpec(memory_space=pltpu.VMEM)


def anywhere():
    return pl.BlockSpec(memory_space=pl.ANY)


def cost(flops, moved):
    return pl.CostEstimate(flops=1000, bytes_accessed=1000, transcendentals=0)


def exponent_of(largest):
    power = jnp.floor(14.0 - jnp.log2(jnp.maximum(largest, 1e-36)))
    return jnp.clip(power, -115.0, 120.0)


def pack_kernel(order, planes, cells, chip_ref, d_ref, after_ref, *refs):
    outs, scratch = refs[:-1], refs[-1]
    chip = chip_ref[0]
    step = pl.program_id(0)
    rows = d_ref.reshape(LANES * planes, LANES)
    for x in range(planes):
        part = rows[pl.ds(x, LANES, stride=planes), :]
        scratch[x, pl.ds(pl.multiple_of(step * LANES, LANES), LANES), :] = part.T

    @pl.when(step == pl.num_programs(0) - 1)
    def _():
        for mask, out in zip(order, outs):
            first = pl.multiple_of((chip ^ mask) * cells, cells)

            def peak(x, carry):
                return jnp.maximum(carry, jnp.abs(scratch[x, pl.ds(first, cells), :]))

            top = lax.fori_loop(0, planes, peak, jnp.zeros((cells, LANES), jnp.float32))
            power = exponent_of(jnp.max(top, axis=0, keepdims=True))
            scale = jnp.exp2(power)

            def write(x, carry):
                start = place_of(x, cells)
                out[pl.ds(pl.multiple_of(start, 16), cells), :] = (
                    scratch[x, pl.ds(first, cells), :] * scale
                )
                return carry

            lax.fori_loop(0, planes, write, 0)
            out[WIDE * cells : WIDE * cells + HEAD, :] = jnp.broadcast_to(power, (HEAD, LANES))


def place_of(x, cells):
    if isinstance(x, int):
        return x * cells + (HEAD if x >= WIDE else 0)
    return x * cells + jnp.where(x >= WIDE, HEAD, 0)


def pack(distribution, chip, order, chunk, cells, after):
    planes = distribution.shape[1]
    width = cells * len(order)
    steps = width // LANES
    shape = (planes * cells + HEAD, LANES)
    return pl.pallas_call(
        functools.partial(pack_kernel, order, planes, cells),
        grid_spec=pltpu.PrefetchScalarGridSpec(
            num_scalar_prefetch=1,
            grid=(steps,),
            in_specs=[
                pl.BlockSpec((LANES, planes, LANES), lambda i, s: (0, 0, chunk * steps + i)),
                anywhere(),
            ],
            out_specs=[resident() for _ in order],
            scratch_shapes=[pltpu.VMEM((planes, width, LANES), jnp.float32)],
        ),
        out_shape=[jax.ShapeDtypeStruct(shape, jnp.float32) for _ in order],
        compiler_params=params(),
        cost_estimate=cost(1e6, 8 * LANES * planes * width),
        name="pack",
    )(chip, pltpu.with_memory_space_constraint(distribution, pltpu.HBM), after)


def message_kernel(cells, *refs):
    pieces, out = refs[:-2], refs[-1]
    for index, piece in enumerate(pieces):
        out[:, index * LANES : (index + 1) * LANES] = piece[: WIDE * cells + HEAD, :]


def message_of(pieces, cells, after):
    shape = (WIDE * cells + HEAD, LANES * len(pieces))
    return pl.pallas_call(
        functools.partial(message_kernel, cells),
        grid=(1,),
        in_specs=[pl.BlockSpec(p.shape, lambda i: (0, 0)) for p in pieces] + [anywhere()],
        out_specs=resident(),
        out_shape=jax.ShapeDtypeStruct(shape, jnp.float32),
        compiler_params=params([True] * len(pieces) + [False]),
        cost_estimate=cost(1e5, 8 * shape[0] * shape[1]),
        name="message",
    )(*pieces, after)


def spread_kernel(planes, cells, *refs):
    pieces, out = refs[:-2], refs[-1]
    rows = WIDE * cells
    for index, piece in enumerate(pieces):
        columns = slice(index * LANES, (index + 1) * LANES)
        scale = jnp.exp2(-piece[rows : rows + 1, :])
        for x in range(planes):
            start = place_of(x, cells)
            out[x * cells : (x + 1) * cells, columns] = piece[start : start + cells, :] * scale


def spread(pieces, planes, cells, after):
    shape = (planes * cells, LANES * len(pieces))
    return pl.pallas_call(
        functools.partial(spread_kernel, planes, cells),
        grid=(1,),
        in_specs=[pl.BlockSpec(p.shape, lambda i: (0, 0)) for p in pieces] + [anywhere()],
        out_specs=resident(),
        out_shape=jax.ShapeDtypeStruct(shape, jnp.float32),
        compiler_params=params([True] * len(pieces) + [False]),
        cost_estimate=cost(1e6, 8 * shape[0] * shape[1]),
        name="spread",
    )(*pieces, after)


def arrange_kernel(order, planes, cells, word_ref, c_ref, rate_ref, next_ref, g_ref, p_ref, after_ref, speeds_ref, gain_ref, product_ref, *refs):
    rates, scratch = refs[:-1], refs[-1]
    chip, core = word_ref[0], word_ref[1]
    count = len(order)
    for row, mask in enumerate(order):
        own = 2 * (chip ^ mask) + core
        lines = slice(row * LANES, (row + 1) * LANES)
        speeds_ref[:, lines] = jnp.broadcast_to(c_ref[pl.ds(own, 1), :], (8, LANES))
        source = pl.ds(pl.multiple_of(own * LANES, LANES), LANES)
        for column in range(2 * count):
            other = order[column % count]
            block = 2 * (chip ^ other) + (core if column < count else 1 - core)
            lanes = pl.ds(pl.multiple_of(block * LANES, LANES), LANES)
            target = slice(column * LANES, (column + 1) * LANES)
            gain_ref[lines, target] = g_ref[source, lanes]
            product_ref[lines, target] = p_ref[source, lanes]
    tall = jnp.concatenate([rate_ref[...], next_ref[...]], axis=0)
    tall = jnp.concatenate([tall, jnp.zeros((LANES - tall.shape[0], tall.shape[1]), jnp.float32)], axis=0)
    for lane in range(0, tall.shape[1], LANES):
        scratch[lane : lane + LANES, :] = tall[:, lane : lane + LANES].T
    for k in range(len(rates) // 2):
        first = pl.multiple_of((k * count + chip) * cells, cells)
        part = scratch[pl.ds(first, cells), :]
        for x in range(planes + HALO):
            wide = jnp.broadcast_to(part[:, x : x + 1], (cells, LANES))
            if x >= HALO:
                rates[2 * k][(x - HALO) * cells : (x - HALO + 1) * cells, :] = wide
            if x < planes:
                rates[2 * k + 1][x * cells : (x + 1) * cells, :] = wide


def arrange(courant, collision_rate, next_rate, gain_matrix, product_matrix, word, order, cells, after):
    count = len(order)
    planes, plane = collision_rate.shape
    shape = (count * LANES, 2 * count * LANES)
    rate = jax.ShapeDtypeStruct((planes * cells, LANES), jnp.float32)
    results = pl.pallas_call(
        functools.partial(arrange_kernel, order, planes, cells),
        in_specs=[pl.BlockSpec(memory_space=pltpu.SMEM)] + [resident()] * 5 + [anywhere()],
        out_specs=[resident()] * (3 + 2 * CHUNKS),
        out_shape=[
            jax.ShapeDtypeStruct((8, count * LANES), jnp.float32),
            jax.ShapeDtypeStruct(shape, jnp.bfloat16),
            jax.ShapeDtypeStruct(shape, jnp.bfloat16),
        ]
        + [rate] * (2 * CHUNKS),
        scratch_shapes=[pltpu.VMEM((plane, LANES), jnp.float32)],
        compiler_params=params(grid=False),
        cost_estimate=cost(1e5, 12 * shape[0] * shape[1]),
        name="arrange",
    )(word, courant.reshape(-1, LANES), collision_rate, next_rate, gain_matrix, product_matrix, after)
    return results[0], results[1], results[2], results[3::2], results[4::2]


def stage(values, speed, bend, positive):
    differ = [b - a for a, b in zip(values[:-1], values[1:])]
    slopes = [
        jnp.maximum(jnp.minimum(a, b), jnp.minimum(jnp.maximum(a, b), 0.0))
        for a, b in zip(differ[:-1], differ[1:])
    ]
    inner = [speed * u + bend * s for u, s in zip(values[1:-1], slopes)]
    faces = [jnp.where(positive, a, b) for a, b in zip(inner[:-1], inner[1:])]
    return [u - (b - a) for u, a, b in zip(values[2:-2], faces[:-1], faces[1:])]


def advect_kernel(cells, tile, before, c_ref, extra_ref, *refs):
    bodies, smoothed_ref, pieces = refs[: -2 - QUARTERS], refs[-1 - QUARTERS], refs[-QUARTERS:]
    rows = WIDE * cells
    sources = [(extra_ref, x * cells) for x in range(WIDE)] if before else []
    for ref in bodies:
        sources += [(ref, x * cells) for x in range(ref.shape[0] // cells)]
    if not before:
        sources += [(extra_ref, x * cells) for x in range(WIDE)]
    planes = len(sources) - WIDE
    share = planes // QUARTERS

    def column(j, outer):
        lanes = pl.ds(pl.multiple_of(j * LANES, LANES), LANES)
        speed = c_ref[0:1, lanes]
        size = jnp.abs(speed)
        bend = 0.5 * size * (1.0 - size)
        positive = jnp.broadcast_to(speed, (tile, LANES)) > 0.0
        back = jnp.exp2(-extra_ref[rows : rows + 1, lanes])

        def body(t, carry):
            start = t * tile

            def read(x):
                ref, first = sources[x]
                value = ref[pl.ds(pl.multiple_of(first + start, tile), tile), lanes]
                return value * back if ref is extra_ref else value

            section = stage([read(x) for x in range(len(sources))], speed, bend, positive)
            moved = stage(section, speed, bend, positive)
            for x in range(planes):
                result = 0.5 * read(x + HALO) + 0.5 * moved[x]
                smoothed_ref[pl.ds(pl.multiple_of(x * cells + start, tile), tile), lanes] = result
                where = pl.ds(pl.multiple_of((x % share) * cells + start, tile), tile)
                pieces[x // share][where, lanes] = result.astype(jnp.bfloat16)
            return carry

        return lax.fori_loop(0, cells // tile, body, outer)

    lax.fori_loop(0, extra_ref.shape[1] // LANES, column, 0)


def transport(speeds, extra, bodies, before, planes, cells, after):
    rows, width = planes * cells, extra.shape[1]
    results = pl.pallas_call(
        functools.partial(advect_kernel, cells, 16, before),
        in_specs=[resident()] * (2 + len(bodies)) + [anywhere()],
        out_specs=[resident()] * (1 + QUARTERS),
        out_shape=[jax.ShapeDtypeStruct((rows, width), jnp.float32)]
        + [jax.ShapeDtypeStruct((rows // QUARTERS, width), jnp.bfloat16)] * QUARTERS,
        compiler_params=params(grid=False),
        cost_estimate=cost(40 * rows * width, 12 * rows * width),
        name="transport",
    )(speeds, extra, *bodies, after)
    return results[0], results[1:]


def collided(lhs, smoothed, rounded, rate, gain_ref, product_ref, columns):
    dims = (((1,), (1,)), ((), ()))

    def term(ref):
        return lax.dot_general(lhs, ref[columns, :], dims, preferred_element_type=jnp.float32)

    gained = (term(gain_ref) * term(product_ref)).astype(jnp.bfloat16).astype(jnp.float32)
    rate = jnp.concatenate([rate] * (rounded.shape[1] // LANES), axis=1)
    return smoothed + time_step * (gained - rate * rounded.astype(jnp.float32))


def joined(own_refs, other_refs):
    return jnp.concatenate(
        [
            jnp.concatenate([own[...], other[...]], axis=1)
            for own, other in zip(own_refs, other_refs)
        ],
        axis=0,
    )


def half_kernel(count, first, sends, *refs):
    own, other = refs[:count], refs[count : 2 * count]
    smoothed_ref, rate_ref, gain_ref, product_ref, _, state_ref = refs[2 * count : 2 * count + 6]
    size, width = state_ref.shape
    group = 2 * LANES
    lines = slice(first, first + size)
    lhs = joined(own, other)
    for start in range(0, width, group):
        columns = slice(start, start + group)
        state = collided(
            lhs, smoothed_ref[lines, columns], lhs[:, columns], rate_ref[lines, :],
            gain_ref, product_ref, columns,
        )
        state_ref[:, columns] = state
        if sends:
            message_ref = refs[-1]
            power = exponent_of(jnp.max(jnp.abs(state), axis=0, keepdims=True))
            message_ref[:size, columns] = state * jnp.exp2(power)
            message_ref[size:, columns] = jnp.broadcast_to(power, (HEAD, group))


def collide_half(own, other, smoothed, rate, gain, product, first, sends, after):
    width = smoothed.shape[1]
    rows = sum(a.shape[0] for a in own)
    shapes = [jax.ShapeDtypeStruct((rows, width), jnp.float32)]
    if sends:
        shapes.append(jax.ShapeDtypeStruct((rows + HEAD, width), jnp.float32))
    return pl.pallas_call(
        functools.partial(half_kernel, len(own), first, sends),
        in_specs=[resident()] * (2 * len(own) + 4) + [anywhere()],
        out_specs=[resident()] * len(shapes),
        out_shape=shapes,
        compiler_params=params(grid=False),
        cost_estimate=cost(8 * rows * width * width, 20 * rows * width),
        name="faces" if sends else "inside",
    )(*own, *other, smoothed, rate, gain, product, after)


def final_kernel(part, *refs):
    own, other = refs[:QUARTERS], refs[QUARTERS : 2 * QUARTERS]
    smoothed_ref, rate_ref, gain_ref, product_ref = refs[2 * QUARTERS : 2 * QUARTERS + 4]
    outs, scratch = refs[2 * QUARTERS + 5 : -1], refs[-1]
    rows, group = scratch.shape
    columns = slice(part * group, (part + 1) * group)
    half = QUARTERS // 2
    size = rows // 2
    for index in range(2):
        lines = slice(index * size, (index + 1) * size)
        lhs = joined(own[index * half : (index + 1) * half], other[index * half : (index + 1) * half])
        scratch[lines, :] = collided(
            lhs, smoothed_ref[lines, columns], lhs[:, columns], rate_ref[lines, :],
            gain_ref, product_ref, columns,
        )
    for index, out in enumerate(outs):
        lanes = slice(index * LANES, (index + 1) * LANES)

        def block(i):
            return pl.ds(pl.multiple_of(i * LANES, LANES), LANES)

        def peak(i, carry):
            return jnp.maximum(carry, jnp.abs(scratch[block(i), lanes]))

        top = lax.fori_loop(0, rows // LANES, peak, jnp.zeros((LANES, LANES), jnp.float32))
        power = exponent_of(jnp.max(top, axis=0, keepdims=True))
        scale = jnp.exp2(power)

        def write(i, carry):
            out[block(i), :] = scratch[block(i), lanes] * scale
            return carry

        lax.fori_loop(0, rows // LANES, write, 0)
        out[rows:, :] = jnp.broadcast_to(power, (HEAD, LANES))


def final(own, other, smoothed, rate, gain, product, part, after):
    rows, width = smoothed.shape
    group = 2 * LANES
    shape = jax.ShapeDtypeStruct((rows + HEAD, LANES), jnp.float32)
    return pl.pallas_call(
        functools.partial(final_kernel, part),
        in_specs=[resident()] * (2 * QUARTERS + 4) + [anywhere()],
        out_specs=[resident()] * 2,
        out_shape=[shape] * 2,
        scratch_shapes=[pltpu.VMEM((rows, group), jnp.float32)],
        compiler_params=params(grid=False),
        cost_estimate=cost(8 * rows * width * group, 20 * rows * group),
        name="final",
    )(*own, *other, smoothed, rate, gain, product, after)


def unpack_kernel(order, planes, cells, chip_ref, *refs):
    count = len(order)
    pieces, out, scratch = refs[:count], refs[-2], refs[-1]
    chip = chip_ref[0]
    step = pl.program_id(0)
    flat = out.reshape(LANES * planes, LANES)

    @pl.when(step == 0)
    def _():
        for mask, piece in zip(order, pieces):
            first = pl.multiple_of((chip ^ mask) * cells, cells)
            scale = jnp.exp2(-piece[planes * cells : planes * cells + 1, :])

            for x in range(planes):
                scratch[x, pl.ds(first, cells), :] = piece[x * cells : (x + 1) * cells, :] * scale

    for x in range(planes):
        part = scratch[x, pl.ds(pl.multiple_of(step * LANES, LANES), LANES), :]
        flat[pl.ds(x, LANES, stride=planes), :] = part.T


def unpack(pieces, target, chip, order, chunk, planes, cells, after):
    width = cells * len(order)
    steps = width // LANES
    shape = (LANES, planes, width * CHUNKS)
    specs = [pl.BlockSpec(p.shape, lambda i, s: (0, 0)) for p in pieces]
    operands = list(pieces)
    count = len(pieces)
    specs.append(anywhere())
    operands.append(after)
    aliases = {}
    if target is not None:
        specs.append(pl.BlockSpec(memory_space=pl.ANY))
        operands.append(target)
        aliases = {len(operands): 0}
    return pl.pallas_call(
        functools.partial(unpack_kernel, order, planes, cells),
        grid_spec=pltpu.PrefetchScalarGridSpec(
            num_scalar_prefetch=1,
            grid=(steps,),
            in_specs=specs,
            out_specs=pl.BlockSpec((LANES, planes, LANES), lambda i, s: (0, 0, chunk * steps + i)),
            scratch_shapes=[pltpu.VMEM((planes, width, LANES), jnp.float32)],
        ),
        out_shape=jax.ShapeDtypeStruct(shape, jnp.float32),
        input_output_aliases=aliases,
        compiler_params=params([False] + [True] * count + [False] * (len(operands) - count)),
        cost_estimate=cost(1e6, 8 * LANES * planes * width),
        name="unpack",
    )(chip, *operands)


def exchange(array, mask):
    count = lax.axis_size("vel")
    return lax.ppermute(array, "vel", [(i, i ^ mask) for i in range(count)])


def shift(array, step):
    count = lax.axis_size("space")
    return lax.ppermute(array, "space", [(i, (i + step) % count) for i in range(count)])


def half(array):
    return array.astype(jnp.float16)


def full(array):
    return array.astype(jnp.float32)


def body(distribution, courant, gain_matrix, product_matrix, collision_rate):
    planes, plane = distribution.shape[1:]
    chips = lax.axis_size("vel") // 2
    member = lax.axis_index("vel").astype(jnp.int32)
    chip, core = lax.shift_right_logical(member, 1), member & 1
    order = list(range(1, chips)) + [0]
    cells = plane // (chips * CHUNKS)
    span = cells * chips
    word = jnp.stack([chip, core])

    every = range(CHUNKS)
    sent, extra, local, state = {}, {}, {}, {}
    after = distribution
    for k in every:
        pieces = pack(distribution, word, order, k, cells, after)
        after = pieces[-1]
        sent[k] = [
            a if m == 0 else full(exchange(half(a), 2 * m)) for a, m in zip(pieces, order)
        ]
    speeds, gain, product, shifted_rates, rates = arrange(
        courant, collision_rate, shift(collision_rate[:8], -1), gain_matrix, product_matrix,
        word, order, cells, after,
    )
    after = product
    for k in every:
        message = message_of(sent[k], cells, after)
        extra[k] = shift(half(message), -1)
        local[k] = after = spread(sent[k], planes, cells, message)
    middle = QUARTERS // 2
    for k in every:
        arrived, after = lax.optimization_barrier((extra[k], after))
        smoothed, own = transport(speeds, full(arrived), [local[k]], False, planes, cells, after)
        other = [exchange(a, 1) for a in own]
        upper, message = collide_half(
            own[middle:], other[middle:], smoothed, shifted_rates[k], gain, product,
            WIDE * cells, True, after,
        )
        extra[k] = shift(half(message), 1)
        (lower,) = collide_half(
            own[:middle], other[:middle], smoothed, shifted_rates[k], gain, product,
            0, False, message,
        )
        state[k] = [lower, upper]
        after = lower
    back = {}
    for k in every:
        arrived, after = lax.optimization_barrier((extra[k], after))
        smoothed, own = transport(speeds, full(arrived), state[k], True, planes, cells, after)
        other = [exchange(a, 1) for a in own]
        ready = []
        for part in range(chips // 2):
            ready += final(own, other, smoothed, rates[k], gain, product, part, after)
            after = ready[-1]
        back[k] = [a if m == 0 else full(exchange(half(a), 2 * m)) for a, m in zip(ready, order)]
    result = None
    for k in every:
        result = unpack(back[k], result, word, order, k, planes, cells, after)
    return result


def fits(mesh, shape, spaces):
    groups = mesh.shape["vel"]
    local, planes = shape[0] // groups, shape[1] // spaces
    chips = groups // 2
    return (
        groups % 4 == 0
        and chips & (chips - 1) == 0
        and local == LANES
        and planes == 2 * WIDE
        and shape[2] % (CHUNKS * LANES) == 0
        and shape[2] % (CHUNKS * chips * 16) == 0
    )


def solution(mesh):
    in_specs = (P("vel", "space", None), P(), P(), P(), P("space", None))
    out_specs = P("vel", "space", None)

    def run(distribution, courant, gain_matrix, product_matrix, collision_rate):
        special = fits(mesh, distribution.shape, mesh.shape["space"])
        return jax.shard_map(
            body if special else general_body,
            mesh=mesh, in_specs=in_specs, out_specs=out_specs, check_vma=False,
        )(distribution, courant, gain_matrix, product_matrix, collision_rate)

    return run
```

```python
import functools

import jax
import jax.numpy as jnp
from jax import lax
from jax.experimental import pallas as pl
from jax.experimental.pallas import tpu as pltpu
from jax.sharding import PartitionSpec as P

STEPS = 2
HALO = 4
WIDE = 2 * HALO
HEAD = 8
CHUNKS = 2
LANES = 128
QUARTERS = 4
VMEM = 12 * 1024 * 1024

time_step = 0.2


def with_halo(block, sides, width):
    for axis, dim in sides:
        count = lax.axis_size(axis)
        forward = [(i, i + 1) for i in range(count - 1)]
        forward.append((count - 1, 0))
        backward = [(target, source) for source, target in forward]
        low = lax.ppermute(
            lax.slice_in_dim(block, block.shape[dim] - width, None, axis=dim), axis, forward
        )
        high = lax.ppermute(lax.slice_in_dim(block, 0, width, axis=dim), axis, backward)
        block = jnp.concatenate([low, block, high], axis=dim)
    return block


def minmod(first, second):
    return jnp.maximum(jnp.minimum(first, second), 0.0) + jnp.minimum(
        jnp.maximum(first, second), 0.0
    )


def change(widened, speeds):
    differ = widened[:, 1:] - widened[:, :-1]
    slopes = minmod(differ[:, 1:], differ[:, :-1])
    inner = widened.shape[1] - 4
    left_value = widened[:, 1 : inner + 2]
    right_value = widened[:, 2 : inner + 3]
    left_slope = slopes[:, 0 : inner + 1]
    right_slope = slopes[:, 1 : inner + 2]
    upward = jnp.maximum(speeds, 0.0)
    downward = jnp.minimum(speeds, 0.0)
    fluxes = upward * (left_value + 0.5 * (1.0 - speeds) * left_slope) + downward * (
        right_value - 0.5 * (1.0 + speeds) * right_slope
    )
    return -(fluxes[:, 1:] - fluxes[:, :-1])


def extend(field):
    return with_halo(field, (("space", 1),), 2)


def advect(field, speeds):
    section = field + change(extend(field), speeds)
    return 0.5 * field + 0.5 * (section + change(extend(section), speeds))


def collide(pieces, gain_matrix, product_matrix):
    columns = pieces.reshape(pieces.shape[0], -1)
    first_term = jnp.dot(gain_matrix, columns, preferred_element_type=jnp.float32)
    second_term = jnp.dot(product_matrix, columns, preferred_element_type=jnp.float32)
    return (first_term * second_term).astype(jnp.bfloat16).reshape(pieces.shape)


def update(smoothed, rounded, gained, rate):
    return smoothed + time_step * (gained.astype(jnp.float32) - rate * rounded.astype(jnp.float32))


def general_body(distribution, courant, gain_matrix, product_matrix, collision_rate):
    local_count = distribution.shape[0]
    groups = lax.axis_size("vel")
    member = lax.axis_index("vel")
    own_speeds = lax.dynamic_slice_in_dim(courant, member * local_count, local_count, 0)[
        :, None, None
    ]
    field = distribution
    for step_index in range(STEPS):
        smoothed = advect(field, own_speeds)
        rounded = smoothed.astype(jnp.bfloat16)
        grouped = rounded.reshape(local_count, groups, -1)
        gained = lax.all_to_all(
            collide(
                lax.all_to_all(grouped, "vel", split_axis=1, concat_axis=0, tiled=True),
                gain_matrix,
                product_matrix,
            ),
            "vel",
            split_axis=0,
            concat_axis=1,
            tiled=True,
        )
        field = update(smoothed, rounded, gained.reshape(rounded.shape), collision_rate[None])
    return field


def params(fusable=None, grid=True):
    return pltpu.CompilerParams(
        dimension_semantics=("arbitrary",) if grid else None,
        vmem_limit_bytes=VMEM,
        allow_input_fusion=fusable,
    )


def resident():
    return pl.BlockSpec(memory_space=pltpu.VMEM)


def anywhere():
    return pl.BlockSpec(memory_space=pl.ANY)


LIGHT = pl.CostEstimate(flops=1000, bytes_accessed=1000, transcendentals=0)


def exponent_of(largest):
    power = jnp.floor(14.0 - jnp.log2(jnp.maximum(largest, 1e-36)))
    return jnp.clip(power, -115.0, 120.0)


def pack_kernel(order, planes, cells, chip_ref, d_ref, after_ref, *refs):
    outs, scratch = refs[:-1], refs[-1]
    chip = chip_ref[0]
    step = pl.program_id(0)
    rows = d_ref.reshape(LANES * planes, LANES)
    for x in range(planes):
        part = rows[pl.ds(x, LANES, stride=planes), :]
        scratch[x, pl.ds(pl.multiple_of(step * LANES, LANES), LANES), :] = part.T

    @pl.when(step == pl.num_programs(0) - 1)
    def _():
        for mask, out in zip(order, outs):
            first = pl.multiple_of((chip ^ mask) * cells, cells)

            def peak(x, carry):
                return jnp.maximum(carry, jnp.abs(scratch[x, pl.ds(first, cells), :]))

            top = lax.fori_loop(0, planes, peak, jnp.zeros((cells, LANES), jnp.float32))
            power = exponent_of(jnp.max(top, axis=0, keepdims=True))
            scale = jnp.exp2(power)

            def write(x, carry):
                start = place_of(x, cells)
                out[pl.ds(pl.multiple_of(start, HEAD), cells), :] = (
                    scratch[x, pl.ds(first, cells), :] * scale
                )
                return carry

            lax.fori_loop(0, planes, write, 0)
            out[WIDE * cells : WIDE * cells + HEAD, :] = jnp.broadcast_to(power, (HEAD, LANES))


def place_of(x, cells):
    if isinstance(x, int):
        return x * cells + (HEAD if x >= WIDE else 0)
    return x * cells + jnp.where(x >= WIDE, HEAD, 0)


def pack(distribution, chip, order, chunk, cells, after):
    planes = distribution.shape[1]
    width = cells * len(order)
    steps = width // LANES
    shape = (planes * cells + HEAD, LANES)
    return pl.pallas_call(
        functools.partial(pack_kernel, order, planes, cells),
        grid_spec=pltpu.PrefetchScalarGridSpec(
            num_scalar_prefetch=1,
            grid=(steps,),
            in_specs=[
                pl.BlockSpec((LANES, planes, LANES), lambda i, s: (0, 0, chunk * steps + i)),
                anywhere(),
            ],
            out_specs=[resident() for _ in order],
            scratch_shapes=[pltpu.VMEM((planes, width, LANES), jnp.float32)],
        ),
        out_shape=[jax.ShapeDtypeStruct(shape, jnp.float32) for _ in order],
        compiler_params=params(),
        cost_estimate=LIGHT,
        name="pack",
    )(chip, pltpu.with_memory_space_constraint(distribution, pltpu.HBM), after)


def message_kernel(cells, *refs):
    pieces, out = refs[:-2], refs[-1]
    for index, piece in enumerate(pieces):
        out[:, index * LANES : (index + 1) * LANES] = piece[: WIDE * cells + HEAD, :]


def message_of(pieces, cells, after):
    shape = (WIDE * cells + HEAD, LANES * len(pieces))
    return pl.pallas_call(
        functools.partial(message_kernel, cells),
        grid=(1,),
        in_specs=[pl.BlockSpec(p.shape, lambda i: (0, 0)) for p in pieces] + [anywhere()],
        out_specs=resident(),
        out_shape=jax.ShapeDtypeStruct(shape, jnp.float32),
        compiler_params=params([True] * len(pieces) + [False]),
        cost_estimate=LIGHT,
        name="message",
    )(*pieces, after)


def spread_kernel(planes, cells, *refs):
    pieces, out = refs[:-2], refs[-1]
    rows = WIDE * cells
    for index, piece in enumerate(pieces):
        columns = slice(index * LANES, (index + 1) * LANES)
        scale = jnp.exp2(-piece[rows : rows + 1, :])
        for x in range(planes):
            start = place_of(x, cells)
            out[x * cells : (x + 1) * cells, columns] = piece[start : start + cells, :] * scale


def spread(pieces, planes, cells, after):
    shape = (planes * cells, LANES * len(pieces))
    return pl.pallas_call(
        functools.partial(spread_kernel, planes, cells),
        grid=(1,),
        in_specs=[pl.BlockSpec(p.shape, lambda i: (0, 0)) for p in pieces] + [anywhere()],
        out_specs=resident(),
        out_shape=jax.ShapeDtypeStruct(shape, jnp.float32),
        compiler_params=params([True] * len(pieces) + [False]),
        cost_estimate=LIGHT,
        name="spread",
    )(*pieces, after)


def arrange_kernel(order, planes, cells, word_ref, c_ref, rate_ref, next_ref, g_ref, p_ref, after_ref, speeds_ref, gain_ref, product_ref, *refs):
    rates, scratch = refs[:-1], refs[-1]
    chip, core = word_ref[0], word_ref[1]
    count = len(order)
    for row, mask in enumerate(order):
        own = 2 * (chip ^ mask) + core
        lines = slice(row * LANES, (row + 1) * LANES)
        speeds_ref[:, lines] = jnp.broadcast_to(c_ref[pl.ds(own, 1), :], (8, LANES))
        source = pl.ds(pl.multiple_of(own * LANES, LANES), LANES)
        for column in range(2 * count):
            other = order[column % count]
            block = 2 * (chip ^ other) + (core if column < count else 1 - core)
            lanes = pl.ds(pl.multiple_of(block * LANES, LANES), LANES)
            target = slice(column * LANES, (column + 1) * LANES)
            gain_ref[lines, target] = g_ref[source, lanes]
            product_ref[lines, target] = p_ref[source, lanes]
    tall = jnp.concatenate([rate_ref[...], next_ref[...]], axis=0)
    tall = jnp.concatenate([tall, jnp.zeros((LANES - tall.shape[0], tall.shape[1]), jnp.float32)], axis=0)
    for lane in range(0, tall.shape[1], LANES):
        scratch[lane : lane + LANES, :] = tall[:, lane : lane + LANES].T
    for k in range(len(rates) // 2):
        first = pl.multiple_of((k * count + chip) * cells, cells)
        part = scratch[pl.ds(first, cells), :]
        for x in range(planes + HALO):
            wide = jnp.broadcast_to(part[:, x : x + 1], (cells, LANES))
            if x >= HALO:
                rates[2 * k][(x - HALO) * cells : (x - HALO + 1) * cells, :] = wide
            if x < planes:
                rates[2 * k + 1][x * cells : (x + 1) * cells, :] = wide


def arrange(courant, collision_rate, next_rate, gain_matrix, product_matrix, word, order, cells, after):
    count = len(order)
    planes, plane = collision_rate.shape
    shape = (count * LANES, 2 * count * LANES)
    rate = jax.ShapeDtypeStruct((planes * cells, LANES), jnp.float32)
    results = pl.pallas_call(
        functools.partial(arrange_kernel, order, planes, cells),
        in_specs=[pl.BlockSpec(memory_space=pltpu.SMEM)] + [resident()] * 5 + [anywhere()],
        out_specs=[resident()] * (3 + 2 * CHUNKS),
        out_shape=[
            jax.ShapeDtypeStruct((8, count * LANES), jnp.float32),
            jax.ShapeDtypeStruct(shape, jnp.bfloat16),
            jax.ShapeDtypeStruct(shape, jnp.bfloat16),
        ]
        + [rate] * (2 * CHUNKS),
        scratch_shapes=[pltpu.VMEM((plane, LANES), jnp.float32)],
        compiler_params=params(grid=False),
        cost_estimate=LIGHT,
        name="arrange",
    )(word, courant.reshape(-1, LANES), collision_rate, next_rate, gain_matrix, product_matrix, after)
    return results[0], results[1], results[2], results[3::2], results[4::2]


def stage(values, speed, bend, positive):
    differ = [b - a for a, b in zip(values[:-1], values[1:])]
    slopes = [
        jnp.maximum(jnp.minimum(a, b), jnp.minimum(jnp.maximum(a, b), 0.0))
        for a, b in zip(differ[:-1], differ[1:])
    ]
    inner = [speed * u + bend * s for u, s in zip(values[1:-1], slopes)]
    faces = [jnp.where(positive, a, b) for a, b in zip(inner[:-1], inner[1:])]
    return [u - (b - a) for u, a, b in zip(values[2:-2], faces[:-1], faces[1:])]


def advect_kernel(cells, tile, before, count, parts, c_ref, *refs):
    extras, bodies = refs[:parts], refs[parts : -2 - count]
    smoothed_ref, pieces = refs[-1 - count], refs[-count:]
    rows = WIDE * cells
    planes = sum(ref.shape[0] for ref in bodies) // cells
    share = planes // count
    base = 0
    for extra_ref in extras:
        sources = [(extra_ref, x * cells) for x in range(WIDE)] if before else []
        for ref in bodies:
            sources += [(ref, x * cells) for x in range(ref.shape[0] // cells)]
        if not before:
            sources += [(extra_ref, x * cells) for x in range(WIDE)]

        def column(j, outer, extra_ref=extra_ref, sources=sources, base=base):
            lanes = pl.ds(pl.multiple_of(base + j * LANES, LANES), LANES)
            near = pl.ds(pl.multiple_of(j * LANES, LANES), LANES)
            speed = c_ref[0:1, lanes]
            size = jnp.abs(speed)
            bend = 0.5 * size * (1.0 - size)
            positive = jnp.broadcast_to(speed, (tile, LANES)) > 0.0
            back = jnp.exp2(-extra_ref[rows : rows + 1, near])

            def body(t, carry):
                start = t * tile

                def read(x):
                    ref, first = sources[x]
                    where = pl.ds(pl.multiple_of(first + start, tile), tile)
                    return ref[where, near] * back if ref is extra_ref else ref[where, lanes]

                section = stage([read(x) for x in range(len(sources))], speed, bend, positive)
                moved = stage(section, speed, bend, positive)
                for x in range(planes):
                    result = 0.5 * read(x + HALO) + 0.5 * moved[x]
                    smoothed_ref[pl.ds(pl.multiple_of(x * cells + start, tile), tile), lanes] = result
                    where = pl.ds(pl.multiple_of((x % share) * cells + start, tile), tile)
                    pieces[x // share][where, lanes] = result.astype(jnp.bfloat16)
                return carry

            return lax.fori_loop(0, cells // tile, body, outer)

        lax.fori_loop(0, extra_ref.shape[1] // LANES, column, 0)
        base += extra_ref.shape[1]


def transport(speeds, extras, bodies, before, planes, cells, after):
    count = QUARTERS
    rows, width = planes * cells, speeds.shape[1]
    results = pl.pallas_call(
        functools.partial(advect_kernel, cells, 16, before, count, len(extras)),
        in_specs=[resident()] * (1 + len(extras) + len(bodies)) + [anywhere()],
        out_specs=[resident()] * (1 + count),
        out_shape=[jax.ShapeDtypeStruct((rows, width), jnp.float32)]
        + [jax.ShapeDtypeStruct((rows // count, width), jnp.bfloat16)] * count,
        compiler_params=params(grid=False),
        cost_estimate=LIGHT,
        name="transport",
    )(speeds, *extras, *bodies, after)
    return results[0], results[1:]


def collided(lhs, smoothed, rounded, rate, gain_ref, product_ref, columns):
    dims = (((1,), (1,)), ((), ()))

    def term(ref):
        return lax.dot_general(lhs, ref[columns, :], dims, preferred_element_type=jnp.float32)

    gained = (term(gain_ref) * term(product_ref)).astype(jnp.bfloat16).astype(jnp.float32)
    rate = jnp.concatenate([rate] * (rounded.shape[1] // LANES), axis=1)
    return smoothed + time_step * (gained - rate * rounded.astype(jnp.float32))


def joined(own_refs, other_refs):
    return jnp.concatenate(
        [
            jnp.concatenate([own[...], other[...]], axis=1)
            for own, other in zip(own_refs, other_refs)
        ],
        axis=0,
    )


def half_kernel(count, first, sends, *refs):
    own, other = refs[:count], refs[count : 2 * count]
    smoothed_ref, rate_ref, gain_ref, product_ref, _, state_ref = refs[2 * count : 2 * count + 6]
    size, width = state_ref.shape
    group = 2 * LANES
    lines = slice(first, first + size)
    lhs = joined(own, other)
    for start in range(0, width, group):
        columns = slice(start, start + group)
        state = collided(
            lhs, smoothed_ref[lines, columns], lhs[:, columns], rate_ref[lines, :],
            gain_ref, product_ref, columns,
        )
        state_ref[:, columns] = state
        if sends:
            message_ref = refs[-1]
            power = exponent_of(jnp.max(jnp.abs(state), axis=0, keepdims=True))
            message_ref[:size, columns] = state * jnp.exp2(power)
            message_ref[size:, columns] = jnp.broadcast_to(power, (HEAD, group))


def collide_half(own, other, smoothed, rate, gain, product, first, sends, after):
    width = smoothed.shape[1]
    rows = sum(a.shape[0] for a in own)
    shapes = [jax.ShapeDtypeStruct((rows, width), jnp.float32)]
    if sends:
        shapes.append(jax.ShapeDtypeStruct((rows + HEAD, width), jnp.float32))
    return pl.pallas_call(
        functools.partial(half_kernel, len(own), first, sends),
        in_specs=[resident()] * (2 * len(own) + 4) + [anywhere()],
        out_specs=[resident()] * len(shapes),
        out_shape=shapes,
        compiler_params=params(grid=False),
        cost_estimate=LIGHT,
        name="faces" if sends else "inside",
    )(*own, *other, smoothed, rate, gain, product, after)


def final_kernel(part, count, *refs):
    own, other = refs[:count], refs[count : 2 * count]
    smoothed_ref, rate_ref, gain_ref, product_ref = refs[2 * count : 2 * count + 4]
    outs, scratch = refs[2 * count + 5 : -1], refs[-1]
    rows, group = scratch.shape
    columns = slice(part * group, (part + 1) * group)
    half = count // 2
    size = rows // 2
    for index in range(2):
        lines = slice(index * size, (index + 1) * size)
        lhs = joined(own[index * half : (index + 1) * half], other[index * half : (index + 1) * half])
        scratch[lines, :] = collided(
            lhs, smoothed_ref[lines, columns], lhs[:, columns], rate_ref[lines, :],
            gain_ref, product_ref, columns,
        )
    for index, out in enumerate(outs):
        lanes = slice(index * LANES, (index + 1) * LANES)

        def block(i):
            return pl.ds(pl.multiple_of(i * LANES, LANES), LANES)

        def peak(i, carry):
            return jnp.maximum(carry, jnp.abs(scratch[block(i), lanes]))

        top = lax.fori_loop(0, rows // LANES, peak, jnp.zeros((LANES, LANES), jnp.float32))
        power = exponent_of(jnp.max(top, axis=0, keepdims=True))
        scale = jnp.exp2(power)

        def write(i, carry):
            out[block(i), :] = scratch[block(i), lanes] * scale
            return carry

        lax.fori_loop(0, rows // LANES, write, 0)
        out[rows:, :] = jnp.broadcast_to(power, (HEAD, LANES))


def final(own, other, smoothed, rate, gain, product, part, after):
    rows, width = smoothed.shape
    group = 2 * LANES
    shape = jax.ShapeDtypeStruct((rows + HEAD, LANES), jnp.float32)
    return pl.pallas_call(
        functools.partial(final_kernel, part, len(own)),
        in_specs=[resident()] * (2 * len(own) + 4) + [anywhere()],
        out_specs=[resident()] * 2,
        out_shape=[shape] * 2,
        scratch_shapes=[pltpu.VMEM((rows, group), jnp.float32)],
        compiler_params=params(grid=False),
        cost_estimate=LIGHT,
        name="final",
    )(*own, *other, smoothed, rate, gain, product, after)


def unpack_kernel(order, planes, cells, chip_ref, *refs):
    count = len(order)
    pieces, out, scratch = refs[:count], refs[-2], refs[-1]
    chip = chip_ref[0]
    step = pl.program_id(0)
    flat = out.reshape(LANES * planes, LANES)

    @pl.when(step == 0)
    def _():
        for mask, piece in zip(order, pieces):
            first = pl.multiple_of((chip ^ mask) * cells, cells)
            scale = jnp.exp2(-piece[planes * cells : planes * cells + 1, :])

            for x in range(planes):
                scratch[x, pl.ds(first, cells), :] = piece[x * cells : (x + 1) * cells, :] * scale

    for x in range(planes):
        part = scratch[x, pl.ds(pl.multiple_of(step * LANES, LANES), LANES), :]
        flat[pl.ds(x, LANES, stride=planes), :] = part.T


def unpack(pieces, target, chip, order, chunk, planes, cells, after):
    width = cells * len(order)
    steps = width // LANES
    shape = (LANES, planes, width * CHUNKS)
    specs = [pl.BlockSpec(p.shape, lambda i, s: (0, 0)) for p in pieces]
    operands = list(pieces)
    count = len(pieces)
    specs.append(anywhere())
    operands.append(after)
    aliases = {}
    if target is not None:
        specs.append(pl.BlockSpec(memory_space=pl.ANY))
        operands.append(target)
        aliases = {len(operands): 0}
    return pl.pallas_call(
        functools.partial(unpack_kernel, order, planes, cells),
        grid_spec=pltpu.PrefetchScalarGridSpec(
            num_scalar_prefetch=1,
            grid=(steps,),
            in_specs=specs,
            out_specs=pl.BlockSpec((LANES, planes, LANES), lambda i, s: (0, 0, chunk * steps + i)),
            scratch_shapes=[pltpu.VMEM((planes, width, LANES), jnp.float32)],
        ),
        out_shape=jax.ShapeDtypeStruct(shape, jnp.float32),
        input_output_aliases=aliases,
        compiler_params=params([False] + [True] * count + [False] * (len(operands) - count)),
        cost_estimate=LIGHT,
        name="unpack",
    )(chip, *operands)


def exchange(array, mask):
    count = lax.axis_size("vel")
    return lax.ppermute(array, "vel", [(i, i ^ mask) for i in range(count)])


def shift(array, step):
    count = lax.axis_size("space")
    return lax.ppermute(array, "space", [(i, (i + step) % count) for i in range(count)])


def half(array):
    return array.astype(jnp.float16)


def full(array):
    return array.astype(jnp.float32)


def across(message, step, widths):
    cuts = [sum(widths[:i]) for i in range(len(widths) + 1)]
    return [shift(half(message[:, a:b]), step) for a, b in zip(cuts[:-1], cuts[1:])]


def body(distribution, courant, gain_matrix, product_matrix, collision_rate):
    planes, plane = distribution.shape[1:]
    chips = lax.axis_size("vel") // 2
    member = lax.axis_index("vel").astype(jnp.int32)
    chip, core = lax.shift_right_logical(member, 1), member & 1
    order = list(range(1, chips)) + [0]
    cells = plane // (chips * CHUNKS)
    width = chips * LANES
    rows = WIDE * cells + HEAD
    word = jnp.stack([chip, core])
    every = range(CHUNKS)
    sent, extra, local, state, packed = {}, {}, {}, {}, {}

    after = distribution
    for k in every:
        pieces = pack(distribution, word, order, k, cells, after)
        after = packed[k] = pieces[-1]
        sent[k] = [a if m == 0 else exchange(half(a), 2 * m) for a, m in zip(pieces, order)]
    near_rate, packed[0] = lax.optimization_barrier((collision_rate[:8], packed[0]))
    speeds, gain, product, shifted_rates, rates = arrange(
        courant, collision_rate, shift(near_rate, -1), gain_matrix, product_matrix,
        word, order, cells, after,
    )

    soon, after = lax.optimization_barrier((shift(half(packed[0][:rows]), -1), product))
    for k in every:
        whole = [a if m == 0 else full(a) for a, m in zip(sent[k], order)]
        if k == 0:
            message = message_of(whole[:-1], cells, after)
            extra[k] = across(message, -1, [2 * LANES, width - 3 * LANES]) + [soon]
        else:
            message = message_of(whole, cells, after)
            extra[k] = across(message, -1, [width])
        local[k] = after = spread(whole, planes, cells, message)

    middle = QUARTERS // 2
    for k in every:
        extra[k], after = lax.optimization_barrier((extra[k], after))
        arrived = [full(e) for e in extra[k]]
        smoothed, own = transport(speeds, arrived, [local[k]], False, planes, cells, after)
        other = [exchange(a, 1) for a in own]
        upper, message = collide_half(
            own[middle:], other[middle:], smoothed, shifted_rates[k], gain, product,
            WIDE * cells, True, smoothed,
        )
        extra[k] = across(message, 1, [width])
        (lower,) = collide_half(
            own[:middle], other[:middle], smoothed, shifted_rates[k], gain, product,
            0, False, message,
        )
        state[k] = [lower, upper]
        after = lower

    back = {}
    for k in every:
        extra[k], after = lax.optimization_barrier((extra[k], after))
        arrived = [full(e) for e in extra[k]]
        smoothed, own = transport(speeds, arrived, state[k], True, planes, cells, after)
        if k:
            own, ahead = lax.optimization_barrier((own, back[k - 1][:2]))
            back[k - 1] = [*ahead, *back[k - 1][2:]]
        other = [exchange(a, 1) for a in own]
        ready = []
        for part in range(chips // 2):
            ready += final(own, other, smoothed, rates[k], gain, product, part, after)
            after = ready[-1]
        back[k] = [a if m == 0 else exchange(half(a), 2 * m) for a, m in zip(ready, order)]
    result = None
    for k in every:
        pieces = [a if m == 0 else full(a) for a, m in zip(back[k], order)]
        result = unpack(pieces, result, word, order, k, planes, cells, after)
    return result


def fits(mesh, shape, spaces):
    groups = mesh.shape["vel"]
    local, planes = shape[0] // groups, shape[1] // spaces
    chips = groups // 2
    return (
        groups == 8
        and chips & (chips - 1) == 0
        and local == LANES
        and planes == 2 * WIDE
        and shape[2] % (CHUNKS * LANES) == 0
        and shape[2] % (CHUNKS * chips * 16) == 0
    )


def solution(mesh):
    in_specs = (P("vel", "space", None), P(), P(), P(), P("space", None))
    out_specs = P("vel", "space", None)

    def run(distribution, courant, gain_matrix, product_matrix, collision_rate):
        special = fits(mesh, distribution.shape, mesh.shape["space"])
        return jax.shard_map(
            body if special else general_body,
            mesh=mesh, in_specs=in_specs, out_specs=out_specs, check_vma=False,
        )(distribution, courant, gain_matrix, product_matrix, collision_rate)

    return run
```

```python
import functools

import jax
import jax.numpy as jnp
from jax import lax
from jax.experimental import pallas as pl
from jax.experimental.pallas import tpu as pltpu
from jax.sharding import PartitionSpec as P

STEPS = 2
HALO = 4
WIDE = 2 * HALO
HEAD = 8
CHUNKS = 2
LANES = 128
QUARTERS = 4
VMEM = 12 * 1024 * 1024

time_step = 0.2


def with_halo(block, sides, width):
    for axis, dim in sides:
        count = lax.axis_size(axis)
        forward = [(i, i + 1) for i in range(count - 1)]
        forward.append((count - 1, 0))
        backward = [(target, source) for source, target in forward]
        low = lax.ppermute(
            lax.slice_in_dim(block, block.shape[dim] - width, None, axis=dim), axis, forward
        )
        high = lax.ppermute(lax.slice_in_dim(block, 0, width, axis=dim), axis, backward)
        block = jnp.concatenate([low, block, high], axis=dim)
    return block


def minmod(first, second):
    return jnp.maximum(jnp.minimum(first, second), 0.0) + jnp.minimum(
        jnp.maximum(first, second), 0.0
    )


def change(widened, speeds):
    differ = widened[:, 1:] - widened[:, :-1]
    slopes = minmod(differ[:, 1:], differ[:, :-1])
    inner = widened.shape[1] - 4
    left_value = widened[:, 1 : inner + 2]
    right_value = widened[:, 2 : inner + 3]
    left_slope = slopes[:, 0 : inner + 1]
    right_slope = slopes[:, 1 : inner + 2]
    upward = jnp.maximum(speeds, 0.0)
    downward = jnp.minimum(speeds, 0.0)
    fluxes = upward * (left_value + 0.5 * (1.0 - speeds) * left_slope) + downward * (
        right_value - 0.5 * (1.0 + speeds) * right_slope
    )
    return -(fluxes[:, 1:] - fluxes[:, :-1])


def extend(field):
    return with_halo(field, (("space", 1),), 2)


def advect(field, speeds):
    section = field + change(extend(field), speeds)
    return 0.5 * field + 0.5 * (section + change(extend(section), speeds))


def collide(pieces, gain_matrix, product_matrix):
    columns = pieces.reshape(pieces.shape[0], -1)
    first_term = jnp.dot(gain_matrix, columns, preferred_element_type=jnp.float32)
    second_term = jnp.dot(product_matrix, columns, preferred_element_type=jnp.float32)
    return (first_term * second_term).astype(jnp.bfloat16).reshape(pieces.shape)


def update(smoothed, rounded, gained, rate):
    return smoothed + time_step * (gained.astype(jnp.float32) - rate * rounded.astype(jnp.float32))


def general_body(distribution, courant, gain_matrix, product_matrix, collision_rate):
    local_count = distribution.shape[0]
    groups = lax.axis_size("vel")
    member = lax.axis_index("vel")
    own_speeds = lax.dynamic_slice_in_dim(courant, member * local_count, local_count, 0)[
        :, None, None
    ]
    field = distribution
    for step_index in range(STEPS):
        smoothed = advect(field, own_speeds)
        rounded = smoothed.astype(jnp.bfloat16)
        grouped = rounded.reshape(local_count, groups, -1)
        gained = lax.all_to_all(
            collide(
                lax.all_to_all(grouped, "vel", split_axis=1, concat_axis=0, tiled=True),
                gain_matrix,
                product_matrix,
            ),
            "vel",
            split_axis=0,
            concat_axis=1,
            tiled=True,
        )
        field = update(smoothed, rounded, gained.reshape(rounded.shape), collision_rate[None])
    return field


def params(fusable=None, grid=True):
    return pltpu.CompilerParams(
        dimension_semantics=("arbitrary",) if grid else None,
        vmem_limit_bytes=VMEM,
        allow_input_fusion=fusable,
    )


def resident():
    return pl.BlockSpec(memory_space=pltpu.VMEM)


def anywhere():
    return pl.BlockSpec(memory_space=pl.ANY)


LIGHT = pl.CostEstimate(flops=1000, bytes_accessed=1000, transcendentals=0)


def exponent_of(largest):
    power = jnp.floor(14.0 - jnp.log2(jnp.maximum(largest, 1e-36)))
    return jnp.clip(power, -115.0, 120.0)


def pack_kernel(order, planes, cells, chip_ref, d_ref, after_ref, *refs):
    outs, scratch = refs[:-1], refs[-1]
    chip = chip_ref[0]
    step = pl.program_id(0)
    rows = d_ref.reshape(LANES * planes, LANES)
    for x in range(planes):
        part = rows[pl.ds(x, LANES, stride=planes), :]
        scratch[x, pl.ds(pl.multiple_of(step * LANES, LANES), LANES), :] = part.T

    @pl.when(step == pl.num_programs(0) - 1)
    def _():
        for mask, out in zip(order, outs):
            first = pl.multiple_of((chip ^ mask) * cells, cells)

            def peak(x, carry):
                return jnp.maximum(carry, jnp.abs(scratch[x, pl.ds(first, cells), :]))

            top = lax.fori_loop(0, planes, peak, jnp.zeros((cells, LANES), jnp.float32))
            power = exponent_of(jnp.max(top, axis=0, keepdims=True))
            scale = jnp.exp2(power)

            def write(x, carry):
                start = place_of(x, cells)
                out[pl.ds(pl.multiple_of(start, HEAD), cells), :] = (
                    scratch[x, pl.ds(first, cells), :] * scale
                )
                return carry

            lax.fori_loop(0, planes, write, 0)
            out[WIDE * cells : WIDE * cells + HEAD, :] = jnp.broadcast_to(power, (HEAD, LANES))


def place_of(x, cells):
    if isinstance(x, int):
        return x * cells + (HEAD if x >= WIDE else 0)
    return x * cells + jnp.where(x >= WIDE, HEAD, 0)


def pack(distribution, chip, order, chunk, cells, after):
    planes = distribution.shape[1]
    width = cells * len(order)
    steps = width // LANES
    shape = (planes * cells + HEAD, LANES)
    return pl.pallas_call(
        functools.partial(pack_kernel, order, planes, cells),
        grid_spec=pltpu.PrefetchScalarGridSpec(
            num_scalar_prefetch=1,
            grid=(steps,),
            in_specs=[
                pl.BlockSpec((LANES, planes, LANES), lambda i, s: (0, 0, chunk * steps + i)),
                anywhere(),
            ],
            out_specs=[resident() for _ in order],
            scratch_shapes=[pltpu.VMEM((planes, width, LANES), jnp.float32)],
        ),
        out_shape=[jax.ShapeDtypeStruct(shape, jnp.float32) for _ in order],
        compiler_params=params(),
        cost_estimate=LIGHT,
        name="pack",
    )(chip, pltpu.with_memory_space_constraint(distribution, pltpu.HBM), after)


def message_kernel(cells, *refs):
    pieces, out = refs[:-2], refs[-1]
    for index, piece in enumerate(pieces):
        out[:, index * LANES : (index + 1) * LANES] = piece[: WIDE * cells + HEAD, :]


def message_of(pieces, cells, after):
    shape = (WIDE * cells + HEAD, LANES * len(pieces))
    return pl.pallas_call(
        functools.partial(message_kernel, cells),
        grid=(1,),
        in_specs=[pl.BlockSpec(p.shape, lambda i: (0, 0)) for p in pieces] + [anywhere()],
        out_specs=resident(),
        out_shape=jax.ShapeDtypeStruct(shape, jnp.float32),
        compiler_params=params([True] * len(pieces) + [False]),
        cost_estimate=LIGHT,
        name="message",
    )(*pieces, after)


def spread_kernel(planes, cells, *refs):
    pieces, out = refs[:-2], refs[-1]
    rows = WIDE * cells
    for index, piece in enumerate(pieces):
        columns = slice(index * LANES, (index + 1) * LANES)
        scale = jnp.exp2(-piece[rows : rows + 1, :])
        for x in range(planes):
            start = place_of(x, cells)
            out[x * cells : (x + 1) * cells, columns] = piece[start : start + cells, :] * scale


def spread(pieces, planes, cells, after):
    shape = (planes * cells, LANES * len(pieces))
    return pl.pallas_call(
        functools.partial(spread_kernel, planes, cells),
        grid=(1,),
        in_specs=[pl.BlockSpec(p.shape, lambda i: (0, 0)) for p in pieces] + [anywhere()],
        out_specs=resident(),
        out_shape=jax.ShapeDtypeStruct(shape, jnp.float32),
        compiler_params=params([True] * len(pieces) + [False]),
        cost_estimate=LIGHT,
        name="spread",
    )(*pieces, after)


def arrange_kernel(order, planes, cells, word_ref, c_ref, rate_ref, next_ref, g_ref, p_ref, after_ref, speeds_ref, gain_ref, product_ref, *refs):
    rates, scratch = refs[:-1], refs[-1]
    chip, core = word_ref[0], word_ref[1]
    count = len(order)
    for row, mask in enumerate(order):
        own = 2 * (chip ^ mask) + core
        lines = slice(row * LANES, (row + 1) * LANES)
        speeds_ref[:, lines] = jnp.broadcast_to(c_ref[pl.ds(own, 1), :], (8, LANES))
        source = pl.ds(pl.multiple_of(own * LANES, LANES), LANES)
        for column in range(2 * count):
            other = order[column % count]
            block = 2 * (chip ^ other) + (core if column < count else 1 - core)
            lanes = pl.ds(pl.multiple_of(block * LANES, LANES), LANES)
            target = slice(column * LANES, (column + 1) * LANES)
            gain_ref[lines, target] = g_ref[source, lanes]
            product_ref[lines, target] = p_ref[source, lanes]
    tall = jnp.concatenate([rate_ref[...], next_ref[...]], axis=0)
    tall = jnp.concatenate([tall, jnp.zeros((LANES - tall.shape[0], tall.shape[1]), jnp.float32)], axis=0)
    for lane in range(0, tall.shape[1], LANES):
        scratch[lane : lane + LANES, :] = tall[:, lane : lane + LANES].T
    for k in range(len(rates) // 2):
        first = pl.multiple_of((k * count + chip) * cells, cells)
        part = scratch[pl.ds(first, cells), :]
        for x in range(planes + HALO):
            wide = jnp.broadcast_to(part[:, x : x + 1], (cells, LANES))
            if x >= HALO:
                rates[2 * k][(x - HALO) * cells : (x - HALO + 1) * cells, :] = wide
            if x < planes:
                rates[2 * k + 1][x * cells : (x + 1) * cells, :] = wide


def arrange(courant, collision_rate, next_rate, gain_matrix, product_matrix, word, order, cells, after):
    count = len(order)
    planes, plane = collision_rate.shape
    shape = (count * LANES, 2 * count * LANES)
    rate = jax.ShapeDtypeStruct((planes * cells, LANES), jnp.float32)
    results = pl.pallas_call(
        functools.partial(arrange_kernel, order, planes, cells),
        in_specs=[pl.BlockSpec(memory_space=pltpu.SMEM)] + [resident()] * 5 + [anywhere()],
        out_specs=[resident()] * (3 + 2 * CHUNKS),
        out_shape=[
            jax.ShapeDtypeStruct((8, count * LANES), jnp.float32),
            jax.ShapeDtypeStruct(shape, jnp.bfloat16),
            jax.ShapeDtypeStruct(shape, jnp.bfloat16),
        ]
        + [rate] * (2 * CHUNKS),
        scratch_shapes=[pltpu.VMEM((plane, LANES), jnp.float32)],
        compiler_params=params(grid=False),
        cost_estimate=LIGHT,
        name="arrange",
    )(word, courant.reshape(-1, LANES), collision_rate, next_rate, gain_matrix, product_matrix, after)
    return results[0], results[1], results[2], results[3::2], results[4::2]


def stage(values, speed, bend, positive):
    differ = [b - a for a, b in zip(values[:-1], values[1:])]
    slopes = [
        jnp.maximum(jnp.minimum(a, b), jnp.minimum(jnp.maximum(a, b), 0.0))
        for a, b in zip(differ[:-1], differ[1:])
    ]
    inner = [speed * u + bend * s for u, s in zip(values[1:-1], slopes)]
    faces = [jnp.where(positive, a, b) for a, b in zip(inner[:-1], inner[1:])]
    return [u - (b - a) for u, a, b in zip(values[2:-2], faces[:-1], faces[1:])]


def advect_kernel(cells, tile, before, count, parts, c_ref, *refs):
    extras, bodies = refs[:parts], refs[parts : -2 - count]
    smoothed_ref, pieces = refs[-1 - count], refs[-count:]
    rows = WIDE * cells
    planes = sum(ref.shape[0] for ref in bodies) // cells
    share = planes // count
    base = 0
    for extra_ref in extras:
        sources = [(extra_ref, x * cells) for x in range(WIDE)] if before else []
        for ref in bodies:
            sources += [(ref, x * cells) for x in range(ref.shape[0] // cells)]
        if not before:
            sources += [(extra_ref, x * cells) for x in range(WIDE)]

        def column(j, outer, extra_ref=extra_ref, sources=sources, base=base):
            lanes = pl.ds(pl.multiple_of(base + j * LANES, LANES), LANES)
            near = pl.ds(pl.multiple_of(j * LANES, LANES), LANES)
            speed = c_ref[0:1, lanes]
            size = jnp.abs(speed)
            bend = 0.5 * size * (1.0 - size)
            positive = jnp.broadcast_to(speed, (tile, LANES)) > 0.0
            back = jnp.exp2(-extra_ref[rows : rows + 1, near])

            def body(t, carry):
                start = t * tile

                def read(x):
                    ref, first = sources[x]
                    where = pl.ds(pl.multiple_of(first + start, tile), tile)
                    return ref[where, near] * back if ref is extra_ref else ref[where, lanes]

                section = stage([read(x) for x in range(len(sources))], speed, bend, positive)
                moved = stage(section, speed, bend, positive)
                for x in range(planes):
                    result = 0.5 * read(x + HALO) + 0.5 * moved[x]
                    smoothed_ref[pl.ds(pl.multiple_of(x * cells + start, tile), tile), lanes] = result
                    where = pl.ds(pl.multiple_of((x % share) * cells + start, tile), tile)
                    pieces[x // share][where, lanes] = result.astype(jnp.bfloat16)
                return carry

            return lax.fori_loop(0, cells // tile, body, outer)

        lax.fori_loop(0, extra_ref.shape[1] // LANES, column, 0)
        base += extra_ref.shape[1]


def transport(speeds, extras, bodies, before, planes, cells, after):
    count = QUARTERS
    rows, width = planes * cells, speeds.shape[1]
    results = pl.pallas_call(
        functools.partial(advect_kernel, cells, 16, before, count, len(extras)),
        in_specs=[resident()] * (1 + len(extras) + len(bodies)) + [anywhere()],
        out_specs=[resident()] * (1 + count),
        out_shape=[jax.ShapeDtypeStruct((rows, width), jnp.float32)]
        + [jax.ShapeDtypeStruct((rows // count, width), jnp.bfloat16)] * count,
        compiler_params=params(grid=False),
        cost_estimate=LIGHT,
        name="transport",
    )(speeds, *extras, *bodies, after)
    return results[0], results[1:]


def collided(lhs, smoothed, rounded, rate, gain_ref, product_ref, columns):
    dims = (((1,), (1,)), ((), ()))

    def term(ref):
        return lax.dot_general(lhs, ref[columns, :], dims, preferred_element_type=jnp.float32)

    gained = (term(gain_ref) * term(product_ref)).astype(jnp.bfloat16).astype(jnp.float32)
    rate = jnp.concatenate([rate] * (rounded.shape[1] // LANES), axis=1)
    return smoothed + time_step * (gained - rate * rounded.astype(jnp.float32))


def joined(own_refs, other_refs):
    return jnp.concatenate(
        [
            jnp.concatenate([own[...], other[...]], axis=1)
            for own, other in zip(own_refs, other_refs)
        ],
        axis=0,
    )


def half_kernel(count, first, sends, *refs):
    own, other = refs[:count], refs[count : 2 * count]
    smoothed_ref, rate_ref, gain_ref, product_ref, _, state_ref = refs[2 * count : 2 * count + 6]
    size, width = state_ref.shape
    group = 2 * LANES
    lines = slice(first, first + size)
    lhs = joined(own, other)
    for start in range(0, width, group):
        columns = slice(start, start + group)
        state = collided(
            lhs, smoothed_ref[lines, columns], lhs[:, columns], rate_ref[lines, :],
            gain_ref, product_ref, columns,
        )
        state_ref[:, columns] = state
        if sends:
            message_ref = refs[-1]
            power = exponent_of(jnp.max(jnp.abs(state), axis=0, keepdims=True))
            message_ref[:size, columns] = state * jnp.exp2(power)
            message_ref[size:, columns] = jnp.broadcast_to(power, (HEAD, group))


def collide_half(own, other, smoothed, rate, gain, product, first, sends, after):
    width = smoothed.shape[1]
    rows = sum(a.shape[0] for a in own)
    shapes = [jax.ShapeDtypeStruct((rows, width), jnp.float32)]
    if sends:
        shapes.append(jax.ShapeDtypeStruct((rows + HEAD, width), jnp.float32))
    return pl.pallas_call(
        functools.partial(half_kernel, len(own), first, sends),
        in_specs=[resident()] * (2 * len(own) + 4) + [anywhere()],
        out_specs=[resident()] * len(shapes),
        out_shape=shapes,
        compiler_params=params(grid=False),
        cost_estimate=LIGHT,
        name="faces" if sends else "inside",
    )(*own, *other, smoothed, rate, gain, product, after)


def final_kernel(part, count, *refs):
    own, other = refs[:count], refs[count : 2 * count]
    smoothed_ref, rate_ref, gain_ref, product_ref = refs[2 * count : 2 * count + 4]
    outs, scratch = refs[2 * count + 5 : -1], refs[-1]
    rows, group = scratch.shape
    columns = slice(part * group, (part + 1) * group)
    half = count // 2
    size = rows // 2
    for index in range(2):
        lines = slice(index * size, (index + 1) * size)
        lhs = joined(own[index * half : (index + 1) * half], other[index * half : (index + 1) * half])
        scratch[lines, :] = collided(
            lhs, smoothed_ref[lines, columns], lhs[:, columns], rate_ref[lines, :],
            gain_ref, product_ref, columns,
        )
    for index, out in enumerate(outs):
        lanes = slice(index * LANES, (index + 1) * LANES)

        def block(i):
            return pl.ds(pl.multiple_of(i * LANES, LANES), LANES)

        def peak(i, carry):
            return jnp.maximum(carry, jnp.abs(scratch[block(i), lanes]))

        top = lax.fori_loop(0, rows // LANES, peak, jnp.zeros((LANES, LANES), jnp.float32))
        power = exponent_of(jnp.max(top, axis=0, keepdims=True))
        scale = jnp.exp2(power)

        def write(i, carry):
            out[block(i), :] = scratch[block(i), lanes] * scale
            return carry

        lax.fori_loop(0, rows // LANES, write, 0)
        out[rows:, :] = jnp.broadcast_to(power, (HEAD, LANES))


def final(own, other, smoothed, rate, gain, product, part, after):
    rows, width = smoothed.shape
    group = 2 * LANES
    shape = jax.ShapeDtypeStruct((rows + HEAD, LANES), jnp.float32)
    return pl.pallas_call(
        functools.partial(final_kernel, part, len(own)),
        in_specs=[resident()] * (2 * len(own) + 4) + [anywhere()],
        out_specs=[resident()] * 2,
        out_shape=[shape] * 2,
        scratch_shapes=[pltpu.VMEM((rows, group), jnp.float32)],
        compiler_params=params(grid=False),
        cost_estimate=LIGHT,
        name="final",
    )(*own, *other, smoothed, rate, gain, product, after)


def unpack_kernel(order, planes, cells, chip_ref, *refs):
    count = len(order)
    pieces, out, scratch = refs[:count], refs[-2], refs[-1]
    chip = chip_ref[0]
    step = pl.program_id(0)
    flat = out.reshape(LANES * planes, LANES)

    @pl.when(step == 0)
    def _():
        for mask, piece in zip(order, pieces):
            first = pl.multiple_of((chip ^ mask) * cells, cells)
            scale = jnp.exp2(-piece[planes * cells : planes * cells + 1, :])

            for x in range(planes):
                scratch[x, pl.ds(first, cells), :] = piece[x * cells : (x + 1) * cells, :] * scale

    for x in range(planes):
        part = scratch[x, pl.ds(pl.multiple_of(step * LANES, LANES), LANES), :]
        flat[pl.ds(x, LANES, stride=planes), :] = part.T


def unpack(pieces, target, chip, order, chunk, planes, cells, after):
    width = cells * len(order)
    steps = width // LANES
    shape = (LANES, planes, width * CHUNKS)
    specs = [pl.BlockSpec(p.shape, lambda i, s: (0, 0)) for p in pieces]
    operands = list(pieces)
    count = len(pieces)
    specs.append(anywhere())
    operands.append(after)
    aliases = {}
    if target is not None:
        specs.append(pl.BlockSpec(memory_space=pl.ANY))
        operands.append(target)
        aliases = {len(operands): 0}
    return pl.pallas_call(
        functools.partial(unpack_kernel, order, planes, cells),
        grid_spec=pltpu.PrefetchScalarGridSpec(
            num_scalar_prefetch=1,
            grid=(steps,),
            in_specs=specs,
            out_specs=pl.BlockSpec((LANES, planes, LANES), lambda i, s: (0, 0, chunk * steps + i)),
            scratch_shapes=[pltpu.VMEM((planes, width, LANES), jnp.float32)],
        ),
        out_shape=jax.ShapeDtypeStruct(shape, jnp.float32),
        input_output_aliases=aliases,
        compiler_params=params([False] + [True] * count + [False] * (len(operands) - count)),
        cost_estimate=LIGHT,
        name="unpack",
    )(chip, *operands)


def exchange(array, mask):
    count = lax.axis_size("vel")
    return lax.ppermute(array, "vel", [(i, i ^ mask) for i in range(count)])


def shift(array, step):
    count = lax.axis_size("space")
    return lax.ppermute(array, "space", [(i, (i + step) % count) for i in range(count)])


def half(array):
    return array.astype(jnp.float16)


def full(array):
    return array.astype(jnp.float32)


def across(message, step, widths):
    cuts = [sum(widths[:i]) for i in range(len(widths) + 1)]
    return [shift(half(message[:, a:b]), step) for a, b in zip(cuts[:-1], cuts[1:])]


def body(distribution, courant, gain_matrix, product_matrix, collision_rate):
    planes, plane = distribution.shape[1:]
    chips = lax.axis_size("vel") // 2
    member = lax.axis_index("vel").astype(jnp.int32)
    chip, core = lax.shift_right_logical(member, 1), member & 1
    order = [chips - 1] + list(range(1, chips - 1)) + [0]
    cells = plane // (chips * CHUNKS)
    width = chips * LANES
    rows = WIDE * cells + HEAD
    word = jnp.stack([chip, core])
    every = range(CHUNKS)
    sent, extra, local, state, packed = {}, {}, {}, {}, {}

    after = distribution
    for k in every:
        pieces = pack(distribution, word, order, k, cells, after)
        after = packed[k] = pieces[-1]
        sent[k] = [a if m == 0 else exchange(half(a), 2 * m) for a, m in zip(pieces, order)]
    near_rate, packed[0] = lax.optimization_barrier((collision_rate[:8], packed[0]))
    speeds, gain, product, shifted_rates, rates = arrange(
        courant, collision_rate, shift(near_rate, -1), gain_matrix, product_matrix,
        word, order, cells, after,
    )

    soon, after = lax.optimization_barrier((shift(half(packed[0][:rows]), -1), product))
    for k in every:
        whole = [a if m == 0 else full(a) for a, m in zip(sent[k], order)]
        if k == 0:
            message = message_of(whole[:-1], cells, after)
            extra[k] = across(message, -1, [2 * LANES, width - 3 * LANES]) + [soon]
        else:
            message = message_of(whole, cells, after)
            extra[k] = across(message, -1, [width])
        local[k] = after = spread(whole, planes, cells, message)

    middle = QUARTERS // 2
    for k in every:
        extra[k], after = lax.optimization_barrier((extra[k], after))
        arrived = [full(e) for e in extra[k]]
        smoothed, own = transport(speeds, arrived, [local[k]], False, planes, cells, after)
        other = [exchange(a, 1) for a in own]
        upper, message = collide_half(
            own[middle:], other[middle:], smoothed, shifted_rates[k], gain, product,
            WIDE * cells, True, smoothed,
        )
        extra[k] = across(message, 1, [width])
        (lower,) = collide_half(
            own[:middle], other[:middle], smoothed, shifted_rates[k], gain, product,
            0, False, message,
        )
        state[k] = [lower, upper]
        after = lower

    back = {}
    for k in every:
        extra[k], after = lax.optimization_barrier((extra[k], after))
        arrived = [full(e) for e in extra[k]]
        smoothed, own = transport(speeds, arrived, state[k], True, planes, cells, after)
        if k:
            own, ahead = lax.optimization_barrier((own, back[k - 1][:1]))
            back[k - 1] = [*ahead, *back[k - 1][1:]]
        other = [exchange(a, 1) for a in own]
        ready = []
        for part in range(chips // 2):
            ready += final(own, other, smoothed, rates[k], gain, product, part, after)
            after = ready[-1]
        back[k] = [a if m == 0 else exchange(half(a), 2 * m) for a, m in zip(ready, order)]
    result = None
    for k in every:
        pieces = [a if m == 0 else full(a) for a, m in zip(back[k], order)]
        result = unpack(pieces, result, word, order, k, planes, cells, after)
    return result


def fits(mesh, shape, spaces):
    groups = mesh.shape["vel"]
    local, planes = shape[0] // groups, shape[1] // spaces
    chips = groups // 2
    return (
        groups == 8
        and chips & (chips - 1) == 0
        and local == LANES
        and planes == 2 * WIDE
        and shape[2] % (CHUNKS * LANES) == 0
        and shape[2] % (CHUNKS * chips * 16) == 0
    )


def solution(mesh):
    in_specs = (P("vel", "space", None), P(), P(), P(), P("space", None))
    out_specs = P("vel", "space", None)

    def run(distribution, courant, gain_matrix, product_matrix, collision_rate):
        special = fits(mesh, distribution.shape, mesh.shape["space"])
        return jax.shard_map(
            body if special else general_body,
            mesh=mesh, in_specs=in_specs, out_specs=out_specs, check_vma=False,
        )(distribution, courant, gain_matrix, product_matrix, collision_rate)

    return run
```

```python
import functools

import jax
import jax.numpy as jnp
from jax import lax
from jax.experimental import pallas as pl
from jax.experimental.pallas import tpu as pltpu
from jax.sharding import PartitionSpec as P

STEPS = 2
HALO = 4
WIDE = 2 * HALO
HEAD = 8
CHUNKS = 2
LANES = 128
QUARTERS = 4
VMEM = 12 * 1024 * 1024

time_step = 0.2


def with_halo(block, sides, width):
    for axis, dim in sides:
        count = lax.axis_size(axis)
        forward = [(i, i + 1) for i in range(count - 1)]
        forward.append((count - 1, 0))
        backward = [(target, source) for source, target in forward]
        low = lax.ppermute(
            lax.slice_in_dim(block, block.shape[dim] - width, None, axis=dim), axis, forward
        )
        high = lax.ppermute(lax.slice_in_dim(block, 0, width, axis=dim), axis, backward)
        block = jnp.concatenate([low, block, high], axis=dim)
    return block


def minmod(first, second):
    return jnp.maximum(jnp.minimum(first, second), 0.0) + jnp.minimum(
        jnp.maximum(first, second), 0.0
    )


def change(widened, speeds):
    differ = widened[:, 1:] - widened[:, :-1]
    slopes = minmod(differ[:, 1:], differ[:, :-1])
    inner = widened.shape[1] - 4
    left_value = widened[:, 1 : inner + 2]
    right_value = widened[:, 2 : inner + 3]
    left_slope = slopes[:, 0 : inner + 1]
    right_slope = slopes[:, 1 : inner + 2]
    upward = jnp.maximum(speeds, 0.0)
    downward = jnp.minimum(speeds, 0.0)
    fluxes = upward * (left_value + 0.5 * (1.0 - speeds) * left_slope) + downward * (
        right_value - 0.5 * (1.0 + speeds) * right_slope
    )
    return -(fluxes[:, 1:] - fluxes[:, :-1])


def extend(field):
    return with_halo(field, (("space", 1),), 2)


def advect(field, speeds):
    section = field + change(extend(field), speeds)
    return 0.5 * field + 0.5 * (section + change(extend(section), speeds))


def collide(pieces, gain_matrix, product_matrix):
    columns = pieces.reshape(pieces.shape[0], -1)
    first_term = jnp.dot(gain_matrix, columns, preferred_element_type=jnp.float32)
    second_term = jnp.dot(product_matrix, columns, preferred_element_type=jnp.float32)
    return (first_term * second_term).astype(jnp.bfloat16).reshape(pieces.shape)


def update(smoothed, rounded, gained, rate):
    return smoothed + time_step * (gained.astype(jnp.float32) - rate * rounded.astype(jnp.float32))


def general_body(distribution, courant, gain_matrix, product_matrix, collision_rate):
    local_count = distribution.shape[0]
    groups = lax.axis_size("vel")
    member = lax.axis_index("vel")
    own_speeds = lax.dynamic_slice_in_dim(courant, member * local_count, local_count, 0)[
        :, None, None
    ]
    field = distribution
    for step_index in range(STEPS):
        smoothed = advect(field, own_speeds)
        rounded = smoothed.astype(jnp.bfloat16)
        grouped = rounded.reshape(local_count, groups, -1)
        gained = lax.all_to_all(
            collide(
                lax.all_to_all(grouped, "vel", split_axis=1, concat_axis=0, tiled=True),
                gain_matrix,
                product_matrix,
            ),
            "vel",
            split_axis=0,
            concat_axis=1,
            tiled=True,
        )
        field = update(smoothed, rounded, gained.reshape(rounded.shape), collision_rate[None])
    return field


def params(fusable=None, grid=True):
    return pltpu.CompilerParams(
        dimension_semantics=("arbitrary",) if grid else None,
        vmem_limit_bytes=VMEM,
        allow_input_fusion=fusable,
    )


def resident():
    return pl.BlockSpec(memory_space=pltpu.VMEM)


def anywhere():
    return pl.BlockSpec(memory_space=pl.ANY)


LIGHT = pl.CostEstimate(flops=1000, bytes_accessed=1000, transcendentals=0)


def exponent_of(largest):
    power = jnp.floor(14.0 - jnp.log2(jnp.maximum(largest, 1e-36)))
    return jnp.clip(power, -115.0, 120.0)


def pack_kernel(order, planes, cells, chip_ref, d_ref, after_ref, *refs):
    outs, scratch = refs[:-1], refs[-1]
    chip = chip_ref[0]
    step = pl.program_id(0)
    rows = d_ref.reshape(LANES * planes, LANES)
    for x in range(planes):
        part = rows[pl.ds(x, LANES, stride=planes), :]
        scratch[x, pl.ds(pl.multiple_of(step * LANES, LANES), LANES), :] = part.T

    @pl.when(step == pl.num_programs(0) - 1)
    def _():
        for mask, out in zip(order, outs):
            first = pl.multiple_of((chip ^ mask) * cells, cells)

            def peak(x, carry):
                return jnp.maximum(carry, jnp.abs(scratch[x, pl.ds(first, cells), :]))

            top = lax.fori_loop(0, planes, peak, jnp.zeros((cells, LANES), jnp.float32))
            power = exponent_of(jnp.max(top, axis=0, keepdims=True))
            scale = jnp.exp2(power)

            def write(x, carry):
                start = place_of(x, cells)
                out[pl.ds(pl.multiple_of(start, HEAD), cells), :] = (
                    scratch[x, pl.ds(first, cells), :] * scale
                )
                return carry

            lax.fori_loop(0, planes, write, 0)
            out[WIDE * cells : WIDE * cells + HEAD, :] = jnp.broadcast_to(power, (HEAD, LANES))


def place_of(x, cells):
    if isinstance(x, int):
        return x * cells + (HEAD if x >= WIDE else 0)
    return x * cells + jnp.where(x >= WIDE, HEAD, 0)


def pack(distribution, chip, order, chunk, cells, after):
    planes = distribution.shape[1]
    width = cells * len(order)
    steps = width // LANES
    shape = (planes * cells + HEAD, LANES)
    return pl.pallas_call(
        functools.partial(pack_kernel, order, planes, cells),
        grid_spec=pltpu.PrefetchScalarGridSpec(
            num_scalar_prefetch=1,
            grid=(steps,),
            in_specs=[
                pl.BlockSpec((LANES, planes, LANES), lambda i, s: (0, 0, chunk * steps + i)),
                anywhere(),
            ],
            out_specs=[resident() for _ in order],
            scratch_shapes=[pltpu.VMEM((planes, width, LANES), jnp.float32)],
        ),
        out_shape=[jax.ShapeDtypeStruct(shape, jnp.float32) for _ in order],
        compiler_params=params(),
        cost_estimate=LIGHT,
        name="pack",
    )(chip, pltpu.with_memory_space_constraint(distribution, pltpu.HBM), after)


def message_kernel(cells, *refs):
    pieces, out = refs[:-2], refs[-1]
    for index, piece in enumerate(pieces):
        out[:, index * LANES : (index + 1) * LANES] = piece[: WIDE * cells + HEAD, :]


def message_of(pieces, cells, after):
    shape = (WIDE * cells + HEAD, LANES * len(pieces))
    return pl.pallas_call(
        functools.partial(message_kernel, cells),
        grid=(1,),
        in_specs=[pl.BlockSpec(p.shape, lambda i: (0, 0)) for p in pieces] + [anywhere()],
        out_specs=resident(),
        out_shape=jax.ShapeDtypeStruct(shape, jnp.float32),
        compiler_params=params([True] * len(pieces) + [False]),
        cost_estimate=LIGHT,
        name="message",
    )(*pieces, after)


def spread_kernel(planes, cells, *refs):
    pieces, out = refs[:-2], refs[-1]
    rows = WIDE * cells
    for index, piece in enumerate(pieces):
        columns = slice(index * LANES, (index + 1) * LANES)
        scale = jnp.exp2(-piece[rows : rows + 1, :])
        for x in range(planes):
            start = place_of(x, cells)
            out[x * cells : (x + 1) * cells, columns] = piece[start : start + cells, :] * scale


def spread(pieces, planes, cells, after):
    shape = (planes * cells, LANES * len(pieces))
    return pl.pallas_call(
        functools.partial(spread_kernel, planes, cells),
        grid=(1,),
        in_specs=[pl.BlockSpec(p.shape, lambda i: (0, 0)) for p in pieces] + [anywhere()],
        out_specs=resident(),
        out_shape=jax.ShapeDtypeStruct(shape, jnp.float32),
        compiler_params=params([True] * len(pieces) + [False]),
        cost_estimate=LIGHT,
        name="spread",
    )(*pieces, after)


def arrange_kernel(order, planes, cells, word_ref, c_ref, rate_ref, next_ref, g_ref, p_ref, after_ref, speeds_ref, gain_ref, product_ref, *refs):
    rates, scratch = refs[:-1], refs[-1]
    chip, core = word_ref[0], word_ref[1]
    count = len(order)
    for row, mask in enumerate(order):
        own = 2 * (chip ^ mask) + core
        lines = slice(row * LANES, (row + 1) * LANES)
        speeds_ref[:, lines] = jnp.broadcast_to(c_ref[pl.ds(own, 1), :], (8, LANES))
        source = pl.ds(pl.multiple_of(own * LANES, LANES), LANES)
        for column in range(2 * count):
            other = order[column % count]
            block = 2 * (chip ^ other) + (core if column < count else 1 - core)
            lanes = pl.ds(pl.multiple_of(block * LANES, LANES), LANES)
            target = slice(column * LANES, (column + 1) * LANES)
            gain_ref[lines, target] = g_ref[source, lanes]
            product_ref[lines, target] = p_ref[source, lanes]
    tall = jnp.concatenate([rate_ref[...], next_ref[...]], axis=0)
    tall = jnp.concatenate([tall, jnp.zeros((LANES - tall.shape[0], tall.shape[1]), jnp.float32)], axis=0)
    for lane in range(0, tall.shape[1], LANES):
        scratch[lane : lane + LANES, :] = tall[:, lane : lane + LANES].T
    for k in range(len(rates) // 2):
        first = pl.multiple_of((k * count + chip) * cells, cells)
        part = scratch[pl.ds(first, cells), :]
        for x in range(planes + HALO):
            wide = jnp.broadcast_to(part[:, x : x + 1], (cells, LANES))
            if x >= HALO:
                rates[2 * k][(x - HALO) * cells : (x - HALO + 1) * cells, :] = wide
            if x < planes:
                rates[2 * k + 1][x * cells : (x + 1) * cells, :] = wide


def arrange(courant, collision_rate, next_rate, gain_matrix, product_matrix, word, order, cells, after):
    count = len(order)
    planes, plane = collision_rate.shape
    shape = (count * LANES, 2 * count * LANES)
    rate = jax.ShapeDtypeStruct((planes * cells, LANES), jnp.float32)
    results = pl.pallas_call(
        functools.partial(arrange_kernel, order, planes, cells),
        in_specs=[pl.BlockSpec(memory_space=pltpu.SMEM)] + [resident()] * 5 + [anywhere()],
        out_specs=[resident()] * (3 + 2 * CHUNKS),
        out_shape=[
            jax.ShapeDtypeStruct((8, count * LANES), jnp.float32),
            jax.ShapeDtypeStruct(shape, jnp.bfloat16),
            jax.ShapeDtypeStruct(shape, jnp.bfloat16),
        ]
        + [rate] * (2 * CHUNKS),
        scratch_shapes=[pltpu.VMEM((plane, LANES), jnp.float32)],
        compiler_params=params(grid=False),
        cost_estimate=LIGHT,
        name="arrange",
    )(word, courant.reshape(-1, LANES), collision_rate, next_rate, gain_matrix, product_matrix, after)
    return results[0], results[1], results[2], results[3::2], results[4::2]


def stage(values, speed, bend, positive):
    differ = [b - a for a, b in zip(values[:-1], values[1:])]
    slopes = [
        jnp.maximum(jnp.minimum(a, b), jnp.minimum(jnp.maximum(a, b), 0.0))
        for a, b in zip(differ[:-1], differ[1:])
    ]
    inner = [speed * u + bend * s for u, s in zip(values[1:-1], slopes)]
    faces = [jnp.where(positive, a, b) for a, b in zip(inner[:-1], inner[1:])]
    return [u - (b - a) for u, a, b in zip(values[2:-2], faces[:-1], faces[1:])]


def advect_kernel(cells, tile, before, count, parts, c_ref, *refs):
    extras, bodies = refs[:parts], refs[parts : -2 - count]
    smoothed_ref, pieces = refs[-1 - count], refs[-count:]
    rows = WIDE * cells
    planes = sum(ref.shape[0] for ref in bodies) // cells
    share = planes // count
    base = 0
    for extra_ref in extras:
        sources = [(extra_ref, x * cells) for x in range(WIDE)] if before else []
        for ref in bodies:
            sources += [(ref, x * cells) for x in range(ref.shape[0] // cells)]
        if not before:
            sources += [(extra_ref, x * cells) for x in range(WIDE)]

        def column(j, outer, extra_ref=extra_ref, sources=sources, base=base):
            lanes = pl.ds(pl.multiple_of(base + j * LANES, LANES), LANES)
            near = pl.ds(pl.multiple_of(j * LANES, LANES), LANES)
            speed = c_ref[0:1, lanes]
            size = jnp.abs(speed)
            bend = 0.5 * size * (1.0 - size)
            positive = jnp.broadcast_to(speed, (tile, LANES)) > 0.0
            back = jnp.exp2(-extra_ref[rows : rows + 1, near])

            def body(t, carry):
                start = t * tile

                def read(x):
                    ref, first = sources[x]
                    where = pl.ds(pl.multiple_of(first + start, tile), tile)
                    return ref[where, near] * back if ref is extra_ref else ref[where, lanes]

                section = stage([read(x) for x in range(len(sources))], speed, bend, positive)
                moved = stage(section, speed, bend, positive)
                for x in range(planes):
                    result = 0.5 * read(x + HALO) + 0.5 * moved[x]
                    smoothed_ref[pl.ds(pl.multiple_of(x * cells + start, tile), tile), lanes] = result
                    where = pl.ds(pl.multiple_of((x % share) * cells + start, tile), tile)
                    pieces[x // share][where, lanes] = result.astype(jnp.bfloat16)
                return carry

            return lax.fori_loop(0, cells // tile, body, outer)

        lax.fori_loop(0, extra_ref.shape[1] // LANES, column, 0)
        base += extra_ref.shape[1]


def transport(speeds, extras, bodies, before, planes, cells, after):
    count = QUARTERS
    rows, width = planes * cells, speeds.shape[1]
    results = pl.pallas_call(
        functools.partial(advect_kernel, cells, 32 if cells % 32 == 0 else 16, before, count, len(extras)),
        in_specs=[resident()] * (1 + len(extras) + len(bodies)) + [anywhere()],
        out_specs=[resident()] * (1 + count),
        out_shape=[jax.ShapeDtypeStruct((rows, width), jnp.float32)]
        + [jax.ShapeDtypeStruct((rows // count, width), jnp.bfloat16)] * count,
        compiler_params=params(grid=False),
        cost_estimate=LIGHT,
        name="transport",
    )(speeds, *extras, *bodies, after)
    return results[0], results[1:]


def collided(lhs, smoothed, rounded, rate, gain_ref, product_ref, columns):
    dims = (((1,), (1,)), ((), ()))

    def term(ref):
        return lax.dot_general(lhs, ref[columns, :], dims, preferred_element_type=jnp.float32)

    gained = (term(gain_ref) * term(product_ref)).astype(jnp.bfloat16).astype(jnp.float32)
    rate = jnp.concatenate([rate] * (rounded.shape[1] // LANES), axis=1)
    return smoothed + time_step * (gained - rate * rounded.astype(jnp.float32))


def joined(own_refs, other_refs):
    return jnp.concatenate(
        [
            jnp.concatenate([own[...], other[...]], axis=1)
            for own, other in zip(own_refs, other_refs)
        ],
        axis=0,
    )


def half_kernel(count, first, sends, *refs):
    own, other = refs[:count], refs[count : 2 * count]
    smoothed_ref, rate_ref, gain_ref, product_ref, _, state_ref = refs[2 * count : 2 * count + 6]
    size, width = state_ref.shape
    group = 2 * LANES
    lines = slice(first, first + size)
    lhs = joined(own, other)
    for start in range(0, width, group):
        columns = slice(start, start + group)
        state = collided(
            lhs, smoothed_ref[lines, columns], lhs[:, columns], rate_ref[lines, :],
            gain_ref, product_ref, columns,
        )
        state_ref[:, columns] = state
        if sends:
            message_ref = refs[-1]
            power = exponent_of(jnp.max(jnp.abs(state), axis=0, keepdims=True))
            message_ref[:size, columns] = state * jnp.exp2(power)
            message_ref[size:, columns] = jnp.broadcast_to(power, (HEAD, group))


def collide_half(own, other, smoothed, rate, gain, product, first, sends, after):
    width = smoothed.shape[1]
    rows = sum(a.shape[0] for a in own)
    shapes = [jax.ShapeDtypeStruct((rows, width), jnp.float32)]
    if sends:
        shapes.append(jax.ShapeDtypeStruct((rows + HEAD, width), jnp.float32))
    return pl.pallas_call(
        functools.partial(half_kernel, len(own), first, sends),
        in_specs=[resident()] * (2 * len(own) + 4) + [anywhere()],
        out_specs=[resident()] * len(shapes),
        out_shape=shapes,
        compiler_params=params(grid=False),
        cost_estimate=LIGHT,
        name="faces" if sends else "inside",
    )(*own, *other, smoothed, rate, gain, product, after)


def final_kernel(part, count, *refs):
    own, other = refs[:count], refs[count : 2 * count]
    smoothed_ref, rate_ref, gain_ref, product_ref = refs[2 * count : 2 * count + 4]
    outs, scratch = refs[2 * count + 5 : -1], refs[-1]
    rows, group = scratch.shape
    columns = slice(part * group, (part + 1) * group)
    half = count // 2
    size = rows // 2
    for index in range(2):
        lines = slice(index * size, (index + 1) * size)
        lhs = joined(own[index * half : (index + 1) * half], other[index * half : (index + 1) * half])
        scratch[lines, :] = collided(
            lhs, smoothed_ref[lines, columns], lhs[:, columns], rate_ref[lines, :],
            gain_ref, product_ref, columns,
        )
    for index, out in enumerate(outs):
        lanes = slice(index * LANES, (index + 1) * LANES)

        def block(i):
            return pl.ds(pl.multiple_of(i * LANES, LANES), LANES)

        def peak(i, carry):
            return jnp.maximum(carry, jnp.abs(scratch[block(i), lanes]))

        top = lax.fori_loop(0, rows // LANES, peak, jnp.zeros((LANES, LANES), jnp.float32))
        power = exponent_of(jnp.max(top, axis=0, keepdims=True))
        scale = jnp.exp2(power)

        def write(i, carry):
            out[block(i), :] = scratch[block(i), lanes] * scale
            return carry

        lax.fori_loop(0, rows // LANES, write, 0)
        out[rows:, :] = jnp.broadcast_to(power, (HEAD, LANES))


def final(own, other, smoothed, rate, gain, product, part, after):
    rows, width = smoothed.shape
    group = 2 * LANES
    shape = jax.ShapeDtypeStruct((rows + HEAD, LANES), jnp.float32)
    return pl.pallas_call(
        functools.partial(final_kernel, part, len(own)),
        in_specs=[resident()] * (2 * len(own) + 4) + [anywhere()],
        out_specs=[resident()] * 2,
        out_shape=[shape] * 2,
        scratch_shapes=[pltpu.VMEM((rows, group), jnp.float32)],
        compiler_params=params(grid=False),
        cost_estimate=LIGHT,
        name="final",
    )(*own, *other, smoothed, rate, gain, product, after)


def unpack_kernel(order, planes, cells, chip_ref, *refs):
    count = len(order)
    pieces, out, scratch = refs[:count], refs[-2], refs[-1]
    chip = chip_ref[0]
    step = pl.program_id(0)
    flat = out.reshape(LANES * planes, LANES)

    @pl.when(step == 0)
    def _():
        for mask, piece in zip(order, pieces):
            first = pl.multiple_of((chip ^ mask) * cells, cells)
            scale = jnp.exp2(-piece[planes * cells : planes * cells + 1, :])

            for x in range(planes):
                scratch[x, pl.ds(first, cells), :] = piece[x * cells : (x + 1) * cells, :] * scale

    for x in range(planes):
        part = scratch[x, pl.ds(pl.multiple_of(step * LANES, LANES), LANES), :]
        flat[pl.ds(x, LANES, stride=planes), :] = part.T


def unpack(pieces, target, chip, order, chunk, planes, cells, after):
    width = cells * len(order)
    steps = width // LANES
    shape = (LANES, planes, width * CHUNKS)
    specs = [pl.BlockSpec(p.shape, lambda i, s: (0, 0)) for p in pieces]
    operands = list(pieces)
    count = len(pieces)
    specs.append(anywhere())
    operands.append(after)
    aliases = {}
    if target is not None:
        specs.append(pl.BlockSpec(memory_space=pl.ANY))
        operands.append(target)
        aliases = {len(operands): 0}
    return pl.pallas_call(
        functools.partial(unpack_kernel, order, planes, cells),
        grid_spec=pltpu.PrefetchScalarGridSpec(
            num_scalar_prefetch=1,
            grid=(steps,),
            in_specs=specs,
            out_specs=pl.BlockSpec((LANES, planes, LANES), lambda i, s: (0, 0, chunk * steps + i)),
            scratch_shapes=[pltpu.VMEM((planes, width, LANES), jnp.float32)],
        ),
        out_shape=jax.ShapeDtypeStruct(shape, jnp.float32),
        input_output_aliases=aliases,
        compiler_params=params([False] + [True] * count + [False] * (len(operands) - count)),
        cost_estimate=LIGHT,
        name="unpack",
    )(chip, *operands)


def exchange(array, mask):
    count = lax.axis_size("vel")
    return lax.ppermute(array, "vel", [(i, i ^ mask) for i in range(count)])


def shift(array, step):
    count = lax.axis_size("space")
    return lax.ppermute(array, "space", [(i, (i + step) % count) for i in range(count)])


def half(array):
    return array.astype(jnp.float16)


def full(array):
    return array.astype(jnp.float32)


def across(message, step, widths):
    cuts = [sum(widths[:i]) for i in range(len(widths) + 1)]
    return [shift(half(message[:, a:b]), step) for a, b in zip(cuts[:-1], cuts[1:])]


def body(distribution, courant, gain_matrix, product_matrix, collision_rate):
    planes, plane = distribution.shape[1:]
    chips = lax.axis_size("vel") // 2
    member = lax.axis_index("vel").astype(jnp.int32)
    chip, core = lax.shift_right_logical(member, 1), member & 1
    order = [chips - 1] + list(range(1, chips - 1)) + [0]
    cells = plane // (chips * CHUNKS)
    width = chips * LANES
    rows = WIDE * cells + HEAD
    word = jnp.stack([chip, core])
    every = range(CHUNKS)
    sent, extra, local, state, packed = {}, {}, {}, {}, {}

    after = distribution
    for k in every:
        pieces = pack(distribution, word, order, k, cells, after)
        after = packed[k] = pieces[-1]
        sent[k] = [a if m == 0 else exchange(half(a), 2 * m) for a, m in zip(pieces, order)]
    near_rate, packed[0] = lax.optimization_barrier((collision_rate[:8], packed[0]))
    speeds, gain, product, shifted_rates, rates = arrange(
        courant, collision_rate, shift(near_rate, -1), gain_matrix, product_matrix,
        word, order, cells, after,
    )

    soon, after = lax.optimization_barrier((shift(half(packed[0][:rows]), -1), product))
    for k in every:
        whole = [a if m == 0 else full(a) for a, m in zip(sent[k], order)]
        if k == 0:
            message = message_of(whole[:-1], cells, after)
            extra[k] = across(message, -1, [2 * LANES, width - 3 * LANES]) + [soon]
        else:
            message = message_of(whole, cells, after)
            extra[k] = across(message, -1, [width])
        local[k] = after = spread(whole, planes, cells, message)

    middle = QUARTERS // 2
    for k in every:
        extra[k], after = lax.optimization_barrier((extra[k], after))
        arrived = [full(e) for e in extra[k]]
        smoothed, own = transport(speeds, arrived, [local[k]], False, planes, cells, after)
        other = [exchange(a, 1) for a in own]
        upper, message = collide_half(
            own[middle:], other[middle:], smoothed, shifted_rates[k], gain, product,
            WIDE * cells, True, smoothed,
        )
        extra[k] = across(message, 1, [width])
        (lower,) = collide_half(
            own[:middle], other[:middle], smoothed, shifted_rates[k], gain, product,
            0, False, message,
        )
        state[k] = [lower, upper]
        after = lower

    back = {}
    for k in every:
        extra[k], after = lax.optimization_barrier((extra[k], after))
        arrived = [full(e) for e in extra[k]]
        smoothed, own = transport(speeds, arrived, state[k], True, planes, cells, after)
        if k:
            own, ahead = lax.optimization_barrier((own, back[k - 1][:1]))
            back[k - 1] = [*ahead, *back[k - 1][1:]]
        other = [exchange(a, 1) for a in own]
        ready = []
        for part in range(chips // 2):
            ready += final(own, other, smoothed, rates[k], gain, product, part, after)
            after = ready[-1]
        back[k] = [a if m == 0 else exchange(half(a), 2 * m) for a, m in zip(ready, order)]
    result = None
    for k in every:
        pieces = [a if m == 0 else full(a) for a, m in zip(back[k], order)]
        result = unpack(pieces, result, word, order, k, planes, cells, after)
    return result


def fits(mesh, shape, spaces):
    groups = mesh.shape["vel"]
    local, planes = shape[0] // groups, shape[1] // spaces
    chips = groups // 2
    return (
        groups == 8
        and chips & (chips - 1) == 0
        and local == LANES
        and planes == 2 * WIDE
        and shape[2] % (CHUNKS * LANES) == 0
        and shape[2] % (CHUNKS * chips * 16) == 0
    )


def solution(mesh):
    in_specs = (P("vel", "space", None), P(), P(), P(), P("space", None))
    out_specs = P("vel", "space", None)

    def run(distribution, courant, gain_matrix, product_matrix, collision_rate):
        special = fits(mesh, distribution.shape, mesh.shape["space"])
        return jax.shard_map(
            body if special else general_body,
            mesh=mesh, in_specs=in_specs, out_specs=out_specs, check_vma=False,
        )(distribution, courant, gain_matrix, product_matrix, collision_rate)

    return run
```

```python
import functools

import jax
import jax.numpy as jnp
from jax import lax
from jax.experimental import pallas as pl
from jax.experimental.pallas import tpu as pltpu
from jax.sharding import PartitionSpec as P

STEPS = 2
HALO = 4
WIDE = 2 * HALO
HEAD = 8
CHUNKS = 2
LANES = 128
QUARTERS = 4
VMEM = 12 * 1024 * 1024

time_step = 0.2


def with_halo(block, sides, width):
    for axis, dim in sides:
        count = lax.axis_size(axis)
        forward = [(i, i + 1) for i in range(count - 1)]
        forward.append((count - 1, 0))
        backward = [(target, source) for source, target in forward]
        low = lax.ppermute(
            lax.slice_in_dim(block, block.shape[dim] - width, None, axis=dim), axis, forward
        )
        high = lax.ppermute(lax.slice_in_dim(block, 0, width, axis=dim), axis, backward)
        block = jnp.concatenate([low, block, high], axis=dim)
    return block


def minmod(first, second):
    return jnp.maximum(jnp.minimum(first, second), 0.0) + jnp.minimum(
        jnp.maximum(first, second), 0.0
    )


def change(widened, speeds):
    differ = widened[:, 1:] - widened[:, :-1]
    slopes = minmod(differ[:, 1:], differ[:, :-1])
    inner = widened.shape[1] - 4
    left_value = widened[:, 1 : inner + 2]
    right_value = widened[:, 2 : inner + 3]
    left_slope = slopes[:, 0 : inner + 1]
    right_slope = slopes[:, 1 : inner + 2]
    upward = jnp.maximum(speeds, 0.0)
    downward = jnp.minimum(speeds, 0.0)
    fluxes = upward * (left_value + 0.5 * (1.0 - speeds) * left_slope) + downward * (
        right_value - 0.5 * (1.0 + speeds) * right_slope
    )
    return -(fluxes[:, 1:] - fluxes[:, :-1])


def extend(field):
    return with_halo(field, (("space", 1),), 2)


def advect(field, speeds):
    section = field + change(extend(field), speeds)
    return 0.5 * field + 0.5 * (section + change(extend(section), speeds))


def collide(pieces, gain_matrix, product_matrix):
    columns = pieces.reshape(pieces.shape[0], -1)
    first_term = jnp.dot(gain_matrix, columns, preferred_element_type=jnp.float32)
    second_term = jnp.dot(product_matrix, columns, preferred_element_type=jnp.float32)
    return (first_term * second_term).astype(jnp.bfloat16).reshape(pieces.shape)


def update(smoothed, rounded, gained, rate):
    return smoothed + time_step * (gained.astype(jnp.float32) - rate * rounded.astype(jnp.float32))


def general_body(distribution, courant, gain_matrix, product_matrix, collision_rate):
    local_count = distribution.shape[0]
    groups = lax.axis_size("vel")
    member = lax.axis_index("vel")
    own_speeds = lax.dynamic_slice_in_dim(courant, member * local_count, local_count, 0)[
        :, None, None
    ]
    field = distribution
    for step_index in range(STEPS):
        smoothed = advect(field, own_speeds)
        rounded = smoothed.astype(jnp.bfloat16)
        grouped = rounded.reshape(local_count, groups, -1)
        gained = lax.all_to_all(
            collide(
                lax.all_to_all(grouped, "vel", split_axis=1, concat_axis=0, tiled=True),
                gain_matrix,
                product_matrix,
            ),
            "vel",
            split_axis=0,
            concat_axis=1,
            tiled=True,
        )
        field = update(smoothed, rounded, gained.reshape(rounded.shape), collision_rate[None])
    return field


def params(fusable=None, grid=True):
    return pltpu.CompilerParams(
        dimension_semantics=("arbitrary",) if grid else None,
        vmem_limit_bytes=VMEM,
        allow_input_fusion=fusable,
    )


def resident():
    return pl.BlockSpec(memory_space=pltpu.VMEM)


def anywhere():
    return pl.BlockSpec(memory_space=pl.ANY)


LIGHT = pl.CostEstimate(flops=1000, bytes_accessed=1000, transcendentals=0)


def exponent_of(largest):
    power = jnp.floor(14.0 - jnp.log2(jnp.maximum(largest, 1e-36)))
    return jnp.clip(power, -115.0, 120.0)


def pack_kernel(order, planes, cells, chip_ref, d_ref, after_ref, *refs):
    outs, scratch = refs[:-1], refs[-1]
    chip = chip_ref[0]
    step = pl.program_id(0)
    rows = d_ref.reshape(LANES * planes, LANES)
    for x in range(planes):
        part = rows[pl.ds(x, LANES, stride=planes), :]
        scratch[x, pl.ds(pl.multiple_of(step * LANES, LANES), LANES), :] = part.T

    @pl.when(step == pl.num_programs(0) - 1)
    def _():
        for mask, out in zip(order, outs):
            first = pl.multiple_of((chip ^ mask) * cells, cells)

            def peak(x, carry):
                return jnp.maximum(carry, jnp.abs(scratch[x, pl.ds(first, cells), :]))

            top = lax.fori_loop(0, planes, peak, jnp.zeros((cells, LANES), jnp.float32))
            power = exponent_of(jnp.max(top, axis=0, keepdims=True))
            scale = jnp.exp2(power)

            def write(x, carry):
                start = place_of(x, cells)
                out[pl.ds(pl.multiple_of(start, HEAD), cells), :] = (
                    scratch[x, pl.ds(first, cells), :] * scale
                )
                return carry

            lax.fori_loop(0, planes, write, 0)
            out[WIDE * cells : WIDE * cells + HEAD, :] = jnp.broadcast_to(power, (HEAD, LANES))


def place_of(x, cells):
    if isinstance(x, int):
        return x * cells + (HEAD if x >= WIDE else 0)
    return x * cells + jnp.where(x >= WIDE, HEAD, 0)


def pack(distribution, chip, order, chunk, cells, after):
    planes = distribution.shape[1]
    width = cells * len(order)
    steps = width // LANES
    shape = (planes * cells + HEAD, LANES)
    return pl.pallas_call(
        functools.partial(pack_kernel, order, planes, cells),
        grid_spec=pltpu.PrefetchScalarGridSpec(
            num_scalar_prefetch=1,
            grid=(steps,),
            in_specs=[
                pl.BlockSpec((LANES, planes, LANES), lambda i, s: (0, 0, chunk * steps + i)),
                anywhere(),
            ],
            out_specs=[resident() for _ in order],
            scratch_shapes=[pltpu.VMEM((planes, width, LANES), jnp.float32)],
        ),
        out_shape=[jax.ShapeDtypeStruct(shape, jnp.float32) for _ in order],
        compiler_params=params(),
        cost_estimate=LIGHT,
        name="pack",
    )(chip, pltpu.with_memory_space_constraint(distribution, pltpu.HBM), after)


def message_kernel(cells, *refs):
    pieces, out = refs[:-2], refs[-1]
    for index, piece in enumerate(pieces):
        out[:, index * LANES : (index + 1) * LANES] = piece[: WIDE * cells + HEAD, :]


def message_of(pieces, cells, after):
    shape = (WIDE * cells + HEAD, LANES * len(pieces))
    return pl.pallas_call(
        functools.partial(message_kernel, cells),
        grid=(1,),
        in_specs=[resident() for _ in pieces] + [anywhere()],
        out_specs=resident(),
        out_shape=jax.ShapeDtypeStruct(shape, jnp.float32),
        compiler_params=params(),
        cost_estimate=LIGHT,
        name="message",
    )(*pieces, after)


def spread_kernel(planes, cells, *refs):
    pieces, out = refs[:-2], refs[-1]
    rows = WIDE * cells
    for index, piece in enumerate(pieces):
        columns = slice(index * LANES, (index + 1) * LANES)
        scale = jnp.exp2(-piece[rows : rows + 1, :])
        for x in range(planes):
            start = place_of(x, cells)
            out[x * cells : (x + 1) * cells, columns] = piece[start : start + cells, :] * scale


def spread(pieces, planes, cells, after):
    shape = (planes * cells, LANES * len(pieces))
    return pl.pallas_call(
        functools.partial(spread_kernel, planes, cells),
        grid=(1,),
        in_specs=[resident() for _ in pieces] + [anywhere()],
        out_specs=resident(),
        out_shape=jax.ShapeDtypeStruct(shape, jnp.float32),
        compiler_params=params(),
        cost_estimate=LIGHT,
        name="spread",
    )(*pieces, after)


def arrange_kernel(order, planes, cells, word_ref, c_ref, rate_ref, next_ref, g_ref, p_ref, after_ref, speeds_ref, gain_ref, product_ref, *refs):
    rates, scratch = refs[:-1], refs[-1]
    chip, core = word_ref[0], word_ref[1]
    count = len(order)
    for row, mask in enumerate(order):
        own = 2 * (chip ^ mask) + core
        lines = slice(row * LANES, (row + 1) * LANES)
        speeds_ref[:, lines] = jnp.broadcast_to(c_ref[pl.ds(own, 1), :], (8, LANES))
        source = pl.ds(pl.multiple_of(own * LANES, LANES), LANES)
        for column in range(2 * count):
            other = order[column % count]
            block = 2 * (chip ^ other) + (core if column < count else 1 - core)
            lanes = pl.ds(pl.multiple_of(block * LANES, LANES), LANES)
            target = slice(column * LANES, (column + 1) * LANES)
            gain_ref[lines, target] = g_ref[source, lanes]
            product_ref[lines, target] = p_ref[source, lanes]
    tall = jnp.concatenate([rate_ref[...], next_ref[...]], axis=0)
    tall = jnp.concatenate([tall, jnp.zeros((LANES - tall.shape[0], tall.shape[1]), jnp.float32)], axis=0)
    for lane in range(0, tall.shape[1], LANES):
        scratch[lane : lane + LANES, :] = tall[:, lane : lane + LANES].T
    for k in range(len(rates) // 2):
        first = pl.multiple_of((k * count + chip) * cells, cells)
        part = scratch[pl.ds(first, cells), :]
        for x in range(planes + HALO):
            wide = jnp.broadcast_to(part[:, x : x + 1], (cells, LANES))
            if x >= HALO:
                rates[2 * k][(x - HALO) * cells : (x - HALO + 1) * cells, :] = wide
            if x < planes:
                rates[2 * k + 1][x * cells : (x + 1) * cells, :] = wide


def arrange(courant, collision_rate, next_rate, gain_matrix, product_matrix, word, order, cells, after):
    count = len(order)
    planes, plane = collision_rate.shape
    shape = (count * LANES, 2 * count * LANES)
    rate = jax.ShapeDtypeStruct((planes * cells, LANES), jnp.float32)
    results = pl.pallas_call(
        functools.partial(arrange_kernel, order, planes, cells),
        in_specs=[pl.BlockSpec(memory_space=pltpu.SMEM)] + [resident()] * 5 + [anywhere()],
        out_specs=[resident()] * (3 + 2 * CHUNKS),
        out_shape=[
            jax.ShapeDtypeStruct((8, count * LANES), jnp.float32),
            jax.ShapeDtypeStruct(shape, jnp.bfloat16),
            jax.ShapeDtypeStruct(shape, jnp.bfloat16),
        ]
        + [rate] * (2 * CHUNKS),
        scratch_shapes=[pltpu.VMEM((plane, LANES), jnp.float32)],
        compiler_params=params(grid=False),
        cost_estimate=LIGHT,
        name="arrange",
    )(word, courant.reshape(-1, LANES), collision_rate, next_rate, gain_matrix, product_matrix, after)
    return results[0], results[1], results[2], results[3::2], results[4::2]


def stage(values, speed, bend, positive):
    differ = [b - a for a, b in zip(values[:-1], values[1:])]
    slopes = [
        jnp.maximum(jnp.minimum(a, b), jnp.minimum(jnp.maximum(a, b), 0.0))
        for a, b in zip(differ[:-1], differ[1:])
    ]
    inner = [speed * u + bend * s for u, s in zip(values[1:-1], slopes)]
    faces = [jnp.where(positive, a, b) for a, b in zip(inner[:-1], inner[1:])]
    return [u - (b - a) for u, a, b in zip(values[2:-2], faces[:-1], faces[1:])]


def advect_kernel(cells, tile, before, count, parts, c_ref, *refs):
    extras, bodies = refs[:parts], refs[parts : -2 - count]
    smoothed_ref, pieces = refs[-1 - count], refs[-count:]
    rows = WIDE * cells
    planes = sum(ref.shape[0] for ref in bodies) // cells
    share = planes // count
    base = 0
    for extra_ref in extras:
        sources = [(extra_ref, x * cells) for x in range(WIDE)] if before else []
        for ref in bodies:
            sources += [(ref, x * cells) for x in range(ref.shape[0] // cells)]
        if not before:
            sources += [(extra_ref, x * cells) for x in range(WIDE)]

        def column(j, outer, extra_ref=extra_ref, sources=sources, base=base):
            lanes = pl.ds(pl.multiple_of(base + j * LANES, LANES), LANES)
            near = pl.ds(pl.multiple_of(j * LANES, LANES), LANES)
            speed = c_ref[0:1, lanes]
            size = jnp.abs(speed)
            bend = 0.5 * size * (1.0 - size)
            positive = jnp.broadcast_to(speed, (tile, LANES)) > 0.0
            back = jnp.exp2(-extra_ref[rows : rows + 1, near])

            def body(t, carry):
                start = t * tile

                def read(x):
                    ref, first = sources[x]
                    where = pl.ds(pl.multiple_of(first + start, tile), tile)
                    return ref[where, near] * back if ref is extra_ref else ref[where, lanes]

                section = stage([read(x) for x in range(len(sources))], speed, bend, positive)
                moved = stage(section, speed, bend, positive)
                for x in range(planes):
                    result = 0.5 * read(x + HALO) + 0.5 * moved[x]
                    smoothed_ref[pl.ds(pl.multiple_of(x * cells + start, tile), tile), lanes] = result
                    where = pl.ds(pl.multiple_of((x % share) * cells + start, tile), tile)
                    pieces[x // share][where, lanes] = result.astype(jnp.bfloat16)
                return carry

            return lax.fori_loop(0, cells // tile, body, outer)

        lax.fori_loop(0, extra_ref.shape[1] // LANES, column, 0)
        base += extra_ref.shape[1]


def transport(speeds, extras, bodies, before, planes, cells, after):
    count = QUARTERS
    rows, width = planes * cells, speeds.shape[1]
    results = pl.pallas_call(
        functools.partial(advect_kernel, cells, 16, before, count, len(extras)),
        in_specs=[resident()] * (1 + len(extras) + len(bodies)) + [anywhere()],
        out_specs=[resident()] * (1 + count),
        out_shape=[jax.ShapeDtypeStruct((rows, width), jnp.float32)]
        + [jax.ShapeDtypeStruct((rows // count, width), jnp.bfloat16)] * count,
        compiler_params=params(grid=False),
        cost_estimate=LIGHT,
        name="transport",
    )(speeds, *extras, *bodies, after)
    return results[0], results[1:]


def collided(lhs, smoothed, rounded, rate, gain_ref, product_ref, columns):
    dims = (((1,), (1,)), ((), ()))

    def term(ref):
        return lax.dot_general(lhs, ref[columns, :], dims, preferred_element_type=jnp.float32)

    gained = (term(gain_ref) * term(product_ref)).astype(jnp.bfloat16).astype(jnp.float32)
    rate = jnp.concatenate([rate] * (rounded.shape[1] // LANES), axis=1)
    return smoothed + time_step * (gained - rate * rounded.astype(jnp.float32))


def joined(own_refs, other_refs):
    return jnp.concatenate(
        [
            jnp.concatenate([own[...], other[...]], axis=1)
            for own, other in zip(own_refs, other_refs)
        ],
        axis=0,
    )


def half_kernel(count, first, sends, *refs):
    own, other = refs[:count], refs[count : 2 * count]
    smoothed_ref, rate_ref, gain_ref, product_ref, _, state_ref = refs[2 * count : 2 * count + 6]
    size, width = state_ref.shape
    group = 2 * LANES
    lines = slice(first, first + size)
    lhs = joined(own, other)
    for start in range(0, width, group):
        columns = slice(start, start + group)
        state = collided(
            lhs, smoothed_ref[lines, columns], lhs[:, columns], rate_ref[lines, :],
            gain_ref, product_ref, columns,
        )
        state_ref[:, columns] = state
        if sends:
            message_ref = refs[-1]
            power = exponent_of(jnp.max(jnp.abs(state), axis=0, keepdims=True))
            message_ref[:size, columns] = state * jnp.exp2(power)
            message_ref[size:, columns] = jnp.broadcast_to(power, (HEAD, group))


def collide_half(own, other, smoothed, rate, gain, product, first, sends, after):
    width = smoothed.shape[1]
    rows = sum(a.shape[0] for a in own)
    shapes = [jax.ShapeDtypeStruct((rows, width), jnp.float32)]
    if sends:
        shapes.append(jax.ShapeDtypeStruct((rows + HEAD, width), jnp.float32))
    return pl.pallas_call(
        functools.partial(half_kernel, len(own), first, sends),
        in_specs=[resident()] * (2 * len(own) + 4) + [anywhere()],
        out_specs=[resident()] * len(shapes),
        out_shape=shapes,
        compiler_params=params(grid=False),
        cost_estimate=LIGHT,
        name="faces" if sends else "inside",
    )(*own, *other, smoothed, rate, gain, product, after)


def final_kernel(part, count, *refs):
    own, other = refs[:count], refs[count : 2 * count]
    smoothed_ref, rate_ref, gain_ref, product_ref = refs[2 * count : 2 * count + 4]
    outs, scratch = refs[2 * count + 5 : -1], refs[-1]
    rows, group = scratch.shape
    columns = slice(part * group, (part + 1) * group)
    half = count // 2
    size = rows // 2
    for index in range(2):
        lines = slice(index * size, (index + 1) * size)
        lhs = joined(own[index * half : (index + 1) * half], other[index * half : (index + 1) * half])
        scratch[lines, :] = collided(
            lhs, smoothed_ref[lines, columns], lhs[:, columns], rate_ref[lines, :],
            gain_ref, product_ref, columns,
        )
    for index, out in enumerate(outs):
        lanes = slice(index * LANES, (index + 1) * LANES)

        def block(i):
            return pl.ds(pl.multiple_of(i * LANES, LANES), LANES)

        def peak(i, carry):
            return jnp.maximum(carry, jnp.abs(scratch[block(i), lanes]))

        top = lax.fori_loop(0, rows // LANES, peak, jnp.zeros((LANES, LANES), jnp.float32))
        power = exponent_of(jnp.max(top, axis=0, keepdims=True))
        scale = jnp.exp2(power)

        def write(i, carry):
            out[block(i), :] = scratch[block(i), lanes] * scale
            return carry

        lax.fori_loop(0, rows // LANES, write, 0)
        out[rows:, :] = jnp.broadcast_to(power, (HEAD, LANES))


def final(own, other, smoothed, rate, gain, product, part, after):
    rows, width = smoothed.shape
    group = 2 * LANES
    shape = jax.ShapeDtypeStruct((rows + HEAD, LANES), jnp.float32)
    return pl.pallas_call(
        functools.partial(final_kernel, part, len(own)),
        in_specs=[resident()] * (2 * len(own) + 4) + [anywhere()],
        out_specs=[resident()] * 2,
        out_shape=[shape] * 2,
        scratch_shapes=[pltpu.VMEM((rows, group), jnp.float32)],
        compiler_params=params(grid=False),
        cost_estimate=LIGHT,
        name="final",
    )(*own, *other, smoothed, rate, gain, product, after)


def unpack_kernel(order, planes, cells, chip_ref, *refs):
    count = len(order)
    pieces, out, scratch = refs[:count], refs[-2], refs[-1]
    chip = chip_ref[0]
    step = pl.program_id(0)
    flat = out.reshape(LANES * planes, LANES)

    @pl.when(step == 0)
    def _():
        for mask, piece in zip(order, pieces):
            first = pl.multiple_of((chip ^ mask) * cells, cells)
            scale = jnp.exp2(-piece[planes * cells : planes * cells + 1, :])

            for x in range(planes):
                scratch[x, pl.ds(first, cells), :] = piece[x * cells : (x + 1) * cells, :] * scale

    for x in range(planes):
        part = scratch[x, pl.ds(pl.multiple_of(step * LANES, LANES), LANES), :]
        flat[pl.ds(x, LANES, stride=planes), :] = part.T


def unpack(pieces, target, chip, order, chunk, planes, cells, after):
    width = cells * len(order)
    steps = width // LANES
    shape = (LANES, planes, width * CHUNKS)
    specs = [resident() for _ in pieces]
    operands = list(pieces)
    count = len(pieces)
    specs.append(anywhere())
    operands.append(after)
    aliases = {}
    if target is not None:
        specs.append(pl.BlockSpec(memory_space=pl.ANY))
        operands.append(target)
        aliases = {len(operands): 0}
    return pl.pallas_call(
        functools.partial(unpack_kernel, order, planes, cells),
        grid_spec=pltpu.PrefetchScalarGridSpec(
            num_scalar_prefetch=1,
            grid=(steps,),
            in_specs=specs,
            out_specs=pl.BlockSpec((LANES, planes, LANES), lambda i, s: (0, 0, chunk * steps + i)),
            scratch_shapes=[pltpu.VMEM((planes, width, LANES), jnp.float32)],
        ),
        out_shape=jax.ShapeDtypeStruct(shape, jnp.float32),
        input_output_aliases=aliases,
        compiler_params=params(),
        cost_estimate=LIGHT,
        name="unpack",
    )(chip, *operands)


def exchange(array, mask):
    count = lax.axis_size("vel")
    return lax.ppermute(array, "vel", [(i, i ^ mask) for i in range(count)])


def shift(array, step):
    count = lax.axis_size("space")
    return lax.ppermute(array, "space", [(i, (i + step) % count) for i in range(count)])


def half(array):
    return array.astype(jnp.float16)


def full(array):
    return array.astype(jnp.float32)


def across(message, step, widths):
    cuts = [sum(widths[:i]) for i in range(len(widths) + 1)]
    return [shift(half(message[:, a:b]), step) for a, b in zip(cuts[:-1], cuts[1:])]


def body(distribution, courant, gain_matrix, product_matrix, collision_rate):
    planes, plane = distribution.shape[1:]
    chips = lax.axis_size("vel") // 2
    member = lax.axis_index("vel").astype(jnp.int32)
    chip, core = lax.shift_right_logical(member, 1), member & 1
    order = [chips - 1] + list(range(1, chips - 1)) + [0]
    cells = plane // (chips * CHUNKS)
    width = chips * LANES
    rows = WIDE * cells + HEAD
    word = jnp.stack([chip, core])
    every = range(CHUNKS)
    sent, extra, local, state, packed = {}, {}, {}, {}, {}

    after = distribution
    for k in every:
        pieces = pack(distribution, word, order, k, cells, after)
        after = packed[k] = pieces[-1]
        sent[k] = [a if m == 0 else exchange(half(a), 2 * m) for a, m in zip(pieces, order)]
    near_rate, packed[0] = lax.optimization_barrier((collision_rate[:8], packed[0]))
    speeds, gain, product, shifted_rates, rates = arrange(
        courant, collision_rate, shift(near_rate, -1), gain_matrix, product_matrix,
        word, order, cells, after,
    )

    soon, after = lax.optimization_barrier((shift(half(packed[0][:rows]), -1), product))
    for k in every:
        whole = [a if m == 0 else full(a) for a, m in zip(sent[k], order)]
        if k == 0:
            message = message_of(whole[:-1], cells, after)
            extra[k] = across(message, -1, [2 * LANES, width - 3 * LANES]) + [soon]
        else:
            message = message_of(whole, cells, after)
            extra[k] = across(message, -1, [width])
        local[k] = after = spread(whole, planes, cells, message)

    middle = QUARTERS // 2
    for k in every:
        extra[k], after = lax.optimization_barrier((extra[k], after))
        arrived = [full(e) for e in extra[k]]
        smoothed, own = transport(speeds, arrived, [local[k]], False, planes, cells, after)
        other = [exchange(a, 1) for a in own]
        upper, message = collide_half(
            own[middle:], other[middle:], smoothed, shifted_rates[k], gain, product,
            WIDE * cells, True, smoothed,
        )
        extra[k] = across(message, 1, [width])
        (lower,) = collide_half(
            own[:middle], other[:middle], smoothed, shifted_rates[k], gain, product,
            0, False, message,
        )
        state[k] = [lower, upper]
        after = lower

    back = {}
    for k in every:
        extra[k], after = lax.optimization_barrier((extra[k], after))
        arrived = [full(e) for e in extra[k]]
        smoothed, own = transport(speeds, arrived, state[k], True, planes, cells, after)
        if k:
            own, ahead = lax.optimization_barrier((own, back[k - 1][:1]))
            back[k - 1] = [*ahead, *back[k - 1][1:]]
        other = [exchange(a, 1) for a in own]
        ready = []
        for part in range(chips // 2):
            ready += final(own, other, smoothed, rates[k], gain, product, part, after)
            after = ready[-1]
        back[k] = [a if m == 0 else exchange(half(a), 2 * m) for a, m in zip(ready, order)]
    result = None
    for k in every:
        pieces = [a if m == 0 else full(a) for a, m in zip(back[k], order)]
        result = unpack(pieces, result, word, order, k, planes, cells, after)
    return result


def fits(mesh, shape, spaces):
    groups = mesh.shape["vel"]
    local, planes = shape[0] // groups, shape[1] // spaces
    chips = groups // 2
    return (
        groups == 8
        and chips & (chips - 1) == 0
        and local == LANES
        and planes == 2 * WIDE
        and shape[2] % (CHUNKS * LANES) == 0
        and shape[2] % (CHUNKS * chips * 16) == 0
    )


def solution(mesh):
    in_specs = (P("vel", "space", None), P(), P(), P(), P("space", None))
    out_specs = P("vel", "space", None)

    def run(distribution, courant, gain_matrix, product_matrix, collision_rate):
        special = fits(mesh, distribution.shape, mesh.shape["space"])
        return jax.shard_map(
            body if special else general_body,
            mesh=mesh, in_specs=in_specs, out_specs=out_specs, check_vma=False,
        )(distribution, courant, gain_matrix, product_matrix, collision_rate)

    return run
```
